128 devices in a mesh: dp: 32 (over z, x, core), seq: 4 (over y).
Axes of the slice: x: 4, y: 4, z: 4, core: 2. Of those that a mesh axis runs over, the one named last changes fastest.
Arguments:
- tokens: bfloat16 [32, 1024, 1024], P('dp', 'seq'), may hold values from -6 to 6
- captions: bfloat16 [32, 128, 1024], P('dp', None, 'seq'), may hold values from -6 to 6
- cap_lengths: int32 [32], P('dp'), may hold values from 1 to 128, as said below
- w_qkv: bfloat16 [1024, 3072], P(('dp', 'seq')), may hold values from -0.1875 to 0.1875
- w_self_out: bfloat16 [1024, 1024], P(('dp', 'seq')), may hold values from -1 to 1
- w_cross_q: bfloat16 [1024, 1024], P(('dp', 'seq')), may hold values from -0.1875 to 0.1875
- w_cross_kv: bfloat16 [1024, 2048], P(('dp', 'seq')), may hold values from -0.1875 to 0.1875
- w_cross_out: bfloat16 [1024, 1024], P(('dp', 'seq')), may hold values from -0.5 to 0.5
- w_in: bfloat16 [1024, 4096], P(('dp', 'seq')), may hold values from -0.1875 to 0.1875
- w_out: bfloat16 [4096, 1024], P(('dp', 'seq')), may hold values from -0.09375 to 0.09375
- norm_gains: bfloat16 [3, 1024], P(None, ('dp', 'seq')), may hold values from 0.5 to 1.5
- norm_shifts: bfloat16 [3, 1024], P(None, ('dp', 'seq')), may hold values from -4 to 4
- out_biases: bfloat16 [3, 1024], P(None, ('dp', 'seq')), may hold values from -4 to 4
- in_bias: bfloat16 [4096], P(('dp', 'seq')), may hold values from -6 to 6
- out_grad: bfloat16 [32, 1024, 1024], P('dp', 'seq'), may hold values from -6 to 6
Outputs:
- layer_out: bfloat16 [32, 1024, 1024], P('dp', 'seq')
- tokens_grad: float32 [32, 1024, 1024], P('dp', 'seq')
- captions_grad: float32 [32, 128, 1024], P('dp', None, 'seq')
- w_qkv_grad: float32 [1024, 3072], P(('dp', 'seq'))
- w_self_out_grad: float32 [1024, 1024], P(('dp', 'seq'))
- w_cross_q_grad: float32 [1024, 1024], P(('dp', 'seq'))
- w_cross_kv_grad: float32 [1024, 2048], P(('dp', 'seq'))
- w_cross_out_grad: float32 [1024, 1024], P(('dp', 'seq'))
- w_in_grad: float32 [1024, 4096], P(('dp', 'seq'))
- w_out_grad: float32 [4096, 1024], P(('dp', 'seq'))
- norm_gains_grad: float32 [3, 1024], P(None, ('dp', 'seq'))
- norm_shifts_grad: float32 [3, 1024], P(None, ('dp', 'seq'))
- out_biases_grad: float32 [3, 1024], P(None, ('dp', 'seq'))
- in_bias_grad: float32 [4096], P(('dp', 'seq'))
The draws below stay inside these ranges and needn't reach their ends.
Inputs may be any that keep to these rules, and one draw needn't show every extreme that they name: `cap_lengths`: in every draw some image attends to all 128 caption rows.
All inputs are finite; a program needn't handle non-finite values.
Results may differ from the reference program's by a relative error of at most 0.019.
Values may be sent and summed in bfloat16 or wider, within the bound.
A program may use at most 384 MiB of HBM per device.

```python
import jax
import jax.numpy as jnp
from jax import lax

D = 1024
HEADS = 16
HEAD_DIM = 64
FF = 4096
SEQ_LEN = 1024
CAP = 128
IMAGES = 32


def draw_cap_lengths(key, part):
    key = jax.random.fold_in(key, 7)
    streams = jax.random.split(key, 5)
    short_top = CAP // 6 + 1
    middle_top = max(CAP // 2, short_top + 1)
    tier = jax.random.randint(streams[0], (IMAGES,), 0, 16)
    short_rows = jax.random.randint(streams[1], (IMAGES,), 1, short_top + 1)
    middle_rows = jax.random.randint(streams[2], (IMAGES,), short_top, middle_top + 1)
    long_rows = jax.random.randint(streams[3], (IMAGES,), middle_top, CAP + 1)
    lengths = jnp.where(tier < 12, short_rows, jnp.where(tier < 15, middle_rows, long_rows))
    chosen = jax.random.randint(streams[4], (), 0, IMAGES)
    lengths = jnp.where(jnp.arange(IMAGES) == chosen, CAP, lengths)
    return jnp.clip(lengths, 1, CAP).astype(jnp.int32)


def levels(stream_key, dims, cuts, low, top_value):
    factor_of = 1.0
    for dim, parts in cuts:
        steps = jax.random.uniform(jax.random.fold_in(jax.random.fold_in(stream_key, 6), dim), (parts,), jnp.float32, low / len(cuts), top_value / len(cuts))
        factor_of = factor_of * jnp.repeat(jnp.exp(steps), dims[dim] // parts).reshape((-1,) + (1,) * (len(dims) - 1 - dim))
    return factor_of


def bell_draw(key, dims, deviation, reach, cuts=(), kind=jnp.bfloat16):
    values = deviation * jax.random.normal(key, dims, jnp.float32)
    if cuts:
        values = values * levels(key, dims, cuts, -0.22, 0.18)
    return jnp.clip(values, -reach, reach).astype(kind)


def setup_inputs(seed: int = 0) -> dict:
    key_list = jax.random.split(jax.random.key(seed), 16)
    tokens = bell_draw(key_list[0], (IMAGES, SEQ_LEN, D), 1.0, 6.0, ((0, 32), (1, 4)))
    captions = bell_draw(key_list[1], (IMAGES, CAP, D), 1.0, 6.0, ((0, 32), (2, 4)))
    cap_lengths = draw_cap_lengths(jax.random.fold_in(key_list[15], 71), 0)
    w_qkv = bell_draw(key_list[3], (D, 3 * D), D ** -0.5, 0.1875, ((0, 128),))
    w_self_out = bell_draw(key_list[4], (D, D), (D // 32) ** -0.5, 1.0, ((0, 128),))
    w_cross_q = bell_draw(key_list[5], (D, D), D ** -0.5, 0.1875, ((0, 128),))
    w_cross_kv = bell_draw(key_list[6], (D, 2 * D), D ** -0.5, 0.1875, ((0, 128),))
    w_cross_out = bell_draw(key_list[7], (D, D), (D // 8) ** -0.5, 0.5, ((0, 128),))
    w_in = bell_draw(key_list[8], (D, FF), D ** -0.5, 0.1875, ((0, 128),))
    w_out = bell_draw(key_list[9], (FF, D), FF ** -0.5, 0.09375, ((0, 128),))
    norm_gains = jnp.clip(1.0 + 0.1 * jax.random.normal(key_list[10], (3, D), jnp.float32), 0.5, 1.5).astype(jnp.bfloat16)
    norm_shifts = bell_draw(key_list[11], (3, D), 0.3, 4.0, ((1, 128),))
    out_biases = bell_draw(key_list[12], (3, D), 0.3, 4.0, ((1, 128),))
    in_bias = bell_draw(key_list[13], (FF,), 0.5, 6.0, ((0, 128),))
    out_grad = bell_draw(key_list[14], (IMAGES, SEQ_LEN, D), 1.0, 6.0, ((0, 32), (1, 4)))
    return dict(tokens=tokens, captions=captions, cap_lengths=cap_lengths, w_qkv=w_qkv, w_self_out=w_self_out, w_cross_q=w_cross_q, w_cross_kv=w_cross_kv, w_cross_out=w_cross_out, w_in=w_in, w_out=w_out, norm_gains=norm_gains, norm_shifts=norm_shifts, out_biases=out_biases, in_bias=in_bias, out_grad=out_grad)


EPSILON = 1e-05
MASKED = -1e+30
PRECISE = lax.Precision.HIGHEST

@jax.custom_vjp
def low(v):
    return lax.optimization_barrier(v.astype(jnp.bfloat16)).astype(jnp.float32)

@jax.custom_vjp
def low_back(v):
    return v

def low_keep(v):
    return (low(v), None)

def low_pass(kept, grad):
    return (grad,)

def back_keep(v):
    return (v, None)

def back_low(kept, grad):
    return (low(grad),)
low.defvjp(low_keep, low_pass)
low_back.defvjp(back_keep, back_low)

def layer_norm(values, gain, shift):
    center = lax.optimization_barrier(jnp.mean(values, axis=-1, keepdims=True))
    centred = values - center
    spread = lax.optimization_barrier(jnp.mean(centred * centred, axis=-1, keepdims=True))
    return centred * lax.rsqrt(spread + EPSILON) * gain + shift

def matmul(left, right):
    return jnp.dot(left, right, precision=PRECISE)

def attend(queries, key_rows, value_rows, visible):
    query_heads = queries.reshape(queries.shape[0], HEADS, HEAD_DIM)
    key_heads = key_rows.reshape(key_rows.shape[0], HEADS, HEAD_DIM)
    value_heads = value_rows.reshape(value_rows.shape[0], HEADS, HEAD_DIM)
    scores = jnp.einsum('qhe,khe->hqk', query_heads, key_heads, precision=PRECISE) * HEAD_DIM ** (-0.5)
    scores = low_back(scores)
    scores = jnp.where(visible[None], scores, MASKED)
    row_peak = lax.optimization_barrier(jnp.max(scores, axis=-1, keepdims=True))
    expon = jnp.exp(scores - row_peak)
    probs = low(expon / lax.optimization_barrier(jnp.sum(expon, axis=-1, keepdims=True)))
    mixed = jnp.einsum('hqk,khe->qhe', probs, value_heads, precision=PRECISE)
    return low_back(low(mixed.reshape(queries.shape[0], -1)))

def image_forward(tokens_in, captions_in, length, params):
    w_qkv, w_self_out, w_cross_q, w_cross_kv, w_cross_out, w_in, w_out, norm_gains, norm_shifts, out_biases, in_bias = params
    model_width = tokens_in.shape[1]
    norm_one = low(layer_norm(tokens_in, norm_gains[0], norm_shifts[0]))
    qkv_rows = low_back(low(matmul(norm_one, w_qkv)))
    places = jnp.arange(SEQ_LEN, dtype=jnp.int32)
    causal = places[:, None] >= places[None, :]
    self_att = attend(qkv_rows[:, :model_width], qkv_rows[:, model_width:2 * model_width], qkv_rows[:, 2 * model_width:], causal)
    after_self = tokens_in + low_back(matmul(self_att, w_self_out)) + out_biases[0]
    norm_two = low(layer_norm(after_self, norm_gains[1], norm_shifts[1]))
    cross_query = low_back(low(matmul(norm_two, w_cross_q)))
    cross_kv = low_back(low(matmul(captions_in, w_cross_kv)))
    in_use = jnp.arange(CAP, dtype=jnp.int32) < length
    visible = jnp.broadcast_to(in_use[None, :], (SEQ_LEN, CAP))
    cross_att = attend(cross_query, cross_kv[:, :model_width], cross_kv[:, model_width:], visible)
    after_cross = after_self + low_back(matmul(cross_att, w_cross_out)) + out_biases[1]
    norm_three = low(layer_norm(after_cross, norm_gains[2], norm_shifts[2]))
    hidden = low_back(matmul(norm_three, w_in) + in_bias)
    active = low(jax.nn.gelu(hidden, approximate=False))
    return after_cross + low_back(matmul(active, w_out)) + out_biases[2]

def reference(tokens, captions, cap_lengths, w_qkv, w_self_out, w_cross_q, w_cross_kv, w_cross_out, w_in, w_out, norm_gains, norm_shifts, out_biases, in_bias, out_grad):
    params = tuple((weight.astype(jnp.float32) for weight in (w_qkv, w_self_out, w_cross_q, w_cross_kv, w_cross_out, w_in, w_out, norm_gains, norm_shifts, out_biases, in_bias)))

    def image_step(totals, pieces):
        image_tokens, image_captions, length, cotangent = pieces

        def forward(tokens_in, captions_in, weights):
            return image_forward(tokens_in, captions_in, length, weights)
        result, pull = jax.vjp(forward, image_tokens.astype(jnp.float32), image_captions.astype(jnp.float32), params)
        grad_tokens, grad_captions, grad_params = pull(cotangent.astype(jnp.float32))
        totals = jax.tree.map(jnp.add, totals, grad_params)
        return (totals, (result.astype(jnp.bfloat16), grad_tokens, grad_captions))
    zero_grads = jax.tree.map(jnp.zeros_like, params)
    totals, outputs = lax.scan(image_step, zero_grads, (tokens, captions, cap_lengths, out_grad))
    layer_out, tokens_grad, captions_grad = outputs
    return (layer_out, tokens_grad, captions_grad, totals[0], totals[1], totals[2], totals[3], totals[4], totals[5], totals[6], totals[7], totals[8], totals[9], totals[10])
```

```python
import functools

import jax
import jax.numpy as jnp
from jax import lax
from jax.experimental import pallas as pl
from jax.experimental.pallas import tpu as pltpu
from jax.sharding import PartitionSpec as P

MESH = pl.DeviceIdType.MESH


def position():
    dp, y = lax.axis_index("dp"), lax.axis_index("seq")
    return {"z": lax.div(dp, 8), "x": lax.rem(lax.div(dp, 2), 4), "c": lax.rem(dp, 2), "y": y}


def device(at):
    return (at["z"] * 8 + at["x"] * 2 + at["c"], at["y"])


def moved(at, axis, by):
    size = 2 if axis == "c" else 4
    return {**at, axis: lax.rem(at[axis] + by + size, size)}


class Copies:
    def __init__(self, send, recv):
        self.send, self.recv, self.used = send, recv, 0

    def start(self, src, dst, at):
        k = self.used
        self.used += 1
        copy = pltpu.make_async_remote_copy(src_ref=src, dst_ref=dst, send_sem=self.send.at[k], recv_sem=self.recv.at[k], device_id=device(at), device_id_type=MESH)
        copy.start()
        return copy


def block(ref, at, whole, cols, **fixed):
    idx = []
    for axis in ("z", "x", "c", "y"):
        idx.append(fixed[axis] if axis in fixed else slice(None) if axis in whole else at[axis])
    return ref.at[(*idx, slice(None), cols)]


def greet(at):
    barrier = pltpu.get_barrier_semaphore()
    others = [moved(at, a, b) for a in "zxy" for b in (1, -1)] + [moved(at, "c", 1), moved(at, "y", 2)]
    for o in others:
        pl.semaphore_signal(barrier, inc=1, device_id=device(o), device_id_type=MESH)
    pl.semaphore_wait(barrier, len(others))


def gather_flow(ref, at, cols, axes, whole, copies, partner, done):
    whole = set(whole)
    for axis in axes:
        up, down = moved(at, axis, 1), moved(at, axis, -1)
        own = block(ref, at, whole, cols)
        a = copies.start(own, own, up)
        b = copies.start(own, own, down)
        yield
        a.wait_recv()
        b.wait_recv()
        low = block(ref, down, whole, cols, c=0)
        high = block(ref, up, whole, cols, c=1)
        c = copies.start(low, low, up)
        d = copies.start(high, high, down)
        for p in (down, up):
            got = block(ref, p, whole, cols)
            done.append(copies.start(got, got, partner))
        yield
        c.wait_recv()
        d.wait_recv()
        far = block(ref, moved(at, axis, 2), whole, cols)
        done.append(copies.start(far, far, partner))
        for s in (a, b, c, d):
            s.wait_send()
        whole.add(axis)


def ag_kernel(c_in, win_in, wout_in, q_in, x_in, cap_in, c_g, win_g, wout_g, q_g, x_g, cap_g, send, recv, local):
    at = position()
    greet(at)
    copies = Copies(send, recv)
    partner = moved(at, "c", 1)
    me = (at["z"], at["x"], at["c"], at["y"])
    pending, done = [], []

    def halves(n):
        mine = pl.ds(pl.multiple_of(at["c"] * (n // 2), 128), n // 2)
        return mine

    qx = []
    n_q = q_in.shape[-1]
    qm = halves(n_q)
    keep = pltpu.make_async_copy(q_in.at[at["y"]], q_g.at[me], local.at[0])
    keep.start()
    pending.append(keep)
    for by in (1, 3, 2):
        to = moved(at, "y", by)
        qx.append(copies.start(q_in.at[to["y"]], q_g.at[me], to))
    xx = []
    own_x, own_cap = pltpu.make_async_copy(x_in, x_g.at[at["y"]], local.at[1]), pltpu.make_async_copy(cap_in, cap_g.at[at["y"]], local.at[2])
    own_x.start()
    own_cap.start()
    pending += [own_x, own_cap]
    up, down = moved(at, "y", 1), moved(at, "y", -1)
    for to in (up, down):
        xx.append(copies.start(x_in, x_g.at[at["y"]], to))
        xx.append(copies.start(cap_in, cap_g.at[at["y"]], to))
    pairs = []
    for k, (src, dst) in enumerate(((c_in, c_g), (win_in, win_g), (wout_in, wout_g))):
        cp = pltpu.make_async_copy(src, dst.at[me], local.at[3 + k])
        cp.start()
        pending.append(cp)
        pairs.append(copies.start(src, dst.at[me], partner))
    keep.wait()
    for q in qx:
        q.wait()
    q_own = block(q_g, at, {"y"}, slice(None))
    qp = copies.start(q_own, q_own, partner)
    for p in pending[1:]:
        p.wait()
    for p in pairs:
        p.wait()
    qp.wait()
    qflow = gather_flow(q_g, at, qm, ("x", "z"), {"y", "c"}, copies, partner, done)
    a = gather_flow(wout_g, at, halves(1024), ("y", "z", "x"), {"c"}, copies, partner, done)
    b = gather_flow(win_g, at, halves(4096), ("x", "y", "z"), {"c"}, copies, partner, done)
    c = gather_flow(c_g, at, halves(c_in.shape[-1]), ("z", "x", "y"), {"c"}, copies, partner, done)
    live = [qflow, a, b, c]
    first = True
    while live:
        for f in list(live):
            if next(f, "end") == "end":
                live.remove(f)
        if first:
            first = False
            xs = xx
            for s in xs:
                s.wait()
            low, high = slice(0, 128), slice(128, 256)
            x2 = [copies.start(x_g.at[down["y"], low], x_g.at[down["y"], low], up), copies.start(x_g.at[up["y"], high], x_g.at[up["y"], high], down)]
            l2, h2 = slice(0, 64), slice(64, 128)
            x2 += [copies.start(cap_g.at[down["y"], l2], cap_g.at[down["y"], l2], up), copies.start(cap_g.at[up["y"], h2], cap_g.at[up["y"], h2], down)]
    for s in x2 + done:
        s.wait()


def all_gathered(c_in, win_in, wout_in, q_in, x_in, cap_in):
    bf = jnp.bfloat16
    outs = [jax.ShapeDtypeStruct((4, 4, 2, 4, *a.shape), bf) for a in (c_in, win_in, wout_in)]
    outs += [jax.ShapeDtypeStruct((4, 4, 2, 4, 8, q_in.shape[-1]), bf), jax.ShapeDtypeStruct((4, *x_in.shape), bf), jax.ShapeDtypeStruct((4, *cap_in.shape), bf)]
    n = 96
    return pl.pallas_call(
        ag_kernel, out_shape=outs,
        in_specs=[pl.BlockSpec(memory_space=pl.ANY)] * 6, out_specs=[pl.BlockSpec(memory_space=pl.ANY)] * 6,
        scratch_shapes=[pltpu.SemaphoreType.DMA((n,)), pltpu.SemaphoreType.DMA((n,)), pltpu.SemaphoreType.DMA((6,))],
        compiler_params=pltpu.CompilerParams(collective_id=0, has_side_effects=True),
        name="gather_weights",
    )(c_in, win_in, wout_in, q_in, x_in, cap_in)


ORDER = ("z", "x", "c", "y")


def part(ref, at, whole, **fixed):
    return ref.at[tuple(fixed[a] if a in fixed else slice(None) if a in whole else at[a] for a in ORDER)]


def each(shape, body):
    total = 1
    for s in shape:
        total *= s

    def step(i, _):
        index, rest = [], i
        for s in reversed(shape):
            index.insert(0, lax.rem(rest, s))
            rest = lax.div(rest, s)
        body(tuple(index))
        return 0

    if total == 1:
        body((0,) * len(shape))
    else:
        lax.fori_loop(0, total, step, 0)


def add_into(dst, *srcs):
    def one(index):
        total = dst[index].astype(jnp.float32)
        for s in srcs:
            total += s[index].astype(jnp.float32)
        dst[index] = total.astype(dst.dtype)

    each(dst.shape[:-2], one)


def landing_shapes(lead, rows, cols, axes):
    whole = {"z", "x", "y"} & set(lead)
    shapes = []
    for axis in axes:
        whole = whole - {axis}
        dims = tuple(4 for a in ("z", "x", "y") if a in whole)
        shapes.append((6, *dims, rows, cols))
    return shapes


def scatter_flow(g, landing, at, axes, whole, copies):
    whole = set(whole)
    for axis, land in zip(axes, landing):
        up, down, far = moved(at, axis, 1), moved(at, axis, -1), moved(at, axis, 2)
        rest = whole - {axis}
        def blk(place, core):
            return part(g, at, rest, **{axis: place[axis], "c": core})
        s = [
            copies.start(blk(far, 0), land.at[0], up),
            copies.start(blk(far, 1), land.at[1], down),
            copies.start(blk(up, 1), land.at[2], up),
            copies.start(blk(down, 0), land.at[3], down),
        ]
        yield
        s[0].wait_recv()
        add_into(blk(up, 0), land.at[0])
        s.append(copies.start(blk(up, 0), land.at[4], up))
        s[1].wait_recv()
        add_into(blk(down, 1), land.at[1])
        s.append(copies.start(blk(down, 1), land.at[5], down))
        yield
        s[2].wait_recv()
        s[5].wait_recv()
        add_into(blk(at, 1), land.at[2], land.at[5])
        s[3].wait_recv()
        s[4].wait_recv()
        add_into(blk(at, 0), land.at[3], land.at[4])
        for q in s:
            q.wait_send()
        whole = rest


def dot_rows(a, b):
    return lax.dot_general(a, b, (((0,), (0,)), ((), ())), preferred_element_type=jnp.float32)


def rs_kernel(u, dy, n3, dh, att, r1, n2, dcq, catt, r2, vec, gq, out_a, out_b, out_c, out_q,
              u2, dy2, n32, dh2, a2, r2s, vec2, ga, gb, gc, gqs, gql, la1, la2, la3, lb1, lb2, lb3, lc1, lc2, lc3, lq1, lq2,
              fa, fb, fc, send, recv, local):
    at = position()
    partner = moved(at, "c", 1)
    barrier = pltpu.get_barrier_semaphore()
    others = [moved(at, a, b) for a in "zx" for b in (1, -1)]
    ring = [moved(moved(at, "y", b), "c", d) for b in range(4) for d in range(2) if b or d]
    others += ring
    for o in others:
        pl.semaphore_signal(barrier, inc=1, device_id=device(o), device_id_type=MESH)
    pl.semaphore_wait(barrier, len(others))
    copies = Copies(send, recv)
    c = at["c"]
    rows = u.shape[0]

    def half(n, of):
        return pl.ds(pl.multiple_of(of["c"] * (n // 2), 128), n // 2)

    loads, pairs = [], []

    def both(src, dst, split):
        n = src.shape[-1]
        mine = src.at[:, half(n, at)] if split else src
        theirs = src.at[:, half(n, partner)] if split else src
        cp = pltpu.make_async_copy(mine, dst.at[pl.ds(0, rows)], local.at[len(loads)])
        cp.start()
        loads.append(cp)
        pairs.append(copies.start(theirs, dst.at[pl.ds(rows, rows)], partner))
        return len(loads) - 1

    def ready(k):
        loads[k].wait()
        pairs[k].wait()

    kq = pltpu.make_async_copy(gq, gqs, local.at[31])
    kq.start()
    pq = copies.start(gq.at[:, :, :, :, :, half(gq.shape[-1], partner)], gql, partner)
    kb = [both(n3, n32, False), both(dh, dh2, True)]
    ka = [both(u, u2, False), both(dy, dy2, True)]
    kc = []
    for k, (a, b) in enumerate(((att, r1), (n2, dcq), (catt, r2))):
        kc += [both(a, a2.at[k], False), both(b, r2s.at[k], True)]
    kv = pltpu.make_async_copy(vec.at[c], vec2.at[0], local.at[30])
    kv.start()
    pv = copies.start(vec.at[partner["c"]], vec2.at[1], partner)

    def grad_b(z):
        lhs = n32[:, pl.ds(pl.multiple_of(z * 256, 256), 256)]
        for k in range(4):
            g = dot_rows(lhs, dh2[:, k * 512:(k + 1) * 512])
            gb[z, :, :, :, :, k * 512:(k + 1) * 512] = g.reshape(4, 2, 4, 8, 512).astype(jnp.bfloat16)

    def grad_a(z, x):
        lhs = u2[:, pl.ds(pl.multiple_of((z * 4 + x) * 256, 256), 256)]
        ga[z, x] = dot_rows(lhs, dy2[...]).reshape(2, 4, 32, 512).astype(jnp.bfloat16)

    def grad_c(k, z):
        g = dot_rows(a2[k, :, pl.ds(pl.multiple_of(z * 256, 256), 256)], r2s[k])
        gc[z, :, :, :, :, k * 512:(k + 1) * 512] = g.reshape(4, 2, 4, 8, 512).astype(jnp.bfloat16)

    def loop(n, body):
        def step(i, _):
            body(i)
            return 0
        lax.fori_loop(0, n, step, 0)

    kq.wait()
    pq.wait()
    add_into(gqs.at[:, :, :, :, :, half(gq.shape[-1], at)], gql)
    fq = scatter_flow(gqs.at[:, :, :, :, :, half(gq.shape[-1], at)], (lq1, lq2), at, ("x", "z"), {"z", "x", "y"}, copies)
    for k in kb:
        ready(k)
    far_z = moved(at, "z", 2)["z"]
    loop(4, lambda i: grad_b(lax.rem(far_z + i, 4)))
    fl_b = scatter_flow(gb, (lb1, lb2, lb3), at, ("z", "y", "x"), {"z", "x", "y"}, copies)
    next(fl_b)
    for k in ka:
        ready(k)
    loop(16, lambda i: grad_a(lax.rem(i, 4), lax.div(i, 4)))
    fl_a = scatter_flow(ga, (la1, la2, la3), at, ("x", "z", "y"), {"z", "x", "y"}, copies)
    next(fl_a)
    for k in kc:
        ready(k)
    for k in range(3):
        loop(4, functools.partial(grad_c, k))
    kv.wait()
    pv.wait()

    def vec_sum(index):
        z, x = index
        total = vec2[0, z, x].astype(jnp.float32) + vec2[1, z, x].astype(jnp.float32)
        gc[z, x, :, :, :, 1536:1664] = total.astype(jnp.bfloat16)

    each((4, 4), vec_sum)
    fl_c = scatter_flow(gc, (lc1, lc2, lc3), at, ("y", "x", "z"), {"z", "x", "y"}, copies)
    next(fl_c)
    next(fq)
    live = [fl_b, fl_a, fl_c, fq]
    while live:
        for f in list(live):
            if next(f, "end") == "end":
                live.remove(f)

    last = []
    for g, f, o in ((ga, fa, out_a), (gb, fb, out_b), (gc, fc, out_c)):
        theirs = g.at[at["z"], at["x"], partner["c"], at["y"]]
        last.append(copies.start(theirs, f, partner))
    qh = gqs.at[:, :, :, :, :, half(gq.shape[-1], at)]
    for o in ring:
        last.append(copies.start(qh.at[at["z"], at["x"], o["c"], o["y"]], out_q.at[c, at["y"]], o))
    mine_q = pltpu.make_async_copy(qh.at[at["z"], at["x"], c, at["y"]], out_q.at[c, at["y"]], local.at[29])
    mine_q.start()
    for g, o in ((ga, out_a), (gb, out_b), (gc, out_c)):
        o[c] = g[at["z"], at["x"], c, at["y"]]
    for s in last:
        s.wait()
    for f, o in ((fa, out_a), (fb, out_b), (fc, out_c)):
        o[partner["c"]] = f[...]
    mine_q.wait()


def reduced(u, dy, n3, dh, att, r1, n2, dcq, catt, r2, vec, gq):
    bf = jnp.bfloat16
    n_c, n_q = 1664, gq.shape[-1] // 2
    lead = ("z", "x", "y")
    scratch = [
        pltpu.VMEM((512, 4096), bf), pltpu.VMEM((512, 512), bf), pltpu.VMEM((512, 1024), bf), pltpu.VMEM((512, 2048), bf),
        pltpu.VMEM((3, 512, 1024), bf), pltpu.VMEM((3, 512, 512), bf), pltpu.VMEM((2, 4, 4, 2, 4, 8, 128), bf),
        pltpu.VMEM((4, 4, 2, 4, 32, 512), bf), pltpu.VMEM((4, 4, 2, 4, 8, 2048), bf), pltpu.VMEM((4, 4, 2, 4, 8, n_c), bf),
        pltpu.VMEM((4, 4, 2, 4, 8, 2 * n_q), bf), pltpu.VMEM((4, 4, 2, 4, 8, n_q), bf),
    ]
    for r, n, axes in ((32, 512, "xzy"), (8, 2048, "zyx"), (8, n_c, "yxz"), (8, n_q, "xz")):
        scratch += [pltpu.VMEM(s, bf) for s in landing_shapes(lead, r, n, axes)]
    scratch += [pltpu.VMEM((32, 512), bf), pltpu.VMEM((8, 2048), bf), pltpu.VMEM((8, n_c), bf)]
    n = 100
    scratch += [pltpu.SemaphoreType.DMA((n,)), pltpu.SemaphoreType.DMA((n,)), pltpu.SemaphoreType.DMA((32,))]
    outs = [jax.ShapeDtypeStruct(s, bf) for s in ((2, 32, 512), (2, 8, 2048), (2, 8, n_c), (2, 4, 8, n_q))]
    anywhere, vmem = pl.BlockSpec(memory_space=pl.ANY), pl.BlockSpec(memory_space=pltpu.VMEM)
    return pl.pallas_call(
        rs_kernel, out_shape=outs, in_specs=[anywhere] * 12, out_specs=[vmem] * 4,
        scratch_shapes=scratch,
        compiler_params=pltpu.CompilerParams(collective_id=1, has_side_effects=True, vmem_limit_bytes=60 << 20),
        name="reduce_gradients",
    )(u, dy, n3, dh, att, r1, n2, dcq, catt, r2, vec, gq)


HEADS = 16
HEAD_DIM = 64
EPSILON = 1e-05
MASKED = -1e30


def layer_norm(values, gain, shift):
    center = jnp.mean(values, axis=-1, keepdims=True)
    centred = values - center
    spread = jnp.mean(centred * centred, axis=-1, keepdims=True)
    return centred * lax.rsqrt(spread + EPSILON) * gain + shift


def gelu_exact(values):
    return jax.nn.gelu(values, approximate=False)


def matmul(left, right):
    return jnp.dot(left, right, preferred_element_type=jnp.float32)


def dot_cols(left, right):
    return lax.dot_general(left, right, (((1,), (1,)), ((), ())), preferred_element_type=jnp.float32)


def split_heads(values, head_count):
    return values.reshape(values.shape[0], head_count, -1)


def attend_forward(queries, key_rows, value_rows, visible, head_count):
    q, k, v = (split_heads(t, head_count) for t in (queries, key_rows, value_rows))
    scores = jnp.einsum("qhe,khe->hqk", q, k, preferred_element_type=jnp.float32) * HEAD_DIM ** -0.5
    scores = jnp.where(visible[None], scores, MASKED)
    peak = jnp.max(scores, axis=-1, keepdims=True)
    expon = jnp.exp(scores - peak)
    total = jnp.sum(expon, axis=-1, keepdims=True)
    weights = (expon / total).astype(jnp.bfloat16)
    mixed = jnp.einsum("hqk,khe->qhe", weights, v, preferred_element_type=jnp.float32)
    return mixed.reshape(queries.shape[0], -1).astype(jnp.bfloat16), peak, total


def attend_backward(queries, key_rows, value_rows, visible, peak, total, grad_mixed, head_count):
    q, k, v, g = (split_heads(t, head_count) for t in (queries, key_rows, value_rows, grad_mixed))
    scale = HEAD_DIM ** -0.5
    scores = jnp.einsum("qhe,khe->hqk", q, k, preferred_element_type=jnp.float32) * scale
    scores = jnp.where(visible[None], scores, MASKED)
    probs = jnp.exp(scores - peak) / total
    rounded = probs.astype(jnp.bfloat16)
    grad_v = jnp.einsum("hqk,qhe->khe", rounded, g, preferred_element_type=jnp.float32)
    grad_p = jnp.einsum("qhe,khe->hqk", g, v, preferred_element_type=jnp.float32)
    inner = jnp.sum(grad_p * probs, axis=-1, keepdims=True)
    grad_s = (probs * (grad_p - inner)).astype(jnp.bfloat16)
    grad_q = jnp.einsum("hqk,khe->qhe", grad_s, k, preferred_element_type=jnp.float32) * scale
    grad_k = jnp.einsum("hqk,qhe->khe", grad_s, q, preferred_element_type=jnp.float32) * scale
    n, m = queries.shape[0], key_rows.shape[0]
    return grad_q.reshape(n, -1), grad_k.reshape(m, -1), grad_v.reshape(m, -1)


def exchanged(x):
    return lax.all_to_all(x, "seq", split_axis=0, concat_axis=0, tiled=True)


def local(tokens, captions, cap_lengths, w_qkv, w_self_out, w_cross_q, w_cross_kv, w_cross_out, w_in, w_out,
          norm_gains, norm_shifts, out_biases, in_bias, out_grad):
    bf, f32 = jnp.bfloat16, jnp.float32
    vectors = jnp.concatenate([norm_gains.T, norm_shifts.T, out_biases.T, in_bias.reshape(8, 4)], axis=1)
    c_in = jnp.concatenate([w_self_out, w_cross_q, w_cross_out, jnp.pad(vectors, ((0, 0), (0, 256 - 13)))], axis=1)
    q_in = jnp.concatenate([w_qkv, w_cross_kv], axis=1).reshape(8, 5, 4, 256).transpose(2, 0, 1, 3).reshape(4, 8, 1280)
    c_g, win_g, wout_g, q_g, x_g, cap_g = all_gathered(c_in, w_in, w_out, q_in, tokens[0], captions[0])
    wc, full_in, full_out, wq = c_g.reshape(1024, -1), win_g.reshape(1024, -1), wout_g.reshape(4096, 1024), q_g.reshape(1024, 1280)
    full_self_out, full_cross_q, full_cross_out = wc[:, :1024], wc[:, 1024:2048], wc[:, 2048:3072]
    vecs = wc[:, 3072:3085].astype(f32)
    gain, shift, bias = vecs[:, :3].T, vecs[:, 3:6].T, vecs[:, 6:9].T
    hidden_bias = vecs[:, 9:13].reshape(4096)

    x_all = x_g.reshape(1024, 1024).astype(f32)
    n1 = layer_norm(x_all, gain[0], shift[0]).astype(bf)
    qkv = matmul(n1, wq[:, :768]).astype(bf)
    q, k, v = qkv[:, :256], qkv[:, 256:512], qkv[:, 512:]
    place = lax.iota(jnp.int32, 1024)
    causal = place[:, None] >= place[None, :]
    att4, peak, total = attend_forward(q, k, v, causal, 4)
    att = exchanged(att4.reshape(4, 256, 256)).transpose(1, 0, 2).reshape(256, 1024)

    e = cap_g.transpose(1, 0, 2).reshape(128, 1024)
    ckv4 = matmul(e, wq[:, 768:]).astype(bf)
    ckv = lax.all_gather(ckv4, "seq", axis=0).reshape(4, 128, 2, 256).transpose(1, 2, 0, 3).reshape(128, 2, 1024)
    ck, cv = ckv[:, 0], ckv[:, 1]

    x = tokens[0].astype(f32)
    x1 = x + matmul(att, full_self_out) + bias[0]
    n2 = layer_norm(x1, gain[1], shift[1]).astype(bf)
    cq = matmul(n2, full_cross_q).astype(bf)
    seen = jnp.broadcast_to(lax.iota(jnp.int32, 128)[None, :] < cap_lengths[0], (256, 128))
    catt, cpeak, ctotal = attend_forward(cq, ck, cv, seen, 16)
    x2 = x1 + matmul(catt, full_cross_out) + bias[1]
    n3 = layer_norm(x2, gain[2], shift[2]).astype(bf)
    h = matmul(n3, full_in) + hidden_bias
    u = gelu_exact(h).astype(bf)
    layer_out = (x2 + matmul(u, full_out) + bias[2]).astype(bf)

    g_out = out_grad[0]
    dy = g_out.astype(f32)
    du = dot_cols(g_out, full_out)
    dh = jax.vjp(gelu_exact, h)[1](du)[0].astype(bf)
    dn3 = dot_cols(dh, full_in)
    d_in_bias = jnp.sum(dh, axis=0, dtype=f32)
    dres, dgain3, dshift3 = jax.vjp(layer_norm, x2, gain[2], shift[2])[1](dn3)
    dx2 = dy + dres
    r2 = dx2.astype(bf)
    dcatt = dot_cols(r2, full_cross_out).astype(bf)
    dcq, dck, dcv = attend_backward(cq, ck, cv, seen, cpeak, ctotal, dcatt, 16)
    dcq = dcq.astype(bf)
    dckv = jnp.concatenate([dck.reshape(128, 4, 256), dcv.reshape(128, 4, 256)], axis=2).transpose(1, 0, 2).astype(bf)
    dckv4 = exchanged(dckv).astype(f32).sum(axis=0).astype(bf)
    dcap = dot_cols(dckv4, wq[:, 768:]).reshape(128, 4, 256).transpose(1, 0, 2).astype(bf)
    captions_grad = exchanged(dcap).astype(f32).sum(axis=0)
    dn2 = dot_cols(dcq, full_cross_q)
    dres, dgain2, dshift2 = jax.vjp(layer_norm, x1, gain[1], shift[1])[1](dn2)
    dx1 = dx2 + dres
    r1 = dx1.astype(bf)
    datt = dot_cols(r1, full_self_out).astype(bf)
    datt4 = exchanged(datt.reshape(256, 4, 256).transpose(1, 0, 2)).reshape(1024, 256)
    dq, dk, dv = attend_backward(q, k, v, causal, peak, total, datt4, 4)
    dqkv = jnp.concatenate([dq, dk, dv], axis=1).astype(bf)
    dn1_part = dot_cols(dqkv, wq[:, :768]).astype(bf)
    dn1 = exchanged(dn1_part.reshape(4, 256, 1024)).astype(f32).sum(axis=0)
    dres, dgain1, dshift1 = jax.vjp(layer_norm, x, gain[0], shift[0])[1](dn1)
    tokens_grad = dx1 + dres

    gq = jnp.concatenate([dot_rows(n1, dqkv), dot_rows(e, dckv4)], axis=1).astype(bf).reshape(4, 4, 2, 4, 8, 1280)
    sums = jnp.stack([dgain1, dgain2, dgain3, dshift1, dshift2, dshift3, dx1.sum(0), dx2.sum(0), dy.sum(0)])
    sums = jnp.concatenate([sums.T, d_in_bias.reshape(1024, 4)], axis=1)
    vec = jnp.stack([jnp.pad(sums[:, :9], ((0, 0), (0, 119))), jnp.pad(sums[:, 9:], ((0, 0), (0, 124)))])
    vec = vec.astype(bf).reshape(2, 4, 4, 2, 4, 8, 128)
    out_a, out_b, out_c, out_q = reduced(u, g_out, n3, dh, att, r1, n2, dcq, catt, r2, vec, gq)
    out_a, out_b, out_c, out_q = (t.astype(f32) for t in (out_a, out_b, out_c, out_q))
    joined = lambda t: jnp.concatenate([t[0], t[1]], axis=1)
    q_out = out_q.transpose(2, 1, 0, 3).reshape(8, 4, 5, 256).transpose(0, 2, 1, 3).reshape(8, 5120)
    v0, v1 = out_c[0, :, 1536:1545], out_c[1, :, 1536:1540]
    return (
        layer_out[None], tokens_grad[None], captions_grad[None],
        q_out[:, :3072], joined(out_c[..., :512]), joined(out_c[..., 512:1024]), q_out[:, 3072:], joined(out_c[..., 1024:1536]),
        joined(out_b), joined(out_a), v0[:, :3].T, v0[:, 3:6].T, v0[:, 6:9].T, v1.reshape(32),
    )


def solution(mesh):
    rows, tokens, vectors = P(("dp", "seq"), None), P("dp", "seq", None), P(None, ("dp", "seq"))
    captions = P("dp", None, "seq")
    return jax.shard_map(
        local, mesh=mesh,
        in_specs=(tokens, captions, P("dp"), *[rows] * 7, *[vectors] * 3, P(("dp", "seq")), tokens),
        out_specs=(tokens, tokens, captions, *[rows] * 7, *[vectors] * 3, P(("dp", "seq"))),
        check_vma=False,
    )
```

```python
import functools

import jax
import jax.numpy as jnp
from jax import lax
from jax.experimental import pallas as pl
from jax.experimental.pallas import tpu as pltpu
from jax.sharding import PartitionSpec as P

MESH = pl.DeviceIdType.MESH
def position():
    dp, y = lax.axis_index("dp"), lax.axis_index("seq")
    return {"z": lax.div(dp, 8), "x": lax.rem(lax.div(dp, 2), 4), "c": lax.rem(dp, 2), "y": y}


def device(at):
    return (at["z"] * 8 + at["x"] * 2 + at["c"], at["y"])


def moved(at, axis, by):
    size = 2 if axis == "c" else 4
    return {**at, axis: lax.rem(at[axis] + by + size, size)}


class Copies:
    def __init__(self, send, recv):
        self.send, self.recv, self.used = send, recv, 0

    def start(self, src, dst, at):
        k = self.used
        self.used += 1
        copy = pltpu.make_async_remote_copy(src_ref=src, dst_ref=dst, send_sem=self.send.at[k], recv_sem=self.recv.at[k], device_id=device(at), device_id_type=MESH)
        copy.start()
        return copy


def block(ref, at, whole, cols, **fixed):
    idx = []
    for axis in ("z", "x", "c", "y"):
        idx.append(fixed[axis] if axis in fixed else slice(None) if axis in whole else at[axis])
    return ref.at[(*idx, slice(None), cols)]


def gather_flow(ref, at, cols, axes, whole, copies, partner, done):
    whole = set(whole)
    for axis in axes:
        up, down = moved(at, axis, 1), moved(at, axis, -1)
        own = block(ref, at, whole, cols)
        a = copies.start(own, own, up)
        b = copies.start(own, own, down)
        yield
        a.wait_recv()
        b.wait_recv()
        low = block(ref, down, whole, cols, c=0)
        high = block(ref, up, whole, cols, c=1)
        c = copies.start(low, low, up)
        d = copies.start(high, high, down)
        for p in (down, up):
            got = block(ref, p, whole, cols)
            done.append(copies.start(got, got, partner))
        yield
        c.wait_recv()
        d.wait_recv()
        far = block(ref, moved(at, axis, 2), whole, cols)
        done.append(copies.start(far, far, partner))
        for s in (a, b, c, d):
            s.wait_send()
        whole.add(axis)


EPSILON = 1e-05
MASKED = -1e30
SCALE = 64 ** -0.5
BF, F32 = jnp.bfloat16, jnp.float32
def mm(a, b):
    return jnp.dot(a, b, preferred_element_type=F32)


def mm_rows(a, b):
    return lax.dot_general(a, b, (((0,), (0,)), ((), ())), preferred_element_type=F32)


def mm_cols(a, b):
    return lax.dot_general(a, b, (((1,), (1,)), ((), ())), preferred_element_type=F32)


def normed(v):
    centred = v - jnp.mean(v, axis=-1, keepdims=True)
    r = lax.rsqrt(jnp.mean(centred * centred, axis=-1, keepdims=True) + EPSILON)
    return centred * r, r


def norm_back(v, d, gain):
    z, r = normed(v)
    w = d * gain
    dv = r * (w - jnp.mean(w, axis=-1, keepdims=True) - z * jnp.mean(w * z, axis=-1, keepdims=True))
    return dv, jnp.sum(d * z, axis=0, keepdims=True), jnp.sum(d, axis=0, keepdims=True)


def loop(n, body):
    def step(i, _):
        body(i)
        return 0

    lax.fori_loop(0, n, step, 0)


def gelu_both(h):
    cdf = 0.5 * (1.0 + lax.erf(h * (0.5 ** 0.5)))
    return h * cdf, cdf + h * jnp.exp(-0.5 * h * h) * (1.0 / (2.0 * 3.141592653589793) ** 0.5)


def lanes_of(pair_shape, head):
    lane = lax.broadcasted_iota(jnp.int32, pair_shape, 1)
    return (lane < 64) if head == 0 else (lane >= 64)


def middle_kernel(length, x_in, att_in, dy_in, ck_in, cv_in, vec, inb, wc, win, wout,
                  out, dx1_o, datt_o, dckv_o, n2_o, n3_o, catt_o, u_o, dh_o, r1_o, r2_o, dcq_o, sums, dinb,
                  so, wcq, co, wi, wo, x1, x2, probs, cq, ya, dn, dca, sem):
    loads = []
    for k, dst in enumerate((so, wcq, co)):
        loads.append(pltpu.make_async_copy(wc.at[:, pl.ds(k * 1024, 1024)], dst, sem.at[k]))
    for l in loads:
        l.start()
    chunk = 512
    n_chunk = wi.shape[1] // chunk

    def ff_loads(i):
        cols = pl.ds(pl.multiple_of(i * chunk, chunk), chunk)
        return (pltpu.make_async_copy(win.at[:, cols], wi.at[:, cols], sem.at[3 + 2 * i]),
                pltpu.make_async_copy(wout.at[cols], wo.at[cols], sem.at[4 + 2 * i]))

    for i in range(n_chunk):
        for l in ff_loads(i):
            l.start()

    step_rows = 64
    def by_rows(body):
        loop(256 // step_rows, lambda i: body(pl.ds(pl.multiple_of(i * step_rows, step_rows), step_rows)))

    def row(k):
        return vec[k:k + 1, :]

    sums[...] = jnp.zeros_like(sums)

    loads[0].wait()
    x1[...] = mm(att_in[...], so[...])

    def after_self(r):
        v = x_in[r, :].astype(F32) + x1[r, :] + row(6)
        x1[r, :] = v
        z, _ = normed(v)
        n2_o[r, :] = (z * row(1) + row(4)).astype(BF)

    by_rows(after_self)
    loads[1].wait()
    cq[...] = mm(n2_o[...], wcq[...]).astype(BF)

    seen = lax.broadcasted_iota(jnp.int32, (128, 256), 0) < length[0]

    def cross_forward(p):
        cols = pl.ds(pl.multiple_of(p * 128, 128), 128)
        k, v, q = ck_in[:, cols], cv_in[:, cols], cq[:, cols]
        mixed = []
        for head in range(2):
            qh = jnp.where(lanes_of(q.shape, head), q, jnp.zeros_like(q))
            s = jnp.where(seen, mm_cols(k, qh) * SCALE, MASKED)
            e = jnp.exp(s - jnp.max(s, axis=0, keepdims=True))
            prob = e / jnp.sum(e, axis=0, keepdims=True)
            probs[2 * p + head] = prob
            mixed.append(mm_rows(prob.astype(BF), v))
        catt_o[:, cols] = jnp.where(lanes_of(q.shape, 0), mixed[0], mixed[1]).astype(BF)

    loop(8, cross_forward)
    loads[2].wait()
    x2[...] = mm(catt_o[...], co[...])

    def after_cross(r):
        v = x1[r, :] + x2[r, :] + row(7)
        x2[r, :] = v
        z, _ = normed(v)
        n3_o[r, :] = (z * row(2) + row(5)).astype(BF)

    by_rows(after_cross)

    ya[...] = jnp.zeros_like(ya)
    dn[...] = jnp.zeros_like(dn)

    def feed(i):
        for l in ff_loads(i):
            l.wait()
        cols = pl.ds(pl.multiple_of(i * chunk, chunk), chunk)
        h = mm(n3_o[...], wi[:, cols]) + inb[:, cols]
        u, slope = gelu_both(h)
        u = u.astype(BF)
        u_o[:, cols] = u
        ya[...] += mm(u, wo[cols, :])
        dh = (mm_cols(dy_in[...], wo[cols, :]) * slope).astype(BF)
        dh_o[:, cols] = dh
        dinb[:, cols] = jnp.sum(dh.astype(F32), axis=0, keepdims=True)
        dn[...] += mm_cols(dh, wi[:, cols])

    loop(n_chunk, feed)

    def after_feed(r):
        v = x2[r, :]
        out[r, :] = (v + ya[r, :] + row(8)).astype(BF)
        dy = dy_in[r, :].astype(F32)
        dv, dgain, dshift = norm_back(v, dn[r, :], row(2))
        d = dy + dv
        x2[r, :] = d
        r2_o[r, :] = d.astype(BF)
        sums[2:3, :] += dgain
        sums[5:6, :] += dshift
        sums[7:8, :] += jnp.sum(d, axis=0, keepdims=True)
        sums[8:9, :] += jnp.sum(dy, axis=0, keepdims=True)

    by_rows(after_feed)

    dca[...] = mm_cols(r2_o[...], co[...]).astype(BF)

    def cross_backward(p):
        cols = pl.ds(pl.multiple_of(p * 128, 128), 128)
        k, v, q, d = ck_in[:, cols], cv_in[:, cols], cq[:, cols], dca[:, cols]
        dk = dv = jnp.zeros((128, 128), F32)
        dq = []
        for head in range(2):
            lanes = lanes_of(q.shape, head)
            qh = jnp.where(lanes, q, jnp.zeros_like(q))
            dout = jnp.where(lanes, d, jnp.zeros_like(d))
            prob = probs[2 * p + head]
            dp = mm_cols(v, dout)
            ds = (prob * (dp - jnp.sum(dp * prob, axis=0, keepdims=True))).astype(BF)
            dv += mm(prob.astype(BF), dout)
            dk += mm(ds, qh)
            dq.append(mm_rows(ds, k))
        dcq_o[:, cols] = (jnp.where(lanes_of(q.shape, 0), dq[0], dq[1]) * SCALE).astype(BF)
        dckv_o[:, cols] = (dk * SCALE).astype(BF)
        dckv_o[:, pl.ds(pl.multiple_of(1024 + p * 128, 128), 128)] = dv.astype(BF)

    loop(8, cross_backward)
    dn[...] = mm_cols(dcq_o[...], wcq[...])

    def before_cross(r):
        dv, dgain, dshift = norm_back(x1[r, :], dn[r, :], row(1))
        d = x2[r, :] + dv
        dx1_o[r, :] = d
        r1_o[r, :] = d.astype(BF)
        sums[1:2, :] += dgain
        sums[4:5, :] += dshift
        sums[6:7, :] += jnp.sum(d, axis=0, keepdims=True)

    by_rows(before_cross)
    datt_o[...] = mm_cols(r1_o[...], so[...]).astype(BF)


def middle(length, x, att, dy, ck, cv, vec, inb, wc, win, wout):
    s = jax.ShapeDtypeStruct
    outs = [s((256, 1024), BF), s((256, 1024), F32), s((256, 1024), BF), s((128, 2048), BF), s((256, 1024), BF), s((256, 1024), BF),
            s((256, 1024), BF), s((256, 4096), BF), s((256, 4096), BF), s((256, 1024), BF), s((256, 1024), BF), s((256, 1024), BF),
            s((16, 1024), F32), s((1, 4096), F32)]
    vm, anywhere = pl.BlockSpec(memory_space=pltpu.VMEM), pl.BlockSpec(memory_space=pl.ANY)
    scratch = [pltpu.VMEM((1024, 1024), BF)] * 3 + [pltpu.VMEM((1024, 4096), BF), pltpu.VMEM((4096, 1024), BF)]
    scratch += [pltpu.VMEM((256, 1024), F32)] * 2 + [pltpu.VMEM((16, 128, 256), F32), pltpu.VMEM((256, 1024), BF)]
    scratch += [pltpu.VMEM((256, 1024), F32)] * 2 + [pltpu.VMEM((256, 1024), BF), pltpu.SemaphoreType.DMA((19,))]
    return pl.pallas_call(
        middle_kernel, out_shape=outs,
        in_specs=[pl.BlockSpec(memory_space=pltpu.SMEM)] + [vm] * 7 + [anywhere] * 3, out_specs=[vm] * len(outs),
        scratch_shapes=scratch, compiler_params=pltpu.CompilerParams(vmem_limit_bytes=60 << 20),
        name="middle",
    )(length, x, att, dy, ck, cv, vec, inb, wc, win, wout)


BLOCK = 256
def causal_keep(n, at):
    keys = lax.broadcasted_iota(jnp.int32, (n, BLOCK), 0)
    return keys <= lax.broadcasted_iota(jnp.int32, (n, BLOCK), 1) + at


def project(x, wq, vec, n1, qkv):
    def rows(i):
        r = pl.ds(pl.multiple_of(i * 128, 128), 128)
        z, _ = normed(x[r, :].astype(F32))
        n1[r, :] = (z * vec[0:1, :] + vec[3:4, :]).astype(BF)

    loop(8, rows)

    def cols(i):
        r = pl.ds(pl.multiple_of(i * BLOCK, BLOCK), BLOCK)
        qkv[r, :] = mm(n1[r, :], wq[:, 0:768]).astype(BF)

    loop(4, cols)


def self_forward(qkv, att, lse):
    def pair(p):
        for i in range(1024 // BLOCK):
            n, r = (i + 1) * BLOCK, slice(i * BLOCK, (i + 1) * BLOCK)
            at = lambda part: pl.ds(pl.multiple_of(part * 256 + p * 128, 128), 128)
            q, k, v = qkv[r, at(0)], qkv[0:n, at(1)], qkv[0:n, at(2)]
            keep = causal_keep(n, i * BLOCK)
            mixed = []
            for head in range(2):
                qh = jnp.where(lanes_of(q.shape, head), q, jnp.zeros_like(q))
                s = jnp.where(keep, mm_cols(k, qh) * SCALE, MASKED)
                top = jnp.max(s, axis=0, keepdims=True)
                e = jnp.exp(s - top)
                total = jnp.sum(e, axis=0, keepdims=True)
                lse[2 * p + head, :, r] = top + jnp.log(total)
                mixed.append(mm_rows((e * (1.0 / total)).astype(BF), v))
            att[r, at(0)] = jnp.where(lanes_of(q.shape, 0), mixed[0], mixed[1]).astype(BF)

    loop(2, pair)


def self_backward(qkv, lse, datt, dqkv, dk, dv):
    def pair(p):
        at = lambda part: pl.ds(pl.multiple_of(part * 256 + p * 128, 128), 128)
        dk[...] = jnp.zeros_like(dk)
        dv[...] = jnp.zeros_like(dv)
        for i in range(1024 // BLOCK):
            n, r = (i + 1) * BLOCK, slice(i * BLOCK, (i + 1) * BLOCK)
            q, k, v, d = qkv[r, at(0)], qkv[0:n, at(1)], qkv[0:n, at(2)], datt[r, at(0)]
            keep = causal_keep(n, i * BLOCK)
            dq = []
            for head in range(2):
                lanes = lanes_of(q.shape, head)
                qh = jnp.where(lanes, q, jnp.zeros_like(q))
                dout = jnp.where(lanes, d, jnp.zeros_like(d))
                prob = jnp.where(keep, jnp.exp(mm_cols(k, qh) * SCALE - lse[2 * p + head, :, r]), 0.0)
                dp = mm_cols(v, dout)
                ds = (prob * (dp - jnp.sum(dp * prob, axis=0, keepdims=True))).astype(BF)
                dv[0:n, :] += mm(prob.astype(BF), dout)
                dk[0:n, :] += mm(ds, qh)
                dq.append(mm_rows(ds, k))
            dqkv[r, at(0)] = (jnp.where(lanes_of(q.shape, 0), dq[0], dq[1]) * SCALE).astype(BF)
        dqkv[:, at(1)] = (dk[...] * SCALE).astype(BF)
        dqkv[:, at(2)] = dv[...].astype(BF)

    loop(2, pair)


def greet(others):
    barrier = pltpu.get_barrier_semaphore()
    for o in others:
        pl.semaphore_signal(barrier, inc=1, device_id=device(o), device_id_type=MESH)
    pl.semaphore_wait(barrier, len(others))


def half(n, of):
    return pl.ds(pl.multiple_of(of["c"] * (n // 2), 128), n // 2)


def finish(flows):
    live = list(flows)
    while live:
        for f in list(live):
            if next(f, "end") == "end":
                live.remove(f)


def quarter(of):
    return pl.ds(pl.multiple_of(of["y"] * 256, 256), 256)


def gather_kernel(c_in, win_in, wout_in, q_in, x_in, cap_in, c_g, win_g, wout_g, x_g, wq_o, qkv, lse, att_o, ck_o, cv_o, e_o, vec,
                  q_g, n1, att, ckv, send, recv, local):
    at = position()
    partner = moved(at, "c", 1)
    row = [moved(at, "y", b) for b in (1, 3, 2)]
    greet([moved(at, a, b) for a in "zx" for b in (1, -1)] + row + [partner])
    copies = Copies(send, recv)
    me = (at["z"], at["x"], at["c"], at["y"])
    kept, sent = [], []

    def keep(src, dst):
        cp = pltpu.make_async_copy(src, dst, local.at[len(kept)])
        cp.start()
        kept.append(cp)

    keep(q_in.at[at["y"]], q_g.at[me])
    qx = [copies.start(q_in.at[to["y"]], q_g.at[me], to) for to in row]
    pairs = [copies.start(src, dst.at[me], partner) for src, dst in ((wout_in, wout_g), (win_in, win_g), (c_in, c_g))]
    for src, dst in ((wout_in, wout_g), (win_in, win_g), (c_in, c_g)):
        keep(src, dst.at[me])
    keep(x_in, x_g.at[at["y"]])
    keep(cap_in, e_o.at[:, quarter(at)])
    up, down = row[0], row[1]
    xx = [copies.start(x_in, x_g.at[at["y"]], to) for to in (up, down)]
    ee = [copies.start(cap_in, e_o.at[:, quarter(at)], to) for to in row]
    for s in kept + qx:
        s.wait()
    q_own = block(q_g, at, {"y"}, slice(None))
    qp = copies.start(q_own, q_own, partner)
    for s in pairs:
        s.wait()
    q_done, done = [], []
    fq = gather_flow(q_g, at, half(q_g.shape[-1], at), ("x", "z"), {"y", "c"}, copies, partner, q_done)
    fa = gather_flow(wout_g, at, half(1024, at), ("y", "z", "x"), {"c"}, copies, partner, done)
    fb = gather_flow(win_g, at, half(4096, at), ("x", "y", "z"), {"c"}, copies, partner, done)
    fc = gather_flow(c_g, at, half(c_g.shape[-1], at), ("z", "x", "y"), {"c"}, copies, partner, done)
    flows = [fa, fb, fc]
    for f in flows:
        next(f)
    qp.wait()
    next(fq)
    for s in xx:
        s.wait()
    low, high = slice(0, 128), slice(128, 256)
    x2 = [copies.start(x_g.at[down["y"], low], x_g.at[down["y"], low], up), copies.start(x_g.at[up["y"], high], x_g.at[up["y"], high], down)]
    for _ in range(4):
        next(fq, None)
        for f in flows:
            next(f)
    for s in x2 + ee + q_done:
        s.wait()

    wide = q_g[:, :, :, :, :, 1280:1408].astype(F32).reshape(1024, 128)
    vec[...] = wide.T[0:16, :]
    wq_o[...] = q_g[:, :, :, :, :, 0:1280].reshape(1024, 1280)
    x_rows = x_g.reshape(1024, 1024)
    project(x_rows, wq_o, vec, n1, qkv)
    ckv[...] = mm(e_o[...], wq_o[:, 768:1280]).astype(BF)
    self_forward(qkv, att, lse)
    for to in row:
        sent.append(copies.start(att.at[quarter(to)], att_o.at[:, quarter(at)], to))
        sent.append(copies.start(ckv.at[:, 0:256], ck_o.at[:, quarter(at)], to))
        sent.append(copies.start(ckv.at[:, 256:512], cv_o.at[:, quarter(at)], to))
    late = len(kept)
    keep(att.at[quarter(at)], att_o.at[:, quarter(at)])
    keep(ckv.at[:, 0:256], ck_o.at[:, quarter(at)])
    keep(ckv.at[:, 256:512], cv_o.at[:, quarter(at)])
    finish(flows)
    for s in sent + done + kept[late:]:
        s.wait()


def gathered(c_in, win_in, wout_in, q_in, x_in, cap_in):
    s = jax.ShapeDtypeStruct
    anywhere, vm = pl.BlockSpec(memory_space=pl.ANY), pl.BlockSpec(memory_space=pltpu.VMEM)
    outs = [s((4, 4, 2, 4, *a.shape), BF) for a in (c_in, win_in, wout_in)]
    outs += [s((4, 256, 1024), BF), s((1024, 1280), BF), s((1024, 768), BF), s((4, 1, 1024), F32), s((256, 1024), BF),
             s((128, 1024), BF), s((128, 1024), BF), s((128, 1024), BF), s((16, 1024), F32)]
    n = 100
    return pl.pallas_call(
        gather_kernel, out_shape=outs, in_specs=[anywhere] * 6, out_specs=[anywhere] * 3 + [vm] * 9,
        scratch_shapes=[pltpu.VMEM((4, 4, 2, 4, *q_in.shape[1:]), BF), pltpu.VMEM((1024, 1024), BF), pltpu.VMEM((1024, 256), BF),
                        pltpu.VMEM((128, 512), BF), pltpu.SemaphoreType.DMA((n,)), pltpu.SemaphoreType.DMA((n,)), pltpu.SemaphoreType.DMA((10,))],
        compiler_params=pltpu.CompilerParams(collective_id=0, has_side_effects=True, vmem_limit_bytes=60 << 20),
        name="gather_and_attend",
    )(c_in, win_in, wout_in, q_in, x_in, cap_in)


ORDER = ("z", "x", "c", "y")
def part(ref, at, whole, **fixed):
    return ref.at[tuple(fixed[a] if a in fixed else slice(None) if a in whole else at[a] for a in ORDER)]


def each(shape, body):
    total = 1
    for s in shape:
        total *= s

    def step(i, _):
        index, rest = [], i
        for s in reversed(shape):
            index.insert(0, lax.rem(rest, s))
            rest = lax.div(rest, s)
        body(tuple(index))
        return 0

    if total == 1:
        body((0,) * len(shape))
    else:
        lax.fori_loop(0, total, step, 0)


def add_into(dst, *srcs):
    def one(index):
        total = dst[index].astype(jnp.float32)
        for s in srcs:
            total += s[index].astype(jnp.float32)
        dst[index] = total.astype(dst.dtype)

    each(dst.shape[:-2], one)


def landing_shapes(lead, rows, cols, axes):
    whole = {"z", "x", "y"} & set(lead)
    shapes = []
    for axis in axes:
        whole = whole - {axis}
        dims = tuple(4 for a in ("z", "x", "y") if a in whole)
        shapes.append((6, *dims, rows, cols))
    return shapes


def scatter_flow(g, landing, at, axes, whole, copies):
    whole = set(whole)
    for axis, land in zip(axes, landing):
        up, down, far = moved(at, axis, 1), moved(at, axis, -1), moved(at, axis, 2)
        rest = whole - {axis}
        def blk(place, core):
            return part(g, at, rest, **{axis: place[axis], "c": core})
        s = [
            copies.start(blk(far, 0), land.at[0], up),
            copies.start(blk(far, 1), land.at[1], down),
            copies.start(blk(up, 1), land.at[2], up),
            copies.start(blk(down, 0), land.at[3], down),
        ]
        yield
        s[0].wait_recv()
        add_into(blk(up, 0), land.at[0])
        s.append(copies.start(blk(up, 0), land.at[4], up))
        s[1].wait_recv()
        add_into(blk(down, 1), land.at[1])
        s.append(copies.start(blk(down, 1), land.at[5], down))
        yield
        s[2].wait_recv()
        s[5].wait_recv()
        add_into(blk(at, 1), land.at[2], land.at[5])
        s[3].wait_recv()
        s[4].wait_recv()
        add_into(blk(at, 0), land.at[3], land.at[4])
        for q in s:
            q.wait_send()
        whole = rest


def reduce_kernel(u, dy, n3, dh, att, r1, n2, dcq, catt, r2, datt, dckv, vec_sums, x_all, qkv, lse, wq, e, dx1, vec,
                  out_a, out_b, out_c, out_q, tok, cap,
                  u2, dy2, n32, dh2, a2, r2s, ga, gb, gc, gq, gql, datt4, dckv4, dcap, dcap4, dqkv, n1, dk, dv, dn, dn4, v13,
                  la1, la2, la3, lb1, lb2, lb3, lc1, lc2, lc3, lq1, lq2, fa, fb, fc, fq, send, recv, local):
    at = position()
    partner = moved(at, "c", 1)
    row = [moved(at, "y", b) for b in (1, 3, 2)]
    ring = row + [moved(o, "c", 1) for o in row] + [partner]
    greet([moved(at, a, b) for a in "zx" for b in (1, -1)] + ring)
    copies = Copies(send, recv)
    c, y = at["c"], at["y"]
    loads, pairs = [], []

    def both(src, dst, split):
        n = src.shape[-1]
        rows = src.shape[0]
        mine = src.at[:, half(n, at)] if split else src
        theirs = src.at[:, half(n, partner)] if split else src
        cp = pltpu.make_async_copy(mine, dst.at[pl.ds(0, rows)], local.at[len(loads)])
        cp.start()
        loads.append(cp)
        pairs.append(copies.start(theirs, dst.at[pl.ds(rows, rows)], partner))
        return len(loads) - 1

    def ready(*ks):
        for k in ks:
            loads[k].wait()
            pairs[k].wait()

    kb = [both(n3, n32, False), both(dh, dh2, True)]
    own_rows = pl.ds(pl.multiple_of(y * 256, 256), 256)
    d_own = pltpu.make_async_copy(datt.at[:, quarter(at)], datt4.at[own_rows], local.at[30])
    d_own.start()
    dd = [copies.start(datt.at[:, quarter(to)], datt4.at[own_rows], to) for to in row]
    kv_own = [pltpu.make_async_copy(dckv.at[:, pl.ds(pl.multiple_of(k * 1024 + y * 256, 256), 256)], dckv4.at[y, :, pl.ds(k * 256, 256)], local.at[28 + k]) for k in range(2)]
    for s in kv_own:
        s.start()
    kvs = [copies.start(dckv.at[:, pl.ds(pl.multiple_of(k * 1024 + to["y"] * 256, 256), 256)], dckv4.at[y, :, pl.ds(k * 256, 256)], to)
           for to in row for k in range(2)]
    ka = [both(u, u2, False), both(dy, dy2, True)]
    kc = []
    for k, (a, b) in enumerate(((att, r1), (n2, dcq), (catt, r2))):
        kc += [both(a, a2.at[k], False), both(b, r2s.at[k], True)]

    def grad_b(z):
        lhs = n32[:, pl.ds(pl.multiple_of(z * 256, 256), 256)]
        for k in range(4):
            g = mm_rows(lhs, dh2[:, k * 512:(k + 1) * 512])
            gb[z, :, :, :, :, k * 512:(k + 1) * 512] = g.reshape(4, 2, 4, 8, 512).astype(BF)

    def grad_a(z, x):
        lhs = u2[:, pl.ds(pl.multiple_of((z * 4 + x) * 256, 256), 256)]
        ga[z, x] = mm_rows(lhs, dy2[...]).reshape(2, 4, 32, 512).astype(BF)

    def grad_c(k, z):
        g = mm_rows(a2[k, :, pl.ds(pl.multiple_of(z * 256, 256), 256)], r2s[k])
        gc[z, :, :, :, :, k * 512:(k + 1) * 512] = g.reshape(4, 2, 4, 8, 512).astype(BF)

    ready(*kb)
    far_z, far_x = moved(at, "z", 2)["z"], moved(at, "x", 2)["x"]
    loop(4, lambda i: grad_b(lax.rem(far_z + i, 4)))
    fl_b = scatter_flow(gb, (lb1, lb2, lb3), at, ("z", "y", "x"), {"z", "x", "y"}, copies)
    next(fl_b)
    ready(*ka)
    loop(16, lambda i: grad_a(lax.rem(i, 4), lax.rem(far_x + lax.div(i, 4), 4)))
    fl_a = scatter_flow(ga, (la1, la2, la3), at, ("x", "z", "y"), {"z", "x", "y"}, copies)
    next(fl_a)
    ready(*kc)
    for k in range(3):
        loop(4, functools.partial(grad_c, k))
    fl_c = scatter_flow(gc, (lc1, lc2, lc3), at, ("y", "x", "z"), {"z", "x", "y"}, copies)
    next(fl_c)

    for s in kv_own + kvs:
        s.wait()
    dckv4[0] = sum(dckv4[k].astype(F32) for k in range(4)).astype(BF)
    dcap[...] = mm_cols(dckv4[0], wq[:, 768:1280]).astype(BF)
    cap_own = pltpu.make_async_copy(dcap.at[:, quarter(at)], dcap4.at[y], local.at[27])
    cap_own.start()
    caps = [copies.start(dcap.at[:, quarter(to)], dcap4.at[y], to) for to in row]

    d_own.wait()
    for s in dd:
        s.wait()
    self_backward(qkv, lse, datt4, dqkv, dk, dv)
    v13[...] = vec_sums[...]
    gain, shift = vec[0:1, :], vec[3:4, :]

    def norm_rows(i):
        r = pl.ds(pl.multiple_of(i * 128, 128), 128)
        z, _ = normed(x_all[r, :].astype(F32))
        n1[r, :] = (z * gain + shift).astype(BF)
        d = mm_cols(dqkv[r, :], wq[:, 0:768])
        dn[r, :] = d.astype(BF)
        v13[0:1, :] += jnp.sum(d * z, axis=0, keepdims=True)
        v13[3:4, :] += jnp.sum(d, axis=0, keepdims=True)

    loop(8, norm_rows)
    dns = [copies.start(dn.at[pl.ds(pl.multiple_of(to["y"] * 256, 256), 256)], dn4.at[k], to) for k, to in enumerate(row)]

    def grad_q(z):
        cols = pl.ds(pl.multiple_of(z * 256, 256), 256)
        gq[z, :, :, :, :, 0:768] = mm_rows(n1[:, cols], dqkv[...]).reshape(4, 2, 4, 8, 768).astype(BF)
        gq[z, :, :, :, :, 768:1280] = mm_rows(e[:, cols], dckv4[0]).reshape(4, 2, 4, 8, 512).astype(BF)

    loop(4, grad_q)
    gq[:, :, :, :, :, 1280:1408] = v13[...].T.reshape(4, 4, 2, 4, 8, 128).astype(BF)
    gq[:, :, :, :, :, 1408:1536] = jnp.zeros((4, 4, 2, 4, 8, 128), BF)
    n_q = gq.shape[-1]
    pq = copies.start(gq.at[:, :, :, :, :, half(n_q, partner)], gql, partner)
    flows = [fl_b, fl_a, fl_c]
    for f in flows:
        next(f)
    pq.wait()
    mine = gq.at[:, :, :, :, :, half(n_q, at)]
    add_into(mine, gql)
    fl_q = scatter_flow(mine, (lq1, lq2), at, ("x", "z"), {"z", "x", "y"}, copies)
    next(fl_q)
    for f in flows:
        next(f)
    next(fl_q)
    for s in dns + caps + [cap_own]:
        s.wait()

    def token_rows(i):
        r = pl.ds(pl.multiple_of(i * 64, 64), 64)
        here = pl.ds(pl.multiple_of(y * 256 + i * 64, 64), 64)
        d = dn[here, :].astype(F32) + dn4[0, r, :].astype(F32) + dn4[1, r, :].astype(F32) + dn4[2, r, :].astype(F32)
        back, _, _ = norm_back(x_all[here, :].astype(F32), d, gain)
        tok[r, :] = dx1[r, :] + back

    loop(4, token_rows)
    cap[...] = sum(dcap4[k].astype(F32) for k in range(4))
    finish(flows + [fl_q])

    last = []
    for g, f in ((ga, fa), (gb, fb), (gc, fc)):
        last.append(copies.start(g.at[at["z"], at["x"], partner["c"], y], f, partner))
    for o in ring:
        last.append(copies.start(mine.at[at["z"], at["x"], o["c"], o["y"]], fq.at[c, y], o))
    own_q = pltpu.make_async_copy(mine.at[at["z"], at["x"], c, y], fq.at[c, y], local.at[26])
    own_q.start()
    for g, o in ((ga, out_a), (gb, out_b), (gc, out_c)):
        o[c] = g[at["z"], at["x"], c, y].astype(F32)
    for s in last + [own_q]:
        s.wait()
    for f, o in ((fa, out_a), (fb, out_b), (fc, out_c)):
        o[partner["c"]] = f[...].astype(F32)
    out_q[...] = fq[...].astype(F32)


def reduced(u, dy, n3, dh, att, r1, n2, dcq, catt, r2, datt, dckv, vec_sums, x_all, qkv, lse, wq, e, dx1, vec):
    n_c, n_q = 1536, 768
    lead = ("z", "x", "y")
    V = pltpu.VMEM
    scratch = [
        V((512, 4096), BF), V((512, 512), BF), V((512, 1024), BF), V((512, 2048), BF), V((3, 512, 1024), BF), V((3, 512, 512), BF),
        V((4, 4, 2, 4, 32, 512), BF), V((4, 4, 2, 4, 8, 2048), BF), V((4, 4, 2, 4, 8, n_c), BF),
        V((4, 4, 2, 4, 8, 2 * n_q), BF), V((4, 4, 2, 4, 8, n_q), BF),
        V((1024, 256), BF), V((4, 128, 512), BF), V((128, 1024), BF), V((4, 128, 256), BF), V((1024, 768), BF), V((1024, 1024), BF),
        V((1024, 128), F32), V((1024, 128), F32), V((1024, 1024), BF), V((3, 256, 1024), BF), V((128, 1024), F32),
    ]
    for r, n, axes in ((32, 512, "xzy"), (8, 2048, "zyx"), (8, n_c, "yxz"), (8, n_q, "xz")):
        scratch += [V(s, BF) for s in landing_shapes(lead, r, n, axes)]
    scratch += [V((32, 512), BF), V((8, 2048), BF), V((8, n_c), BF), V((2, 4, 8, n_q), BF)]
    n = 112
    scratch += [pltpu.SemaphoreType.DMA((n,)), pltpu.SemaphoreType.DMA((n,)), pltpu.SemaphoreType.DMA((32,))]
    s = jax.ShapeDtypeStruct
    outs = [s((2, 32, 512), F32), s((2, 8, 2048), F32), s((2, 8, n_c), F32), s((2, 4, 8, n_q), F32), s((256, 1024), F32), s((128, 256), F32)]
    anywhere, vm = pl.BlockSpec(memory_space=pl.ANY), pl.BlockSpec(memory_space=pltpu.VMEM)
    return pl.pallas_call(
        reduce_kernel, out_shape=outs, in_specs=[anywhere] * 12 + [vm] * 8, out_specs=[vm] * 6,
        scratch_shapes=scratch,
        compiler_params=pltpu.CompilerParams(collective_id=1, has_side_effects=True, vmem_limit_bytes=62 << 20),
        name="reduce_gradients",
    )(u, dy, n3, dh, att, r1, n2, dcq, catt, r2, datt, dckv, vec_sums, x_all, qkv, lse, wq, e, dx1, vec)


def local(tokens, captions, cap_lengths, w_qkv, w_self_out, w_cross_q, w_cross_kv, w_cross_out, w_in, w_out,
          norm_gains, norm_shifts, out_biases, in_bias, out_grad):
    vectors = jnp.concatenate([norm_gains.T, norm_shifts.T, out_biases.T, in_bias.reshape(4, 8).T], axis=1)
    vectors = jnp.pad(vectors, ((0, 0), (0, 256 - 13)))
    c_in = jnp.concatenate([w_self_out, w_cross_q, w_cross_out], axis=1)
    q_in = jnp.concatenate([w_qkv, w_cross_kv], axis=1).reshape(8, 5, 4, 256).transpose(2, 0, 1, 3).reshape(4, 8, 1280)
    q_in = jnp.concatenate([q_in, jnp.broadcast_to(vectors, (4, 8, 256))], axis=2)
    c_g, win_g, wout_g, x_g, wq, qkv, lse, att, ck, cv, e, vec = gathered(c_in, w_in, w_out, q_in, tokens[0], captions[0])
    wc, full_in, full_out = c_g.reshape(1024, -1), win_g.reshape(1024, -1), wout_g.reshape(4096, 1024)
    hidden_bias = vec[9:13].reshape(4, 128, 8).transpose(1, 0, 2).reshape(1, 4096)
    dy = out_grad[0]
    (layer_out, dx1, datt, dckv, n2, n3, catt, u, dh, r1, r2, dcq, sums, d_in_bias) = middle(
        cap_lengths, tokens[0], att, dy, ck, cv, vec, hidden_bias, wc, full_in, full_out)
    d_hidden = d_in_bias.reshape(128, 4, 8).transpose(1, 0, 2).reshape(4, 1024)
    vec_sums = jnp.concatenate([sums[:9], d_hidden, jnp.zeros((115, 1024), jnp.float32)], axis=0)
    out_a, out_b, out_c, out_q, tokens_grad, captions_grad = reduced(
        u, dy, n3, dh, att, r1, n2, dcq, catt, r2, datt, dckv, vec_sums, x_g.reshape(1024, 1024), qkv, lse, wq, e, dx1, vec)
    joined = lambda t: jnp.concatenate([t[0], t[1]], axis=1)
    q_out = out_q.transpose(2, 1, 0, 3).reshape(8, 4, 1536)
    vec_out = q_out[:, :, 1280:1293].sum(axis=1)
    q_out = q_out[:, :, :1280].reshape(8, 4, 5, 256).transpose(0, 2, 1, 3).reshape(8, 5120)
    return (
        layer_out[None], tokens_grad[None], captions_grad[None],
        q_out[:, :3072], joined(out_c[..., :512]), joined(out_c[..., 512:1024]), q_out[:, 3072:], joined(out_c[..., 1024:1536]),
        joined(out_b), joined(out_a), vec_out[:, :3].T, vec_out[:, 3:6].T, vec_out[:, 6:9].T, vec_out[:, 9:13].T.reshape(32),
    )


def solution(mesh):
    rows, tokens, vectors = P(("dp", "seq"), None), P("dp", "seq", None), P(None, ("dp", "seq"))
    captions = P("dp", None, "seq")
    return jax.shard_map(
        local, mesh=mesh,
        in_specs=(tokens, captions, P("dp"), *[rows] * 7, *[vectors] * 3, P(("dp", "seq")), tokens),
        out_specs=(tokens, tokens, captions, *[rows] * 7, *[vectors] * 3, P(("dp", "seq"))),
        check_vma=False,
    )
```

```python
import functools

import jax
import jax.numpy as jnp
from jax import lax
from jax.experimental import pallas as pl
from jax.experimental.pallas import tpu as pltpu
from jax.sharding import PartitionSpec as P

MESH = pl.DeviceIdType.MESH
def position():
    dp, y = lax.axis_index("dp"), lax.axis_index("seq")
    return {"z": lax.div(dp, 8), "x": lax.rem(lax.div(dp, 2), 4), "c": lax.rem(dp, 2), "y": y}


def device(at):
    return (at["z"] * 8 + at["x"] * 2 + at["c"], at["y"])


def moved(at, axis, by):
    size = 2 if axis == "c" else 4
    return {**at, axis: lax.rem(at[axis] + by + size, size)}


class Copies:
    def __init__(self, send, recv):
        self.send, self.recv, self.used = send, recv, 0

    def start(self, src, dst, at):
        k = self.used
        self.used += 1
        assert k < self.send.shape[0]
        copy = pltpu.make_async_remote_copy(src_ref=src, dst_ref=dst, send_sem=self.send.at[k], recv_sem=self.recv.at[k], device_id=device(at), device_id_type=MESH)
        copy.start()
        return copy


def block(ref, at, whole, cols):
    idx = [slice(None) if axis in whole else at[axis] for axis in ("z", "x", "c", "y")]
    return ref.at[(*idx, slice(None), cols)]


def gather_flow(ref, at, cols, axes, whole, copies, partner, done, source=None):
    start, size = cols
    low_cols, high_cols = pl.ds(start, size // 256 * 128), pl.ds(start + size // 256 * 128, size - size // 256 * 128)
    cols = pl.ds(start, size)
    whole = set(whole)
    for axis in axes:
        up, down = moved(at, axis, 1), moved(at, axis, -1)
        own = block(ref, at, whole, cols)
        src = own if source is None else source.at[:, cols]
        source = None
        a = copies.start(src, own, up)
        b = copies.start(src, own, down)
        yield
        a.wait_recv()
        b.wait_recv()
        low, high = block(ref, down, whole, low_cols), block(ref, up, whole, high_cols)
        c = copies.start(low, low, up)
        d = copies.start(high, high, down)
        for p in (down, up):
            got = block(ref, p, whole, cols)
            done.append(copies.start(got, got, partner))
        yield
        c.wait_recv()
        d.wait_recv()
        far = block(ref, moved(at, axis, 2), whole, cols)
        done.append(copies.start(far, far, partner))
        for s in (a, b, c, d):
            s.wait_send()
        whole.add(axis)


EPSILON = 1e-05
MASKED = -1e30
SCALE = 64 ** -0.5
BF, F32 = jnp.bfloat16, jnp.float32
def mm(a, b):
    return jnp.dot(a, b, preferred_element_type=F32)


def mm_rows(a, b):
    return lax.dot_general(a, b, (((0,), (0,)), ((), ())), preferred_element_type=F32)


def mm_cols(a, b):
    return lax.dot_general(a, b, (((1,), (1,)), ((), ())), preferred_element_type=F32)


def normed(v):
    centred = v - jnp.mean(v, axis=-1, keepdims=True)
    r = lax.rsqrt(jnp.mean(centred * centred, axis=-1, keepdims=True) + EPSILON)
    return centred * r, r


def norm_back(v, d, gain):
    z, r = normed(v)
    w = d * gain
    dv = r * (w - jnp.mean(w, axis=-1, keepdims=True) - z * jnp.mean(w * z, axis=-1, keepdims=True))
    return dv, jnp.sum(d * z, axis=0, keepdims=True), jnp.sum(d, axis=0, keepdims=True)


def loop(n, body):
    def step(i, _):
        body(i)
        return 0

    lax.fori_loop(0, n, step, 0)


def gelu_both(h):
    cdf = 0.5 * (1.0 + lax.erf(h * (0.5 ** 0.5)))
    return h * cdf, cdf + h * jnp.exp(-0.5 * h * h) * (1.0 / (2.0 * 3.141592653589793) ** 0.5)


def lanes_of(pair_shape, head):
    lane = lax.broadcasted_iota(jnp.int32, pair_shape, 1)
    return (lane < 64) if head == 0 else (lane >= 64)


def middle_kernel(length, x_in, att_in, dy_in, ck_in, cv_in, vec, inb, wc, win, wout,
                  out, dx1_o, datt_o, dckv_o, n2_o, n3_o, catt_o, u_o, dh_o, r1_o, r2_o, dcq_o, sums, dinb,
                  so, wcq, co, wi, wo, x1, x2, probs, cq, ya, dn, dca, sem):
    loads = []
    for k, dst in enumerate((so, wcq, co)):
        loads.append(pltpu.make_async_copy(wc.at[:, pl.ds(k * 1024, 1024)], dst, sem.at[k]))
    for l in loads:
        l.start()
    chunk = 512
    n_chunk = wi.shape[1] // chunk

    def ff_loads(i):
        cols = pl.ds(pl.multiple_of(i * chunk, chunk), chunk)
        return (pltpu.make_async_copy(win.at[:, cols], wi.at[:, cols], sem.at[3 + 2 * i]),
                pltpu.make_async_copy(wout.at[cols], wo.at[cols], sem.at[4 + 2 * i]))

    for i in range(n_chunk):
        for l in ff_loads(i):
            l.start()

    step_rows = 64
    def by_rows(body):
        loop(256 // step_rows, lambda i: body(pl.ds(pl.multiple_of(i * step_rows, step_rows), step_rows)))

    def row(k):
        return vec[k:k + 1, :]

    sums[...] = jnp.zeros_like(sums)

    loads[0].wait()
    x1[...] = mm(att_in[...], so[...])

    def after_self(r):
        v = x_in[r, :].astype(F32) + x1[r, :] + row(6)
        x1[r, :] = v
        z, _ = normed(v)
        n2_o[r, :] = (z * row(1) + row(4)).astype(BF)

    by_rows(after_self)
    loads[1].wait()
    cq[...] = mm(n2_o[...], wcq[...]).astype(BF)

    seen = lax.broadcasted_iota(jnp.int32, (128, 256), 0) < length[0]

    def cross_forward(p):
        cols = pl.ds(pl.multiple_of(p * 128, 128), 128)
        k, v, q = ck_in[:, cols], cv_in[:, cols], cq[:, cols]
        mixed = []
        for head in range(2):
            qh = jnp.where(lanes_of(q.shape, head), q, jnp.zeros_like(q))
            s = jnp.where(seen, mm_cols(k, qh) * SCALE, MASKED)
            e = jnp.exp(s - jnp.max(s, axis=0, keepdims=True))
            prob = e / jnp.sum(e, axis=0, keepdims=True)
            probs[2 * p + head] = prob
            mixed.append(mm_rows(prob.astype(BF), v))
        catt_o[:, cols] = jnp.where(lanes_of(q.shape, 0), mixed[0], mixed[1]).astype(BF)

    loop(8, cross_forward)
    loads[2].wait()
    x2[...] = mm(catt_o[...], co[...])

    def after_cross(r):
        v = x1[r, :] + x2[r, :] + row(7)
        x2[r, :] = v
        z, _ = normed(v)
        n3_o[r, :] = (z * row(2) + row(5)).astype(BF)

    by_rows(after_cross)

    ya[...] = jnp.zeros_like(ya)
    dn[...] = jnp.zeros_like(dn)

    def feed(i):
        for l in ff_loads(i):
            l.wait()
        cols = pl.ds(pl.multiple_of(i * chunk, chunk), chunk)
        h = mm(n3_o[...], wi[:, cols]) + inb[:, cols]
        u, slope = gelu_both(h)
        u = u.astype(BF)
        u_o[:, cols] = u
        ya[...] += mm(u, wo[cols, :])
        dh = (mm_cols(dy_in[...], wo[cols, :]) * slope).astype(BF)
        dh_o[:, cols] = dh
        dinb[:, cols] = jnp.sum(dh.astype(F32), axis=0, keepdims=True)
        dn[...] += mm_cols(dh, wi[:, cols])

    loop(n_chunk, feed)

    def after_feed(r):
        v = x2[r, :]
        out[r, :] = (v + ya[r, :] + row(8)).astype(BF)
        dy = dy_in[r, :].astype(F32)
        dv, dgain, dshift = norm_back(v, dn[r, :], row(2))
        d = dy + dv
        x2[r, :] = d
        r2_o[r, :] = d.astype(BF)
        sums[2:3, :] += dgain
        sums[5:6, :] += dshift
        sums[7:8, :] += jnp.sum(d, axis=0, keepdims=True)
        sums[8:9, :] += jnp.sum(dy, axis=0, keepdims=True)

    by_rows(after_feed)

    dca[...] = mm_cols(r2_o[...], co[...]).astype(BF)

    def cross_backward(p):
        cols = pl.ds(pl.multiple_of(p * 128, 128), 128)
        k, v, q, d = ck_in[:, cols], cv_in[:, cols], cq[:, cols], dca[:, cols]
        dk = dv = jnp.zeros((128, 128), F32)
        dq = []
        for head in range(2):
            lanes = lanes_of(q.shape, head)
            qh = jnp.where(lanes, q, jnp.zeros_like(q))
            dout = jnp.where(lanes, d, jnp.zeros_like(d))
            prob = probs[2 * p + head]
            dp = mm_cols(v, dout)
            ds = (prob * (dp - jnp.sum(dp * prob, axis=0, keepdims=True))).astype(BF)
            dv += mm(prob.astype(BF), dout)
            dk += mm(ds, qh)
            dq.append(mm_rows(ds, k))
        dcq_o[:, cols] = (jnp.where(lanes_of(q.shape, 0), dq[0], dq[1]) * SCALE).astype(BF)
        dckv_o[:, cols] = (dk * SCALE).astype(BF)
        dckv_o[:, pl.ds(pl.multiple_of(1024 + p * 128, 128), 128)] = dv.astype(BF)

    loop(8, cross_backward)
    dn[...] = mm_cols(dcq_o[...], wcq[...])

    def before_cross(r):
        dv, dgain, dshift = norm_back(x1[r, :], dn[r, :], row(1))
        d = x2[r, :] + dv
        dx1_o[r, :] = d
        r1_o[r, :] = d.astype(BF)
        sums[1:2, :] += dgain
        sums[4:5, :] += dshift
        sums[6:7, :] += jnp.sum(d, axis=0, keepdims=True)

    by_rows(before_cross)
    datt_o[...] = mm_cols(r1_o[...], so[...]).astype(BF)


def middle(length, x, att, dy, ck, cv, vec, inb, wc, win, wout):
    s = jax.ShapeDtypeStruct
    outs = [s((256, 1024), BF), s((256, 1024), F32), s((256, 1024), BF), s((128, 2048), BF), s((256, 1024), BF), s((256, 1024), BF),
            s((256, 1024), BF), s((256, 4096), BF), s((256, 4096), BF), s((256, 1024), BF), s((256, 1024), BF), s((256, 1024), BF),
            s((16, 1024), F32), s((1, 4096), F32)]
    vm, anywhere = pl.BlockSpec(memory_space=pltpu.VMEM), pl.BlockSpec(memory_space=pl.ANY)
    scratch = [pltpu.VMEM((1024, 1024), BF)] * 3 + [pltpu.VMEM((1024, 4096), BF), pltpu.VMEM((4096, 1024), BF)]
    scratch += [pltpu.VMEM((256, 1024), F32)] * 2 + [pltpu.VMEM((16, 128, 256), F32), pltpu.VMEM((256, 1024), BF)]
    scratch += [pltpu.VMEM((256, 1024), F32)] * 2 + [pltpu.VMEM((256, 1024), BF), pltpu.SemaphoreType.DMA((19,))]
    return pl.pallas_call(
        middle_kernel, out_shape=outs,
        in_specs=[pl.BlockSpec(memory_space=pltpu.SMEM)] + [vm] * 7 + [anywhere] * 3, out_specs=[vm] * len(outs),
        scratch_shapes=scratch, compiler_params=pltpu.CompilerParams(vmem_limit_bytes=60 << 20),
        name="middle",
    )(length, x, att, dy, ck, cv, vec, inb, wc, win, wout)


BLOCK = 256
def causal_keep(n, at):
    keys = lax.broadcasted_iota(jnp.int32, (n, BLOCK), 0)
    return keys <= lax.broadcasted_iota(jnp.int32, (n, BLOCK), 1) + at


def project(x, wq, vec, n1, qkv):
    def rows(i):
        r = pl.ds(pl.multiple_of(i * 128, 128), 128)
        z, _ = normed(x[r, :].astype(F32))
        n1[r, :] = (z * vec[0:1, :] + vec[3:4, :]).astype(BF)

    loop(8, rows)

    def cols(i):
        r = pl.ds(pl.multiple_of(i * BLOCK, BLOCK), BLOCK)
        qkv[r, :] = mm(n1[r, :], wq[:, 0:768]).astype(BF)

    loop(4, cols)


def self_forward(qkv, att, lse):
    def pair(p):
        for i in range(1024 // BLOCK):
            n, r = (i + 1) * BLOCK, slice(i * BLOCK, (i + 1) * BLOCK)
            at = lambda part: pl.ds(pl.multiple_of(part * 256 + p * 128, 128), 128)
            q, k, v = qkv[r, at(0)], qkv[0:n, at(1)], qkv[0:n, at(2)]
            keep = causal_keep(n, i * BLOCK)
            mixed = []
            for head in range(2):
                qh = jnp.where(lanes_of(q.shape, head), q, jnp.zeros_like(q))
                s = jnp.where(keep, mm_cols(k, qh) * SCALE, MASKED)
                top = jnp.max(s, axis=0, keepdims=True)
                e = jnp.exp(s - top)
                total = jnp.sum(e, axis=0, keepdims=True)
                lse[2 * p + head, :, r] = top + jnp.log(total)
                mixed.append(mm_rows((e * (1.0 / total)).astype(BF), v))
            att[r, at(0)] = jnp.where(lanes_of(q.shape, 0), mixed[0], mixed[1]).astype(BF)

    loop(2, pair)


def self_backward(p, qkv, lse, datt, dqkv, dk, dv):
    def pair(p):
        at = lambda part: pl.ds(part * 256 + p * 128, 128)
        dk[...] = jnp.zeros_like(dk)
        dv[...] = jnp.zeros_like(dv)
        for i in range(1024 // BLOCK):
            n, r = (i + 1) * BLOCK, slice(i * BLOCK, (i + 1) * BLOCK)
            q, k, v, d = qkv[r, at(0)], qkv[0:n, at(1)], qkv[0:n, at(2)], datt[r, at(0)]
            keep = causal_keep(n, i * BLOCK)
            dq = []
            for head in range(2):
                lanes = lanes_of(q.shape, head)
                qh = jnp.where(lanes, q, jnp.zeros_like(q))
                dout = jnp.where(lanes, d, jnp.zeros_like(d))
                prob = jnp.where(keep, jnp.exp(mm_cols(k, qh) * SCALE - lse[2 * p + head, :, r]), 0.0)
                dp = mm_cols(v, dout)
                ds = (prob * (dp - jnp.sum(dp * prob, axis=0, keepdims=True))).astype(BF)
                dv[0:n, :] += mm(prob.astype(BF), dout)
                dk[0:n, :] += mm(ds, qh)
                dq.append(mm_rows(ds, k))
            dqkv[r, at(0)] = (jnp.where(lanes_of(q.shape, 0), dq[0], dq[1]) * SCALE).astype(BF)
        dqkv[:, at(1)] = (dk[...] * SCALE).astype(BF)
        dqkv[:, at(2)] = dv[...].astype(BF)

    pair(p)


def greet(others):
    barrier = pltpu.get_barrier_semaphore()
    for o in others:
        pl.semaphore_signal(barrier, inc=1, device_id=device(o), device_id_type=MESH)
    pl.semaphore_wait(barrier, len(others))


def half(n, of):
    return pl.ds(pl.multiple_of(of["c"] * (n // 2), 128), n // 2)


def finish(flows):
    live = list(flows)
    while live:
        for f in list(live):
            if next(f, "end") == "end":
                live.remove(f)


def quarter(of):
    return pl.ds(pl.multiple_of(of["y"] * 256, 256), 256)


def gather_kernel(c_in, win_in, wout_in, q_in, x_in, cap_in, c_g, win_g, wout_g, x_g, wq_o, qkv, lse, att_o, ck_o, cv_o, e_o, vec,
                  q_g, n1, att, ckv, send, recv, local):
    at = position()
    partner = moved(at, "c", 1)
    row = [moved(at, "y", b) for b in (1, 3, 2)]
    greet([moved(at, a, b) for a in "zx" for b in (1, -1)] + row + [partner])
    copies = Copies(send, recv)
    me = (at["z"], at["x"], at["c"], at["y"])
    kept, sent = [], []

    def keep(src, dst):
        cp = pltpu.make_async_copy(src, dst, local.at[len(kept)])
        cp.start()
        kept.append(cp)

    keep(q_in.at[at["y"]], q_g.at[me])
    qx = [copies.start(q_in.at[to["y"]], q_g.at[me], to) for to in row]
    q_done, done = [], []
    flows = []
    for src, dst, axes, st, n in ((wout_in, wout_g, "yzx", 0, 512), (win_in, win_g, "yxz", 0, 2048), (c_in, c_g, "xzy", 0, 1536),
                                  (wout_in, wout_g, "yzx", 512, 512), (win_in, win_g, "yxz", 2048, 2048), (c_in, c_g, "zxy", 1536, 1536)):
        flows.append(gather_flow(dst, at, (st, n), axes, (), copies, partner, done, src))
    for f in flows:
        next(f)
    keep(x_in, x_g.at[at["y"]])
    up, down = row[0], row[1]
    keep(cap_in, e_o.at[:, quarter(at)])
    ee = [copies.start(cap_in, e_o.at[:, quarter(at)], to) for to in row]
    for src, dst in ((wout_in, wout_g), (win_in, win_g), (c_in, c_g)):
        keep(src, dst.at[me])
        done.append(copies.start(src, dst.at[me], partner))
    for s in [kept[0]] + qx:
        s.wait()
    q_own = block(q_g, at, {"y"}, slice(None))
    q_done.append(copies.start(q_own, q_own, partner))
    fq = [gather_flow(q_g, at, (0, 640), "zx", {"y"}, copies, partner, q_done),
          gather_flow(q_g, at, (640, 768), "xz", {"y"}, copies, partner, q_done)]
    for f in fq:
        next(f)
    for s in kept[1:]:
        s.wait()
    for k in range(4):
        for f in fq:
            next(f, None)
        for f in flows:
            next(f)
        if k == 0:
            xx = [copies.start(x_in, x_g.at[at["y"]], to) for to in (up, down)]
        if k == 1:
            for s in xx:
                s.wait()
            low, high = slice(0, 128), slice(128, 256)
            x2 = [copies.start(x_g.at[down["y"], low], x_g.at[down["y"], low], up),
                  copies.start(x_g.at[up["y"], high], x_g.at[up["y"], high], down)]
    for s in x2 + ee + q_done:
        s.wait()

    wide = q_g[:, :, :, :, :, 1280:1408].astype(F32).reshape(1024, 128)
    vec[...] = wide.T[0:16, :]
    wq_o[...] = q_g[:, :, :, :, :, 0:1280].reshape(1024, 1280)
    x_rows = x_g.reshape(1024, 1024)
    project(x_rows, wq_o, vec, n1, qkv)
    ckv[...] = mm(e_o[...], wq_o[:, 768:1280]).astype(BF)
    self_forward(qkv, att, lse)
    for to in row:
        sent.append(copies.start(att.at[quarter(to)], att_o.at[:, quarter(at)], to))
        sent.append(copies.start(ckv.at[:, 0:256], ck_o.at[:, quarter(at)], to))
        sent.append(copies.start(ckv.at[:, 256:512], cv_o.at[:, quarter(at)], to))
    late = len(kept)
    keep(att.at[quarter(at)], att_o.at[:, quarter(at)])
    keep(ckv.at[:, 0:256], ck_o.at[:, quarter(at)])
    keep(ckv.at[:, 256:512], cv_o.at[:, quarter(at)])
    finish(flows)
    for s in sent + done + kept[late:]:
        s.wait()


def gathered(c_in, win_in, wout_in, q_in, x_in, cap_in):
    s = jax.ShapeDtypeStruct
    anywhere, vm = pl.BlockSpec(memory_space=pl.ANY), pl.BlockSpec(memory_space=pltpu.VMEM)
    outs = [s((4, 4, 2, 4, *a.shape), BF) for a in (c_in, win_in, wout_in)]
    outs += [s((4, 256, 1024), BF), s((1024, 1280), BF), s((1024, 768), BF), s((4, 1, 1024), F32), s((256, 1024), BF),
             s((128, 1024), BF), s((128, 1024), BF), s((128, 1024), BF), s((16, 1024), F32)]
    n = 196
    return pl.pallas_call(
        gather_kernel, out_shape=outs, in_specs=[anywhere] * 6, out_specs=[anywhere] * 3 + [vm] * 9,
        scratch_shapes=[pltpu.VMEM((4, 4, 2, 4, *q_in.shape[1:]), BF), pltpu.VMEM((1024, 1024), BF), pltpu.VMEM((1024, 256), BF),
                        pltpu.VMEM((128, 512), BF), pltpu.SemaphoreType.DMA((n,)), pltpu.SemaphoreType.DMA((n,)), pltpu.SemaphoreType.DMA((10,))],
        compiler_params=pltpu.CompilerParams(collective_id=0, has_side_effects=True, vmem_limit_bytes=60 << 20),
        name="gather_and_attend",
    )(c_in, win_in, wout_in, q_in, x_in, cap_in)


ORDER = ("z", "x", "c", "y")
def part(ref, at, whole, **fixed):
    return ref.at[tuple(fixed[a] if a in fixed else slice(None) if a in whole else at[a] for a in ORDER)]


def each(shape, body):
    total = 1
    for s in shape:
        total *= s

    def step(i, _):
        index, rest = [], i
        for s in reversed(shape):
            index.insert(0, lax.rem(rest, s))
            rest = lax.div(rest, s)
        body(tuple(index))
        return 0

    if total == 1:
        body((0,) * len(shape))
    else:
        lax.fori_loop(0, total, step, 0)


def add_into(dst, *srcs):
    def one(index):
        total = dst[index].astype(jnp.float32)
        for s in srcs:
            total += s[index].astype(jnp.float32)
        dst[index] = total.astype(dst.dtype)

    each(dst.shape[:-2], one)


def landing_shapes(rows, cols, axes):
    whole, shapes = {"z", "x", "y"}, []
    for axis in axes:
        whole = whole - {axis}
        shapes.append(pltpu.VMEM((6, *[4 for a in ("z", "x", "y") if a in whole], rows, cols), jnp.bfloat16))
    return tuple(shapes)


def scatter_flow(g, landing, at, axes, whole, copies):
    whole = set(whole)
    for axis, land in zip(axes, landing):
        up, down, far = moved(at, axis, 1), moved(at, axis, -1), moved(at, axis, 2)
        rest = whole - {axis}
        def blk(place, core):
            return part(g, at, rest, **{axis: place[axis], "c": core})
        s = [
            copies.start(blk(far, 0), land.at[0], up),
            copies.start(blk(far, 1), land.at[1], down),
            copies.start(blk(up, 1), land.at[2], up),
            copies.start(blk(down, 0), land.at[3], down),
        ]
        yield
        s[0].wait_recv()
        add_into(blk(up, 0), land.at[0])
        s.append(copies.start(blk(up, 0), land.at[4], up))
        s[1].wait_recv()
        add_into(blk(down, 1), land.at[1])
        s.append(copies.start(blk(down, 1), land.at[5], down))
        yield
        s[2].wait_recv()
        s[5].wait_recv()
        add_into(blk(at, 1), land.at[2], land.at[5])
        s[3].wait_recv()
        s[4].wait_recv()
        add_into(blk(at, 0), land.at[3], land.at[4])
        for q in s:
            q.wait_send()
        whole = rest


def reduce_kernel(u, dy, n3, dh, att, r1, n2, dcq, catt, r2, datt, dckv, vec_sums, x_all, qkv, lse, wq, e, dx1, vec,
                  out_a, out_b, out_c, out_q, tok, cap,
                  u2, dy2, n32, dh2, a2, r2s, ga, gb, gc, gq, gql, datt4, dckv4, dcap, dcap4, dqkv, n1, dk, dv, dn, dn4, v13,
                  la, lb, lc0, lc1, lc2, lq0, lq1, fa, fb, fc, fq, send, recv, local):
    at = position()
    partner = moved(at, "c", 1)
    row = [moved(at, "y", b) for b in (1, 3, 2)]
    ring = row + [moved(o, "c", 1) for o in row] + [partner]
    greet([moved(at, a, b) for a in "zx" for b in (1, -1)] + ring)
    copies = Copies(send, recv)
    c, y = at["c"], at["y"]
    loads, pairs = [], []

    def both(src, dst, split):
        n = src.shape[-1]
        rows = src.shape[0]
        mine = src.at[:, half(n, at)] if split else src
        theirs = src.at[:, half(n, partner)] if split else src
        cp = pltpu.make_async_copy(mine, dst.at[pl.ds(0, rows)], local.at[len(loads)])
        cp.start()
        loads.append(cp)
        pairs.append(copies.start(theirs, dst.at[pl.ds(rows, rows)], partner))
        return len(loads) - 1

    def ready(*ks):
        for k in ks:
            loads[k].wait()
            pairs[k].wait()

    kb = [both(n3, n32, False), both(dh, dh2, True)]
    own_rows = pl.ds(pl.multiple_of(y * 256, 256), 256)
    d_own = pltpu.make_async_copy(datt.at[:, quarter(at)], datt4.at[own_rows], local.at[30])
    d_own.start()
    dd = [copies.start(datt.at[:, quarter(to)], datt4.at[own_rows], to) for to in row]
    kv_own = [pltpu.make_async_copy(dckv.at[:, pl.ds(pl.multiple_of(k * 1024 + y * 256, 256), 256)], dckv4.at[y, :, pl.ds(k * 256, 256)], local.at[28 + k]) for k in range(2)]
    for s in kv_own:
        s.start()
    kvs = [copies.start(dckv.at[:, pl.ds(pl.multiple_of(k * 1024 + to["y"] * 256, 256), 256)], dckv4.at[y, :, pl.ds(k * 256, 256)], to)
           for to in row for k in range(2)]
    ka = [both(u, u2, False), both(dy, dy2, True)]
    kc = []
    for k, (a, b) in enumerate(((att, r1), (n2, dcq), (catt, r2))):
        kc += [both(a, a2.at[k], False), both(b, r2s.at[k], True)]

    def grad_b(z):
        lhs = n32[:, pl.ds(pl.multiple_of(z * 256, 256), 256)]
        for k in range(4):
            g = mm_rows(lhs, dh2[:, k * 512:(k + 1) * 512])
            gb[z, :, :, :, :, k * 512:(k + 1) * 512] = g.reshape(4, 2, 4, 8, 512).astype(BF)

    def grad_a(z, x):
        lhs = u2[:, pl.ds(pl.multiple_of((z * 4 + x) * 256, 256), 256)]
        ga[z, x] = mm_rows(lhs, dy2[...]).reshape(2, 4, 32, 512).astype(BF)

    def grad_c(k, z):
        g = mm_rows(a2[k, :, pl.ds(pl.multiple_of(z * 256, 256), 256)], r2s[k])
        gc[z, :, :, :, :, k * 512:(k + 1) * 512] = g.reshape(4, 2, 4, 8, 512).astype(BF)

    every = {"z", "x", "y"}
    ready(*kb)
    loop(4, grad_b)
    fl_b = scatter_flow(gb, lb, at, ("z", "x", "y"), every, copies)
    next(fl_b)
    ready(*ka)
    loop(16, lambda i: grad_a(lax.rem(i, 4), lax.div(i, 4)))
    fl_a = scatter_flow(ga, la, at, ("x", "z", "y"), every, copies)
    next(fl_a)
    ready(*kc)
    fl_c = []
    for k, (land, axes) in enumerate(((lc0, "yzx"), (lc1, "zyx"), (lc2, "yzx"))):
        loop(4, functools.partial(grad_c, k))
        fl_c.append(scatter_flow(gc.at[:, :, :, :, :, pl.ds(k * 512, 512)], land, at, tuple(axes), every, copies))
        next(fl_c[k])

    for s in kv_own + kvs:
        s.wait()
    dckv4[0] = sum(dckv4[k].astype(F32) for k in range(4)).astype(BF)
    dcap[...] = mm_cols(dckv4[0], wq[:, 768:1280]).astype(BF)
    cap_own = pltpu.make_async_copy(dcap.at[:, quarter(at)], dcap4.at[y], local.at[27])
    cap_own.start()
    caps = [copies.start(dcap.at[:, quarter(to)], dcap4.at[y], to) for to in row]

    d_own.wait()
    for s in dd:
        s.wait()
    self_backward(0, qkv, lse, datt4, dqkv, dk, dv)
    self_backward(1, qkv, lse, datt4, dqkv, dk, dv)
    next(fl_b)
    next(fl_a)
    v13[...] = vec_sums[...]
    gain, shift = vec[0:1, :], vec[3:4, :]

    def norm_rows(i):
        r = pl.ds(pl.multiple_of(i * 128, 128), 128)
        z, _ = normed(x_all[r, :].astype(F32))
        n1[r, :] = (z * gain + shift).astype(BF)
        d = mm_cols(dqkv[r, :], wq[:, 0:768])
        dn[r, :] = d.astype(BF)
        v13[0:1, :] += jnp.sum(d * z, axis=0, keepdims=True)
        v13[3:4, :] += jnp.sum(d, axis=0, keepdims=True)

    loop(8, norm_rows)
    dns = [copies.start(dn.at[pl.ds(pl.multiple_of(to["y"] * 256, 256), 256)], dn4.at[k], to) for k, to in enumerate(row)]
    for f in fl_c:
        next(f)

    def grad_q(z):
        cols = pl.ds(pl.multiple_of(z * 256, 256), 256)
        gq[z, :, :, :, :, 0:768] = mm_rows(n1[:, cols], dqkv[...]).reshape(4, 2, 4, 8, 768).astype(BF)
        gq[z, :, :, :, :, 768:1280] = mm_rows(e[:, cols], dckv4[0]).reshape(4, 2, 4, 8, 512).astype(BF)

    loop(4, grad_q)
    gq[:, :, :, :, :, 1280:1408] = v13[...].T.reshape(4, 4, 2, 4, 8, 128).astype(BF)
    gq[:, :, :, :, :, 1408:1536] = jnp.zeros((4, 4, 2, 4, 8, 128), BF)
    n_q = gq.shape[-1]
    pq = copies.start(gq.at[:, :, :, :, :, half(n_q, partner)], gql, partner)
    next(fl_b)
    next(fl_a)
    pq.wait()
    mine = gq.at[:, :, :, :, :, half(n_q, at)]
    add_into(mine, gql)
    q_cols = lambda k: gq.at[:, :, :, :, :, pl.ds(pl.multiple_of(c * 768 + k * 384, 128), 384)]
    fl_q = [scatter_flow(q_cols(0), lq0, at, ("x", "z"), every, copies), scatter_flow(q_cols(1), lq1, at, ("z", "x"), every, copies)]
    for f in fl_q + fl_c + [fl_b, fl_a] + fl_q:
        next(f)
    for s in dns + caps + [cap_own]:
        s.wait()

    def token_rows(i):
        r = pl.ds(pl.multiple_of(i * 64, 64), 64)
        here = pl.ds(pl.multiple_of(y * 256 + i * 64, 64), 64)
        d = dn[here, :].astype(F32) + dn4[0, r, :].astype(F32) + dn4[1, r, :].astype(F32) + dn4[2, r, :].astype(F32)
        back, _, _ = norm_back(x_all[here, :].astype(F32), d, gain)
        tok[r, :] = dx1[r, :] + back

    loop(4, token_rows)
    cap[...] = sum(dcap4[k].astype(F32) for k in range(4))
    finish(fl_c + [fl_b, fl_a] + fl_q)

    last = []
    for g, f in ((ga, fa), (gb, fb), (gc, fc)):
        last.append(copies.start(g.at[at["z"], at["x"], partner["c"], y], f, partner))
    for o in ring:
        last.append(copies.start(mine.at[at["z"], at["x"], o["c"], o["y"]], fq.at[c, y], o))
    own_q = pltpu.make_async_copy(mine.at[at["z"], at["x"], c, y], fq.at[c, y], local.at[26])
    own_q.start()
    for g, o in ((ga, out_a), (gb, out_b), (gc, out_c)):
        o[c] = g[at["z"], at["x"], c, y]
    for s in last + [own_q]:
        s.wait()
    for f, o in ((fa, out_a), (fb, out_b), (fc, out_c)):
        o[partner["c"]] = f[...]
    out_q[...] = fq[...]


def reduced(u, dy, n3, dh, att, r1, n2, dcq, catt, r2, datt, dckv, vec_sums, x_all, qkv, lse, wq, e, dx1, vec):
    n_c, n_q = 1536, 768
    V = pltpu.VMEM
    scratch = [
        V((512, 4096), BF), V((512, 512), BF), V((512, 1024), BF), V((512, 2048), BF), V((3, 512, 1024), BF), V((3, 512, 512), BF),
        V((4, 4, 2, 4, 32, 512), BF), V((4, 4, 2, 4, 8, 2048), BF), V((4, 4, 2, 4, 8, n_c), BF),
        V((4, 4, 2, 4, 8, 2 * n_q), BF), V((4, 4, 2, 4, 8, n_q), BF),
        V((1024, 256), BF), V((4, 128, 512), BF), V((128, 1024), BF), V((4, 128, 256), BF), V((1024, 768), BF), V((1024, 1024), BF),
        V((1024, 128), F32), V((1024, 128), F32), V((1024, 1024), BF), V((3, 256, 1024), BF), V((128, 1024), F32),
    ]
    scratch += [landing_shapes(32, 512, "xzy"), landing_shapes(8, 2048, "zxy")]
    scratch += [landing_shapes(8, 512, axes) for axes in ("yzx", "zyx", "yzx")] + [landing_shapes(8, 384, axes) for axes in ("xz", "zx")]
    scratch += [V((32, 512), BF), V((8, 2048), BF), V((8, n_c), BF), V((2, 4, 8, n_q), BF)]
    n = 160
    scratch += [pltpu.SemaphoreType.DMA((n,)), pltpu.SemaphoreType.DMA((n,)), pltpu.SemaphoreType.DMA((32,))]
    s = jax.ShapeDtypeStruct
    outs = [s((2, 32, 512), BF), s((2, 8, 2048), BF), s((2, 8, n_c), BF), s((2, 4, 8, n_q), BF), s((256, 1024), F32), s((128, 256), F32)]
    anywhere, vm = pl.BlockSpec(memory_space=pl.ANY), pl.BlockSpec(memory_space=pltpu.VMEM)
    return pl.pallas_call(
        reduce_kernel, out_shape=outs, in_specs=[anywhere] * 12 + [vm] * 8, out_specs=[vm] * 6,
        scratch_shapes=scratch,
        compiler_params=pltpu.CompilerParams(collective_id=1, has_side_effects=True, vmem_limit_bytes=62 << 20),
        name="reduce_gradients",
    )(u, dy, n3, dh, att, r1, n2, dcq, catt, r2, datt, dckv, vec_sums, x_all, qkv, lse, wq, e, dx1, vec)


def finish_kernel(a, b, c, q, d_qkv, d_self_out, d_cross_q, d_cross_kv, d_cross_out, d_in, d_out, d_gains, d_shifts, d_biases, d_in_bias):
    for k in range(2):
        d_out[:, k * 512:(k + 1) * 512] = a[k].astype(F32)
        d_in[:, k * 2048:(k + 1) * 2048] = b[k].astype(F32)
        for m, ref in enumerate((d_self_out, d_cross_q, d_cross_out)):
            ref[:, k * 512:(k + 1) * 512] = c[k, :, m * 512:(m + 1) * 512].astype(F32)
    for y in range(4):
        for m in range(3):
            d_qkv[:, m * 1024 + y * 256:m * 1024 + (y + 1) * 256] = q[0, y, :, m * 256:(m + 1) * 256].astype(F32)
        for m in range(2):
            d_cross_kv[:, m * 1024 + y * 256:m * 1024 + (y + 1) * 256] = q[1, y, :, m * 256:(m + 1) * 256].astype(F32)
    vectors = sum(q[1, y, :, 512:640].astype(F32) for y in range(4)).T
    for m, ref in enumerate((d_gains, d_shifts, d_biases)):
        ref[...] = vectors[3 * m:3 * m + 3, :]
    d_in_bias[...] = vectors[9:13, :]


def assembled(a, b, c, q):
    shapes = [(8, 3072), (8, 1024), (8, 1024), (8, 2048), (8, 1024), (8, 4096), (32, 1024), (3, 8), (3, 8), (3, 8), (4, 8)]
    vm = pl.BlockSpec(memory_space=pltpu.VMEM)
    return pl.pallas_call(
        finish_kernel, out_shape=[jax.ShapeDtypeStruct(s, F32) for s in shapes], in_specs=[vm] * 4, out_specs=[vm] * 11, name="assemble",
    )(a, b, c, q)


def local(tokens, captions, cap_lengths, w_qkv, w_self_out, w_cross_q, w_cross_kv, w_cross_out, w_in, w_out,
          norm_gains, norm_shifts, out_biases, in_bias, out_grad):
    vectors = jnp.concatenate([norm_gains.T, norm_shifts.T, out_biases.T, in_bias.reshape(4, 8).T], axis=1)
    vectors = jnp.pad(vectors, ((0, 0), (0, 128 - 13)))
    c_in = jnp.concatenate([w_self_out, w_cross_q, w_cross_out], axis=1)
    q_in = jnp.concatenate([w_qkv, w_cross_kv], axis=1).reshape(8, 5, 4, 256).transpose(2, 0, 1, 3).reshape(4, 8, 1280)
    q_in = jnp.concatenate([q_in, jnp.broadcast_to(vectors, (4, 8, 128))], axis=2)
    c_g, win_g, wout_g, x_g, wq, qkv, lse, att, ck, cv, e, vec = gathered(c_in, w_in, w_out, q_in, tokens[0], captions[0])
    wc, full_in, full_out = c_g.reshape(1024, -1), win_g.reshape(1024, -1), wout_g.reshape(4096, 1024)
    hidden_bias = vec[9:13].reshape(4, 128, 8).transpose(1, 0, 2).reshape(1, 4096)
    dy = out_grad[0]
    (layer_out, dx1, datt, dckv, n2, n3, catt, u, dh, r1, r2, dcq, sums, d_in_bias) = middle(
        cap_lengths, tokens[0], att, dy, ck, cv, vec, hidden_bias, wc, full_in, full_out)
    d_hidden = d_in_bias.reshape(128, 4, 8).transpose(1, 0, 2).reshape(4, 1024)
    vec_sums = jnp.concatenate([sums[:9], d_hidden, jnp.zeros((115, 1024), jnp.float32)], axis=0)
    out_a, out_b, out_c, out_q, tokens_grad, captions_grad = reduced(
        u, dy, n3, dh, att, r1, n2, dcq, catt, r2, datt, dckv, vec_sums, x_g.reshape(1024, 1024), qkv, lse, wq, e, dx1, vec)
    *grads, d_in_bias = assembled(out_a, out_b, out_c, out_q)
    return (layer_out[None], tokens_grad[None], captions_grad[None], *grads, d_in_bias.reshape(32))


def solution(mesh):
    rows, tokens, vectors = P(("dp", "seq"), None), P("dp", "seq", None), P(None, ("dp", "seq"))
    captions = P("dp", None, "seq")
    return jax.shard_map(
        local, mesh=mesh,
        in_specs=(tokens, captions, P("dp"), *[rows] * 7, *[vectors] * 3, P(("dp", "seq")), tokens),
        out_specs=(tokens, tokens, captions, *[rows] * 7, *[vectors] * 3, P(("dp", "seq"))),
        check_vma=False,
    )
```

```python
import functools

import jax
import jax.numpy as jnp
from jax import lax
from jax.experimental import pallas as pl
from jax.experimental.pallas import tpu as pltpu
from jax.sharding import PartitionSpec as P

MESH = pl.DeviceIdType.MESH
def position():
    dp, y = lax.axis_index("dp"), lax.axis_index("seq")
    return {"z": lax.div(dp, 8), "x": lax.rem(lax.div(dp, 2), 4), "c": lax.rem(dp, 2), "y": y}


def device(at):
    return (at["z"] * 8 + at["x"] * 2 + at["c"], at["y"])


def moved(at, axis, by):
    size = 2 if axis == "c" else 4
    return {**at, axis: lax.rem(at[axis] + by + size, size)}


class Copies:
    def __init__(self, send, recv):
        self.send, self.recv, self.used = send, recv, 0

    def start(self, src, dst, at):
        k = self.used
        self.used += 1
        assert k < self.send.shape[0]
        copy = pltpu.make_async_remote_copy(src_ref=src, dst_ref=dst, send_sem=self.send.at[k], recv_sem=self.recv.at[k], device_id=device(at), device_id_type=MESH)
        copy.start()
        return copy


def block(ref, at, whole, cols):
    idx = [slice(None) if axis in whole else at[axis] for axis in ("z", "x", "c", "y")]
    return ref.at[(*idx, slice(None), cols)]


def gather_flow(ref, at, cols, axes, whole, copies, partner, done, source=None):
    start, size = cols
    low_cols, high_cols = pl.ds(start, size // 256 * 128), pl.ds(start + size // 256 * 128, size - size // 256 * 128)
    cols = pl.ds(start, size)
    whole = set(whole)
    for axis in axes:
        up, down = moved(at, axis, 1), moved(at, axis, -1)
        own = block(ref, at, whole, cols)
        src = own if source is None else source.at[:, cols]
        source = None
        a = copies.start(src, own, up)
        b = copies.start(src, own, down)
        yield
        a.wait_recv()
        b.wait_recv()
        low, high = block(ref, down, whole, low_cols), block(ref, up, whole, high_cols)
        c = copies.start(low, low, up)
        d = copies.start(high, high, down)
        for p in (down, up):
            got = block(ref, p, whole, cols)
            done.append(copies.start(got, got, partner))
        yield
        c.wait_recv()
        d.wait_recv()
        far = block(ref, moved(at, axis, 2), whole, cols)
        done.append(copies.start(far, far, partner))
        for s in (a, b, c, d):
            s.wait_send()
        whole.add(axis)


EPSILON = 1e-05
MASKED = -1e30
SCALE = 64 ** -0.5
BF, F32 = jnp.bfloat16, jnp.float32
def mm(a, b):
    return jnp.dot(a, b, preferred_element_type=F32)


def mm_rows(a, b):
    return lax.dot_general(a, b, (((0,), (0,)), ((), ())), preferred_element_type=F32)


def mm_cols(a, b):
    return lax.dot_general(a, b, (((1,), (1,)), ((), ())), preferred_element_type=F32)


def normed(v):
    centred = v - jnp.mean(v, axis=-1, keepdims=True)
    r = lax.rsqrt(jnp.mean(centred * centred, axis=-1, keepdims=True) + EPSILON)
    return centred * r, r


def norm_back(v, d, gain):
    z, r = normed(v)
    w = d * gain
    dv = r * (w - jnp.mean(w, axis=-1, keepdims=True) - z * jnp.mean(w * z, axis=-1, keepdims=True))
    return dv, jnp.sum(d * z, axis=0, keepdims=True), jnp.sum(d, axis=0, keepdims=True)


def loop(n, body):
    def step(i, _):
        body(i)
        return 0

    lax.fori_loop(0, n, step, 0)


def gelu_both(h):
    cdf = 0.5 * (1.0 + lax.erf(h * (0.5 ** 0.5)))
    return h * cdf, cdf + h * jnp.exp(-0.5 * h * h) * (1.0 / (2.0 * 3.141592653589793) ** 0.5)


def lanes_of(pair_shape, head):
    lane = lax.broadcasted_iota(jnp.int32, pair_shape, 1)
    return (lane < 64) if head == 0 else (lane >= 64)


BLOCK = 256
def causal_keep(n, at):
    keys = lax.broadcasted_iota(jnp.int32, (n, BLOCK), 0)
    return keys <= lax.broadcasted_iota(jnp.int32, (n, BLOCK), 1) + at


def project(x, wq, vec, n1, qkv):
    def rows(i):
        r = pl.ds(pl.multiple_of(i * 128, 128), 128)
        z, _ = normed(x[r, :].astype(F32))
        n1[r, :] = (z * vec[0:1, :] + vec[3:4, :]).astype(BF)

    loop(8, rows)

    def cols(i):
        r = pl.ds(pl.multiple_of(i * BLOCK, BLOCK), BLOCK)
        qkv[r, :] = mm(n1[r, :], wq[:, 0:768]).astype(BF)

    loop(4, cols)


def self_forward(qkv, att, lse):
    def pair(p):
        for i in range(1024 // BLOCK):
            n, r = (i + 1) * BLOCK, slice(i * BLOCK, (i + 1) * BLOCK)
            at = lambda part: pl.ds(pl.multiple_of(part * 256 + p * 128, 128), 128)
            q, k, v = qkv[r, at(0)], qkv[0:n, at(1)], qkv[0:n, at(2)]
            keep = causal_keep(n, i * BLOCK)
            mixed = []
            for head in range(2):
                qh = jnp.where(lanes_of(q.shape, head), q, jnp.zeros_like(q))
                s = jnp.where(keep, mm_cols(k, qh) * SCALE, MASKED)
                top = jnp.max(s, axis=0, keepdims=True)
                e = jnp.exp(s - top)
                total = jnp.sum(e, axis=0, keepdims=True)
                lse[2 * p + head, :, r] = top + jnp.log(total)
                mixed.append(mm_rows((e * (1.0 / total)).astype(BF), v))
            att[r, at(0)] = jnp.where(lanes_of(q.shape, 0), mixed[0], mixed[1]).astype(BF)

    loop(2, pair)


def self_backward(p, qkv, lse, datt, dqkv, dk, dv):
    def pair(p):
        at = lambda part: pl.ds(part * 256 + p * 128, 128)
        dk[...] = jnp.zeros_like(dk)
        dv[...] = jnp.zeros_like(dv)
        for i in range(1024 // BLOCK):
            n, r = (i + 1) * BLOCK, slice(i * BLOCK, (i + 1) * BLOCK)
            q, k, v, d = qkv[r, at(0)], qkv[0:n, at(1)], qkv[0:n, at(2)], datt[r, at(0)]
            keep = causal_keep(n, i * BLOCK)
            dq = []
            for head in range(2):
                lanes = lanes_of(q.shape, head)
                qh = jnp.where(lanes, q, jnp.zeros_like(q))
                dout = jnp.where(lanes, d, jnp.zeros_like(d))
                prob = jnp.where(keep, jnp.exp(mm_cols(k, qh) * SCALE - lse[2 * p + head, :, r]), 0.0)
                dp = mm_cols(v, dout)
                ds = (prob * (dp - jnp.sum(dp * prob, axis=0, keepdims=True))).astype(BF)
                dv[0:n, :] += mm(prob.astype(BF), dout)
                dk[0:n, :] += mm(ds, qh)
                dq.append(mm_rows(ds, k))
            dqkv[r, at(0)] = (jnp.where(lanes_of(q.shape, 0), dq[0], dq[1]) * SCALE).astype(BF)
        dqkv[:, at(1)] = (dk[...] * SCALE).astype(BF)
        dqkv[:, at(2)] = dv[...].astype(BF)

    pair(p)


def greet(others):
    barrier = pltpu.get_barrier_semaphore()
    for o in others:
        pl.semaphore_signal(barrier, inc=1, device_id=device(o), device_id_type=MESH)
    pl.semaphore_wait(barrier, len(others))


def half(n, of):
    return pl.ds(pl.multiple_of(of["c"] * (n // 2), 128), n // 2)


def finish(flows):
    live = list(flows)
    while live:
        for f in list(live):
            if next(f, "end") == "end":
                live.remove(f)


def quarter(of):
    return pl.ds(pl.multiple_of(of["y"] * 256, 256), 256)


def cross_forward(p, length, ck, cv, cq, probs, catt):
    cols = pl.ds(pl.multiple_of(p * 128, 128), 128)
    k, v, q = ck[:, cols], cv[:, cols], cq[:, cols]
    seen = lax.broadcasted_iota(jnp.int32, (128, 256), 0) < length
    mixed = []
    for head in range(2):
        qh = jnp.where(lanes_of(q.shape, head), q, jnp.zeros_like(q))
        s = jnp.where(seen, mm_cols(k, qh) * SCALE, MASKED)
        e = jnp.exp(s - jnp.max(s, axis=0, keepdims=True))
        prob = e / jnp.sum(e, axis=0, keepdims=True)
        probs[2 * p + head] = prob
        mixed.append(mm_rows(prob.astype(BF), v))
    catt[:, cols] = jnp.where(lanes_of(q.shape, 0), mixed[0], mixed[1]).astype(BF)


def gather_kernel(length, w_qkv, w_ckv, w_so, w_cq, w_co, vectors, win_in, wout_in, x_in, cap_in, dy_in,
                  c_out, win_g, wout_g, dy_o, x_out, wq_out, qkv_out, lse_out, att_out, ck_out, cv_out, e_out, x1_out, x2_out, n2_out, n3_out,
                  catt_out, probs_out, cq_out, vec, wide_o,
                  x_g, wq_o, qkv, lse, att_o, ck_o, cv_o, e_o, x1, x2, n2_o, n3_o, catt_o, probs, cq,
                  q_in, c_in, c_g, q_g, n1, att, ckv, send, recv, local):
    at = position()
    partner = moved(at, "c", 1)
    row = [moved(at, "y", b) for b in (1, 3, 2)]
    q_in[:, :, 1280:1408] = jnp.broadcast_to(vectors[...], (4, 8, 128))
    for q in range(4):
        for m in range(3):
            q_in[q, :, m * 256:(m + 1) * 256] = w_qkv[:, m * 1024 + q * 256:m * 1024 + (q + 1) * 256]
        for m in range(2):
            q_in[q, :, 768 + m * 256:1024 + m * 256] = w_ckv[:, m * 1024 + q * 256:m * 1024 + (q + 1) * 256]
    for m, ref in enumerate((w_so, w_cq, w_co)):
        c_in[:, m * 1024:(m + 1) * 1024] = ref[...]
    greet([moved(at, a, b) for a in "zx" for b in (1, -1)] + row + [partner])
    copies = Copies(send, recv)
    me = (at["z"], at["x"], at["c"], at["y"])
    kept, sent = [], []

    def keep(src, dst):
        cp = pltpu.make_async_copy(src, dst, local.at[len(kept)])
        cp.start()
        kept.append(cp)
        return cp

    keep(q_in.at[at["y"]], q_g.at[me])
    qx = [copies.start(q_in.at[to["y"]], q_g.at[me], to) for to in row]
    q_done, c_done, done = [], [], []
    fc = [gather_flow(c_g, at, (0, 1536), "xzy", (), copies, partner, c_done, c_in),
          gather_flow(c_g, at, (1536, 1536), "zxy", (), copies, partner, c_done, c_in)]
    fab = [gather_flow(dst, at, (k * n, n), axes, (), copies, partner, done, src)
           for k in range(2) for src, dst, axes, n in ((wout_in, wout_g, "yzx", 512), (win_in, win_g, "yxz", 2048))]
    flows = fab[0:2] + fc[0:1] + fab[2:4] + fc[1:2]
    for f in flows:
        next(f)
    keep(x_in, x_g.at[at["y"]])
    up, down = row[0], row[1]
    keep(cap_in, e_o.at[:, quarter(at)])
    ee = [copies.start(cap_in, e_o.at[:, quarter(at)], to) for to in row]
    for src, dst, to in ((wout_in, wout_g, done), (win_in, win_g, done), (c_in, c_g, c_done)):
        keep(src, dst.at[me])
        to.append(copies.start(src, dst.at[me], partner))
    for s in [kept[0]] + qx:
        s.wait()
    q_own = block(q_g, at, {"y"}, slice(None))
    q_done.append(copies.start(q_own, q_own, partner))
    fq = [gather_flow(q_g, at, (0, 640), "zx", {"y"}, copies, partner, q_done),
          gather_flow(q_g, at, (640, 768), "xz", {"y"}, copies, partner, q_done)]
    for f in fq:
        next(f)
    for s in kept[1:]:
        s.wait()
    for k in range(4):
        for f in fq:
            next(f, None)
        for f in flows:
            next(f)
        if k == 0:
            xx = [copies.start(x_in, x_g.at[at["y"]], to) for to in (up, down)]
        if k == 1:
            for s in xx:
                s.wait()
            low, high = slice(0, 128), slice(128, 256)
            x2s = [copies.start(x_g.at[down["y"], low], x_g.at[down["y"], low], up),
                   copies.start(x_g.at[up["y"], high], x_g.at[up["y"], high], down)]
    for s in x2s + ee + q_done:
        s.wait()

    wide = q_g[:, :, :, :, :, 1280:1408].reshape(1024, 128)
    wide_o[...] = wide
    vec[...] = wide.astype(F32).T[0:16, :]
    wq_o[...] = q_g[:, :, :, :, :, 0:1280].reshape(1024, 1280)
    done.append(keep(x_g, x_out))
    done.append(keep(wq_o, wq_out))
    done.append(keep(e_o, e_out))
    project(x_g.reshape(1024, 1024), wq_o, vec, n1, qkv)
    done.append(keep(qkv, qkv_out))
    ckv[...] = mm(e_o[...], wq_o[:, 768:1280]).astype(BF)
    self_forward(qkv, att, lse)
    done.append(keep(lse, lse_out))
    own, theirs = pl.ds(0, 256), pl.ds(256, 256)
    for to in row:
        sent.append(copies.start(att.at[quarter(to)], att_o.at[:, quarter(at)], to))
        sent.append(copies.start(ckv.at[:, 0:256], ck_o.at[:, quarter(at)], to))
        sent.append(copies.start(ckv.at[:, 256:512], cv_o.at[:, quarter(at)], to))
    sent.append(keep(att.at[quarter(at)], att_o.at[:, quarter(at)]))
    sent.append(keep(ckv.at[:, 0:256], ck_o.at[:, quarter(at)]))
    sent.append(keep(ckv.at[:, 256:512], cv_o.at[:, quarter(at)]))
    done.append(keep(dy_in.at[:, half(1024, at)], dy_o.at[own]))
    done.append(copies.start(dy_in.at[:, half(1024, partner)], dy_o.at[theirs], partner))
    for f in fc:
        next(f)
    for f in fc:
        next(f, None)
    for f in fab:
        next(f)
    for s in sent + c_done:
        s.wait()

    done.append(keep(c_g, c_out))
    done.append(keep(ck_o, ck_out))
    done.append(keep(cv_o, cv_out))

    def hand_over(ref, to):
        done.append(copies.start(ref, to.at[theirs], partner))
        done.append(keep(ref, to.at[own]))

    def square(m):
        return c_g[:, :, :, :, :, m * 1024:(m + 1) * 1024].reshape(1024, 1024)

    hand_over(att_o, att_out)
    x1[...] = mm(att_o[...], square(0))

    def by_rows(body):
        loop(4, lambda i: body(pl.ds(pl.multiple_of(i * 64, 64), 64)))

    def after_self(r):
        v = x_g[at["y"], r, :].astype(F32) + x1[r, :] + vec[6:7, :]
        x1[r, :] = v
        z, _ = normed(v)
        n2_o[r, :] = (z * vec[1:2, :] + vec[4:5, :]).astype(BF)

    by_rows(after_self)
    done.append(keep(x1, x1_out))
    hand_over(n2_o, n2_out)
    cq[...] = mm(n2_o[...], square(1)).astype(BF)
    done.append(keep(cq, cq_out))
    loop(8, lambda p: cross_forward(p, length[0], ck_o, cv_o, cq, probs, catt_o))
    done.append(keep(probs, probs_out))
    hand_over(catt_o, catt_out)
    x2[...] = mm(catt_o[...], square(2))

    def after_cross(r):
        v = x1[r, :] + x2[r, :] + vec[7:8, :]
        x2[r, :] = v
        z, _ = normed(v)
        n3_o[r, :] = (z * vec[2:3, :] + vec[5:6, :]).astype(BF)

    by_rows(after_cross)
    done.append(keep(x2, x2_out))
    hand_over(n3_o, n3_out)
    for f in fab:
        next(f, None)
    for s in done:
        s.wait()


def gathered(length, w_qkv, w_ckv, w_so, w_cq, w_co, vectors, win_in, wout_in, x_in, cap_in, dy_in):
    s = jax.ShapeDtypeStruct
    anywhere, vm = pl.BlockSpec(memory_space=pl.ANY), pl.BlockSpec(memory_space=pltpu.VMEM)
    kept = [((4, 256, 1024), BF), ((1024, 1280), BF), ((1024, 768), BF), ((4, 1, 1024), F32), ((512, 1024), BF), ((128, 1024), BF),
            ((128, 1024), BF), ((128, 1024), BF), ((256, 1024), F32), ((256, 1024), F32), ((512, 1024), BF), ((512, 1024), BF),
            ((512, 1024), BF), ((16, 128, 256), F32), ((256, 1024), BF)]
    outs = [s((4, 4, 2, 4, 8, 3072), BF), s((4, 4, 2, 4, 8, 4096), BF), s((4, 4, 2, 4, 32, 1024), BF), s((512, 512), BF)]
    outs += [s(*o) for o in kept] + [s((16, 1024), F32), s((1024, 128), BF)]
    n = 196
    mine = [pltpu.VMEM((256, 1024) if shape == (512, 1024) else shape, kind) for shape, kind in kept]
    return pl.pallas_call(
        gather_kernel, out_shape=outs, in_specs=[pl.BlockSpec(memory_space=pltpu.SMEM)] + [vm] * 6 + [anywhere] * 5,
        out_specs=[anywhere] * 19 + [vm] * 2,
        scratch_shapes=mine + [pltpu.VMEM((4, 8, 1408), BF), pltpu.VMEM((8, 3072), BF), pltpu.VMEM((4, 4, 2, 4, 8, 3072), BF),
                        pltpu.VMEM((4, 4, 2, 4, 8, 1408), BF), pltpu.VMEM((1024, 1024), BF), pltpu.VMEM((1024, 256), BF), pltpu.VMEM((128, 512), BF),
                        pltpu.SemaphoreType.DMA((n,)), pltpu.SemaphoreType.DMA((n,)), pltpu.SemaphoreType.DMA((40,))],
        compiler_params=pltpu.CompilerParams(collective_id=0, has_side_effects=True, vmem_limit_bytes=60 << 20),
        name="gather_and_attend",
    )(length, w_qkv, w_ckv, w_so, w_cq, w_co, vectors, win_in, wout_in, x_in, cap_in, dy_in)


def middle_kernel(x2_in, n3_in, dy_in, vec, wide, x1_in, probs_in, cq_in, ck_in, cv_in, wc, win, wout,
                  out, dx1_o, datt_o, dckv_o, u_o, dh_o, r1_o, dcq_o, r2_o, sums,
                  so, wcq, co, wi, wo, x1, x2, probs, cq, ck, cv, ya, dn, dca, dh, r1, dcq, r2, n3, spread, sem, send, recv):
    at = position()
    partner = moved(at, "c", 1)
    barrier = pltpu.get_barrier_semaphore()
    pl.semaphore_signal(barrier, inc=1, device_id=device(partner), device_id_type=MESH)
    chunk = 512
    n_chunk = wi.shape[1] // chunk
    width = 8 * chunk // 32

    def ff_loads(i):
        cols = pl.ds(pl.multiple_of(i * chunk, chunk), chunk)
        return (pltpu.make_async_copy(win.at[:, cols], wi.at[:, cols], sem.at[2 * i]),
                pltpu.make_async_copy(wout.at[cols], wo.at[cols], sem.at[2 * i + 1]))

    n3_load = pltpu.make_async_copy(n3_in.at[pl.ds(0, 256)], n3, sem.at[39])
    n3_load.start()
    for i in range(n_chunk):
        for l in ff_loads(i):
            l.start()
    late = [(wc.at[:, pl.ds(2048, 1024)], co), (probs_in, probs), (cq_in, cq), (ck_in, ck), (cv_in, cv),
            (wc.at[:, pl.ds(1024, 1024)], wcq), (x1_in, x1), (wc.at[:, pl.ds(0, 1024)], so)]
    late = [pltpu.make_async_copy(a, b, sem.at[2 * n_chunk + k]) for k, (a, b) in enumerate(late)]
    for l in late:
        l.start()

    def by_rows(body):
        loop(4, lambda i: body(pl.ds(pl.multiple_of(i * 64, 64), 64)))

    def row(k):
        return vec[k:k + 1, :]

    def place(shape, at_row, at_unit):
        src, dst = lax.broadcasted_iota(jnp.int32, shape, at_row), lax.broadcasted_iota(jnp.int32, shape, at_unit)
        return (lax.div(src, 8) * 32 + lax.rem(src, 8)), dst

    for j in range(4):
        src, dst = place((width, chunk), 0, 1)
        spread[j] = jnp.where(src + 8 * j == dst, 1.0, 0.0).astype(BF)

    sums[...] = jnp.zeros_like(sums)
    ya[...] = jnp.zeros_like(ya)
    dn[...] = jnp.zeros_like(dn)

    def feed(i):
        for l in ff_loads(i):
            l.wait()
        cols = pl.ds(pl.multiple_of(i * chunk, chunk), chunk)
        part = pl.ds(pl.multiple_of(i * width, width), width)
        columns = wide[part, :].astype(F32).T.astype(BF)
        bias = sum(mm(columns[9 + j:10 + j, :], spread[j]) for j in range(4))
        h = mm(n3[...], wi[:, cols]) + bias
        u, slope = gelu_both(h)
        u = u.astype(BF)
        u_o[0:256, cols] = u
        ya[...] += mm(u, wo[cols, :])
        d = (mm_cols(dy_in[...], wo[cols, :]) * slope).astype(BF)
        dh[:, cols] = d
        total = jnp.sum(d.astype(F32), axis=0, keepdims=True)
        high = total.astype(BF)
        low = (total - high.astype(F32)).astype(BF)
        for j in range(4):
            sums[9 + j:10 + j, part] = mm_cols(high, spread[j]) + mm_cols(low, spread[j])
        dn[...] += mm_cols(d, wi[:, cols])

    n3_load.wait()
    loop(n_chunk, feed)
    pl.semaphore_wait(barrier, 1)
    copies = Copies(send, recv)
    own, theirs = pl.ds(0, 256), pl.ds(256, 256)
    sent = [copies.start(u_o.at[own], u_o.at[theirs], partner)]

    def share(src, dst):
        n = src.shape[1]
        cp = pltpu.make_async_copy(src.at[:, half(n, at)], dst.at[own], sem.at[2 * n_chunk + 8 + len(sent)])
        cp.start()
        sent.append(cp)
        sent.append(copies.start(src.at[:, half(n, partner)], dst.at[theirs], partner))

    share(dh, dh_o)

    def after_feed(r):
        v = x2_in[r, :]
        out[r, :] = (v + ya[r, :] + row(8)).astype(BF)
        dy = dy_in[r, :].astype(F32)
        dv, dgain, dshift = norm_back(v, dn[r, :], row(2))
        d = dy + dv
        x2[r, :] = d
        r2[r, :] = d.astype(BF)
        sums[2:3, :] += dgain
        sums[5:6, :] += dshift
        sums[7:8, :] += jnp.sum(d, axis=0, keepdims=True)
        sums[8:9, :] += jnp.sum(dy, axis=0, keepdims=True)

    by_rows(after_feed)
    share(r2, r2_o)

    for l in late[:5]:
        l.wait()
    dca[...] = mm_cols(r2[...], co[...]).astype(BF)

    def cross_backward(p):
        cols = pl.ds(pl.multiple_of(p * 128, 128), 128)
        k, v, q, d = ck[:, cols], cv[:, cols], cq[:, cols], dca[:, cols]
        dk = dv = jnp.zeros((128, 128), F32)
        dq = []
        for head in range(2):
            lanes = lanes_of(q.shape, head)
            qh = jnp.where(lanes, q, jnp.zeros_like(q))
            dout = jnp.where(lanes, d, jnp.zeros_like(d))
            prob = probs[2 * p + head]
            dp = mm_cols(v, dout)
            ds = (prob * (dp - jnp.sum(dp * prob, axis=0, keepdims=True))).astype(BF)
            dv += mm(prob.astype(BF), dout)
            dk += mm(ds, qh)
            dq.append(mm_rows(ds, k))
        dcq[:, cols] = (jnp.where(lanes_of(q.shape, 0), dq[0], dq[1]) * SCALE).astype(BF)
        dckv_o[:, cols] = (dk * SCALE).astype(BF)
        dckv_o[:, pl.ds(pl.multiple_of(1024 + p * 128, 128), 128)] = dv.astype(BF)

    loop(8, cross_backward)
    share(dcq, dcq_o)
    for l in late[5:]:
        l.wait()
    dn[...] = mm_cols(dcq[...], wcq[...])

    def before_cross(r):
        dv, dgain, dshift = norm_back(x1[r, :], dn[r, :], row(1))
        d = x2[r, :] + dv
        dx1_o[r, :] = d
        r1[r, :] = d.astype(BF)
        sums[1:2, :] += dgain
        sums[4:5, :] += dshift
        sums[6:7, :] += jnp.sum(d, axis=0, keepdims=True)

    by_rows(before_cross)
    share(r1, r1_o)
    datt_o[...] = mm_cols(r1[...], so[...]).astype(BF)
    for s in sent:
        s.wait()


def middle(x2, n3, dy, vec, wide, x1, probs, cq, ck, cv, wc, win, wout):
    s, V = jax.ShapeDtypeStruct, pltpu.VMEM
    outs = [s((256, 1024), BF), s((256, 1024), F32), s((256, 1024), BF), s((128, 2048), BF), s((512, 4096), BF), s((512, 2048), BF),
            s((512, 512), BF), s((512, 512), BF), s((512, 512), BF), s((16, 1024), F32)]
    vm, anywhere = pl.BlockSpec(memory_space=V), pl.BlockSpec(memory_space=pl.ANY)
    scratch = [V((1024, 1024), BF)] * 3 + [V((1024, 4096), BF), V((4096, 1024), BF)]
    scratch += [V((256, 1024), F32)] * 2 + [V((16, 128, 256), F32), V((256, 1024), BF), V((128, 1024), BF), V((128, 1024), BF)]
    scratch += [V((256, 1024), F32)] * 2 + [V((256, 1024), BF), V((256, 4096), BF)] + [V((256, 1024), BF)] * 4 + [V((4, 128, 512), BF)]
    scratch += [pltpu.SemaphoreType.DMA((40,)), pltpu.SemaphoreType.DMA((8,)), pltpu.SemaphoreType.DMA((8,))]
    return pl.pallas_call(
        middle_kernel, out_shape=outs,
        in_specs=[vm, anywhere] + [vm] * 3 + [anywhere] * 8, out_specs=[vm] * 4 + [vm] * 1 + [anywhere] * 4 + [vm],
        scratch_shapes=scratch,
        compiler_params=pltpu.CompilerParams(collective_id=2, has_side_effects=True, vmem_limit_bytes=60 << 20),
        name="middle",
    )(x2, n3, dy, vec, wide, x1, probs, cq, ck, cv, wc, win, wout)


ORDER = ("z", "x", "c", "y")
def part(ref, at, whole, **fixed):
    return ref.at[tuple(fixed[a] if a in fixed else slice(None) if a in whole else at[a] for a in ORDER)]


def each(shape, body):
    total = 1
    for s in shape:
        total *= s

    def step(i, _):
        index, rest = [], i
        for s in reversed(shape):
            index.insert(0, lax.rem(rest, s))
            rest = lax.div(rest, s)
        body(tuple(index))
        return 0

    if total == 1:
        body((0,) * len(shape))
    else:
        lax.fori_loop(0, total, step, 0)


def add_into(dst, *srcs):
    def one(index):
        total = dst[index].astype(jnp.float32)
        for s in srcs:
            total += s[index].astype(jnp.float32)
        dst[index] = total.astype(dst.dtype)

    each(dst.shape[:-2], one)


def landing_shapes(rows, cols, axes):
    whole, shapes = {"z", "x", "y"}, []
    for axis in axes:
        whole = whole - {axis}
        shapes.append(pltpu.VMEM((6, *[4 for a in ("z", "x", "y") if a in whole], rows, cols), jnp.bfloat16))
    return tuple(shapes)


def scatter_flow(g, landing, at, axes, whole, copies):
    whole = set(whole)
    for axis, land in zip(axes, landing):
        up, down, far = moved(at, axis, 1), moved(at, axis, -1), moved(at, axis, 2)
        rest = whole - {axis}
        def blk(place, core):
            return part(g, at, rest, **{axis: place[axis], "c": core})
        s = [
            copies.start(blk(far, 0), land.at[0], up),
            copies.start(blk(far, 1), land.at[1], down),
        ]
        if axis == axes[0]:
            yield
        s += [copies.start(blk(up, 1), land.at[2], up), copies.start(blk(down, 0), land.at[3], down)]
        yield
        s[0].wait_recv()
        add_into(blk(up, 0), land.at[0])
        s.append(copies.start(blk(up, 0), land.at[4], up))
        s[1].wait_recv()
        add_into(blk(down, 1), land.at[1])
        s.append(copies.start(blk(down, 1), land.at[5], down))
        yield
        s[2].wait_recv()
        s[5].wait_recv()
        add_into(blk(at, 1), land.at[2], land.at[5])
        s[3].wait_recv()
        s[4].wait_recv()
        add_into(blk(at, 0), land.at[3], land.at[4])
        for q in s:
            q.wait_send()
        whole = rest


def reduce_kernel(u, dy, n3, dh, att, r1, n2, dcq, catt, r2, datt, dckv, sums, x_in, qkv_in, lse, wq_in, e, dx1_in, vec,
                  out_a, out_b, out_c, out_q, tok, cap,
                  u2, dy2, n32, dh2, a2, r2s, ga, gb, gc, gq, gql, datt4, dckv4, dcap, dcap4, dqkv, n1, dk, dv, dn, dn4, v13, x_all, qkv, wq, dx1,
                  la, lb, lc0, lc1, lc2, lq0, lq1, fa, fb, fc, fq, send, recv, local):
    at = position()
    partner = moved(at, "c", 1)
    row = [moved(at, "y", b) for b in (1, 3, 2)]
    ring = row + [moved(o, "c", 1) for o in row] + [partner]
    c, y = at["c"], at["y"]
    started = []

    def load(src, dst):
        cp = pltpu.make_async_copy(src, dst, local.at[len(started)])
        cp.start()
        started.append(cp)
        return cp

    def ready(loads):
        for l in loads:
            l.wait()

    kb = [load(n3, n32), load(dh, dh2)]
    ka = [load(u, u2), load(dy, dy2)]
    own_rows = pl.ds(pl.multiple_of(y * 256, 256), 256)
    d_own = load(datt.at[:, quarter(at)], datt4.at[own_rows])
    kv_own = [load(dckv.at[:, pl.ds(pl.multiple_of(k * 1024 + y * 256, 256), 256)], dckv4.at[y, :, pl.ds(k * 256, 256)]) for k in range(2)]
    kp = [load(qkv_in, qkv), load(wq_in, wq), load(x_in, x_all)]
    kc = []
    for k, (a, b) in enumerate(((catt, r2), (n2, dcq), (att, r1))):
        kc += [load(a, a2.at[k]), load(b, r2s.at[k])]
    kp.append(load(dx1_in, dx1))
    greet([moved(at, a, b) for a in "zx" for b in (1, -1)] + ring)
    copies = Copies(send, recv)
    dd = [copies.start(datt.at[:, quarter(to)], datt4.at[own_rows], to) for to in row]
    kvs = [copies.start(dckv.at[:, pl.ds(pl.multiple_of(k * 1024 + to["y"] * 256, 256), 256)], dckv4.at[y, :, pl.ds(k * 256, 256)], to)
           for to in row for k in range(2)]

    def grad_b(z):
        lhs = n32[:, pl.ds(pl.multiple_of(z * 256, 256), 256)]
        for k in range(4):
            g = mm_rows(lhs, dh2[:, k * 512:(k + 1) * 512])
            gb[z, :, :, :, :, k * 512:(k + 1) * 512] = g.reshape(4, 2, 4, 8, 512).astype(BF)

    def grad_a(z, x):
        lhs = u2[:, pl.ds(pl.multiple_of((z * 4 + x) * 256, 256), 256)]
        ga[z, x] = mm_rows(lhs, dy2[...]).reshape(2, 4, 32, 512).astype(BF)

    def grad_c(k, z):
        g = mm_rows(a2[k, :, pl.ds(pl.multiple_of(z * 256, 256), 256)], r2s[k])
        gc[z, :, :, :, :, k * 512:(k + 1) * 512] = g.reshape(4, 2, 4, 8, 512).astype(BF)

    every = {"z", "x", "y"}
    fl_b = scatter_flow(gb, lb, at, ("z", "x", "y"), every, copies)
    fl_a = scatter_flow(ga, la, at, ("x", "z", "y"), every, copies)
    fl_c = [scatter_flow(gc.at[:, :, :, :, :, pl.ds(k * 512, 512)], land, at, axes, every, copies)
            for k, (land, axes) in enumerate(((lc0, "zxy"), (lc1, "xzy"), (lc2, "yzx")))]
    far_z, far_x = moved(at, "z", 2)["z"], moved(at, "x", 2)["x"]
    ready(kb)
    grad_b(far_z)
    next(fl_b)
    ready(ka)
    loop(4, lambda i: grad_a(i, far_x))
    next(fl_a)
    loop(3, lambda i: grad_b(lax.rem(far_z + 1 + i, 4)))
    next(fl_b)
    loop(12, lambda i: grad_a(lax.rem(i, 4), lax.rem(far_x + 1 + lax.div(i, 4), 4)))
    next(fl_a)
    ready(kc)
    for k in range(3):
        loop(4, functools.partial(grad_c, k))
        next(fl_c[k])
        next(fl_c[k])

    ready(kp)
    for s in kv_own + kvs:
        s.wait()
    dckv4[0] = sum(dckv4[k].astype(F32) for k in range(4)).astype(BF)
    dcap[...] = mm_cols(dckv4[0], wq[:, 768:1280]).astype(BF)
    cap_own = load(dcap.at[:, quarter(at)], dcap4.at[y])
    caps = [copies.start(dcap.at[:, quarter(to)], dcap4.at[y], to) for to in row]

    d_own.wait()
    for s in dd:
        s.wait()
    self_backward(0, qkv, lse, datt4, dqkv, dk, dv)
    self_backward(1, qkv, lse, datt4, dqkv, dk, dv)
    next(fl_b)
    next(fl_a)
    v13[...] = jnp.zeros_like(v13)
    v13[0:16, :] = sums[...]
    gain, shift = vec[0:1, :], vec[3:4, :]

    def norm_rows(i):
        r = pl.ds(pl.multiple_of(i * 128, 128), 128)
        z, _ = normed(x_all[r, :].astype(F32))
        n1[r, :] = (z * gain + shift).astype(BF)
        d = mm_cols(dqkv[r, :], wq[:, 0:768])
        dn[r, :] = d.astype(BF)
        v13[0:1, :] += jnp.sum(d * z, axis=0, keepdims=True)
        v13[3:4, :] += jnp.sum(d, axis=0, keepdims=True)

    loop(8, norm_rows)
    dns = [copies.start(dn.at[pl.ds(pl.multiple_of(to["y"] * 256, 256), 256)], dn4.at[k], to) for k, to in enumerate(row)]
    for f in fl_c:
        next(f)

    def grad_q(z):
        cols = pl.ds(pl.multiple_of(z * 256, 256), 256)
        gq[z, :, :, :, :, 0:768] = mm_rows(n1[:, cols], dqkv[...]).reshape(4, 2, 4, 8, 768).astype(BF)
        gq[z, :, :, :, :, 768:1280] = mm_rows(e[:, cols], dckv4[0]).reshape(4, 2, 4, 8, 512).astype(BF)

    loop(4, grad_q)
    gq[:, :, :, :, :, 1280:1408] = v13[...].T.reshape(4, 4, 2, 4, 8, 128).astype(BF)
    gq[:, :, :, :, :, 1408:1536] = jnp.zeros((4, 4, 2, 4, 8, 128), BF)
    n_q = gq.shape[-1]
    pq = copies.start(gq.at[:, :, :, :, :, half(n_q, partner)], gql, partner)
    next(fl_b)
    next(fl_a)
    pq.wait()
    mine = gq.at[:, :, :, :, :, half(n_q, at)]
    add_into(mine, gql)
    q_cols = lambda k: gq.at[:, :, :, :, :, pl.ds(pl.multiple_of(c * 768 + k * 384, 128), 384)]
    fl_q = [scatter_flow(q_cols(0), lq0, at, ("x", "z"), every, copies), scatter_flow(q_cols(1), lq1, at, ("z", "x"), every, copies)]
    for f in fl_q + fl_q + fl_c + [fl_b, fl_a] + fl_q:
        next(f)
    for s in dns + caps + [cap_own]:
        s.wait()

    def token_rows(i):
        r = pl.ds(pl.multiple_of(i * 64, 64), 64)
        here = pl.ds(pl.multiple_of(y * 256 + i * 64, 64), 64)
        d = dn[here, :].astype(F32) + dn4[0, r, :].astype(F32) + dn4[1, r, :].astype(F32) + dn4[2, r, :].astype(F32)
        back, _, _ = norm_back(x_all[here, :].astype(F32), d, gain)
        tok[r, :] = dx1[r, :] + back

    loop(4, token_rows)
    cap[...] = sum(dcap4[k].astype(F32) for k in range(4))
    finish(fl_c + [fl_b, fl_a] + fl_q)

    last = []
    for g, f in ((ga, fa), (gb, fb), (gc, fc)):
        last.append(copies.start(g.at[at["z"], at["x"], partner["c"], y], f, partner))
    for o in ring:
        last.append(copies.start(mine.at[at["z"], at["x"], o["c"], o["y"]], fq.at[c, y], o))
    own_q = load(mine.at[at["z"], at["x"], c, y], fq.at[c, y])
    for g, o in ((ga, out_a), (gb, out_b), (gc, out_c)):
        o[c] = g[at["z"], at["x"], c, y]
    for s in last + [own_q]:
        s.wait()
    for f, o in ((fa, out_a), (fb, out_b), (fc, out_c)):
        o[partner["c"]] = f[...]
    out_q[...] = fq[...]


def reduced(u, dy, n3, dh, att, r1, n2, dcq, catt, r2, datt, dckv, sums, x_all, qkv, lse, wq, e, dx1, vec):
    n_c, n_q = 1536, 768
    V = pltpu.VMEM
    scratch = [
        V((512, 4096), BF), V((512, 512), BF), V((512, 1024), BF), V((512, 2048), BF), V((3, 512, 1024), BF), V((3, 512, 512), BF),
        V((4, 4, 2, 4, 32, 512), BF), V((4, 4, 2, 4, 8, 2048), BF), V((4, 4, 2, 4, 8, n_c), BF),
        V((4, 4, 2, 4, 8, 2 * n_q), BF), V((4, 4, 2, 4, 8, n_q), BF),
        V((1024, 256), BF), V((4, 128, 512), BF), V((128, 1024), BF), V((4, 128, 256), BF), V((1024, 768), BF), V((1024, 1024), BF),
        V((1024, 128), F32), V((1024, 128), F32), V((1024, 1024), BF), V((3, 256, 1024), BF), V((128, 1024), F32),
        V((1024, 1024), BF), V((1024, 768), BF), V((1024, 1280), BF), V((256, 1024), F32),
    ]
    scratch += [landing_shapes(32, 512, "xzy"), landing_shapes(8, 2048, "zxy")]
    scratch += [landing_shapes(8, 512, axes) for axes in ("zxy", "xzy", "yzx")] + [landing_shapes(8, 384, axes) for axes in ("xz", "zx")]
    scratch += [V((32, 512), BF), V((8, 2048), BF), V((8, n_c), BF), V((2, 4, 8, n_q), BF)]
    n = 160
    scratch += [pltpu.SemaphoreType.DMA((n,)), pltpu.SemaphoreType.DMA((n,)), pltpu.SemaphoreType.DMA((32,))]
    s = jax.ShapeDtypeStruct
    outs = [s((2, 32, 512), BF), s((2, 8, 2048), BF), s((2, 8, n_c), BF), s((2, 4, 8, n_q), BF), s((256, 1024), F32), s((128, 256), F32)]
    anywhere, vm = pl.BlockSpec(memory_space=pl.ANY), pl.BlockSpec(memory_space=pltpu.VMEM)
    return pl.pallas_call(
        reduce_kernel, out_shape=outs, in_specs=[anywhere] * 12 + [vm, anywhere, anywhere, vm, anywhere, vm, anywhere, vm], out_specs=[vm] * 6,
        scratch_shapes=scratch,
        compiler_params=pltpu.CompilerParams(collective_id=1, has_side_effects=True, vmem_limit_bytes=62 << 20),
        name="reduce_gradients",
    )(u, dy, n3, dh, att, r1, n2, dcq, catt, r2, datt, dckv, sums, x_all, qkv, lse, wq, e, dx1, vec)


def finish_kernel(a, b, c, q, tok_in, cap_in, tok, cap, d_qkv, d_self_out, d_cross_q, d_cross_kv, d_cross_out, d_in, d_out, d_gains, d_shifts, d_biases, d_in_bias):
    tok[...] = tok_in[...]
    cap[...] = cap_in[...]
    for k in range(2):
        d_out[:, k * 512:(k + 1) * 512] = a[k].astype(F32)
        d_in[:, k * 2048:(k + 1) * 2048] = b[k].astype(F32)
        for m, ref in enumerate((d_cross_out, d_cross_q, d_self_out)):
            ref[:, k * 512:(k + 1) * 512] = c[k, :, m * 512:(m + 1) * 512].astype(F32)
    for y in range(4):
        for m in range(3):
            d_qkv[:, m * 1024 + y * 256:m * 1024 + (y + 1) * 256] = q[0, y, :, m * 256:(m + 1) * 256].astype(F32)
        for m in range(2):
            d_cross_kv[:, m * 1024 + y * 256:m * 1024 + (y + 1) * 256] = q[1, y, :, m * 256:(m + 1) * 256].astype(F32)
    vectors = sum(q[1, y, :, 512:640].astype(F32) for y in range(4)).T
    for m, ref in enumerate((d_gains, d_shifts, d_biases)):
        ref[...] = vectors[3 * m:3 * m + 3, :]
    d_in_bias[...] = jnp.concatenate([vectors[9 + j:10 + j, :] for j in range(4)], axis=1)


def assembled(a, b, c, q, tok, cap):
    shapes = [(256, 1024), (128, 256), (8, 3072), (8, 1024), (8, 1024), (8, 2048), (8, 1024), (8, 4096), (32, 1024), (3, 8), (3, 8), (3, 8), (1, 32)]
    vm = pl.BlockSpec(memory_space=pltpu.VMEM)
    return pl.pallas_call(
        finish_kernel, out_shape=[jax.ShapeDtypeStruct(s, F32) for s in shapes], in_specs=[vm] * 6, out_specs=[vm] * 13, name="assemble",
    )(a, b, c, q, tok, cap)


def local(tokens, captions, cap_lengths, w_qkv, w_self_out, w_cross_q, w_cross_kv, w_cross_out, w_in, w_out,
          norm_gains, norm_shifts, out_biases, in_bias, out_grad):
    vectors = jnp.concatenate([norm_gains.T, norm_shifts.T, out_biases.T, in_bias.reshape(4, 8).T], axis=1)
    vectors = jnp.pad(vectors, ((0, 0), (0, 128 - 13)))
    dy = out_grad[0]
    (c_g, win_g, wout_g, dy_pair, x_g, wq, qkv, lse, att, ck, cv, e, x1, x2, n2, n3, catt, probs, cq, vec, wide) = gathered(
        cap_lengths, w_qkv, w_cross_kv, w_self_out, w_cross_q, w_cross_out, vectors, w_in, w_out, tokens[0], captions[0], dy)
    wc, full_in, full_out = c_g.reshape(1024, -1), win_g.reshape(1024, -1), wout_g.reshape(4096, 1024)
    layer_out, dx1, datt, dckv, u, dh, r1, dcq, r2, sums = middle(
        x2, n3, dy, vec, wide, x1, probs, cq, ck, cv, wc, full_in, full_out)
    out_a, out_b, out_c, out_q, tokens_grad, captions_grad = reduced(
        u, dy_pair, n3, dh, att, r1, n2, dcq, catt, r2, datt, dckv, sums, x_g.reshape(1024, 1024), qkv, lse, wq, e, dx1, vec)
    tokens_grad, captions_grad, *grads, d_in_bias = assembled(out_a, out_b, out_c, out_q, tokens_grad, captions_grad)
    return (layer_out[None], tokens_grad[None], captions_grad[None], *grads, d_in_bias.reshape(32))


def solution(mesh):
    rows, tokens, vectors = P(("dp", "seq"), None), P("dp", "seq", None), P(None, ("dp", "seq"))
    captions = P("dp", None, "seq")
    return jax.shard_map(
        local, mesh=mesh,
        in_specs=(tokens, captions, P("dp"), *[rows] * 7, *[vectors] * 3, P(("dp", "seq")), tokens),
        out_specs=(tokens, tokens, captions, *[rows] * 7, *[vectors] * 3, P(("dp", "seq"))),
        check_vma=False,
    )
```

```python
import functools

import jax
import jax.numpy as jnp
from jax import lax
from jax.experimental import pallas as pl
from jax.experimental.pallas import tpu as pltpu
from jax.sharding import PartitionSpec as P

MESH = pl.DeviceIdType.MESH
def position():
    dp, y = lax.axis_index("dp"), lax.axis_index("seq")
    return {"z": lax.div(dp, 8), "x": lax.rem(lax.div(dp, 2), 4), "c": lax.rem(dp, 2), "y": y}


def device(at):
    return (at["z"] * 8 + at["x"] * 2 + at["c"], at["y"])


def moved(at, axis, by):
    size = 2 if axis == "c" else 4
    return {**at, axis: lax.rem(at[axis] + by + size, size)}


class Copies:
    def __init__(self, send, recv):
        self.send, self.recv, self.used = send, recv, 0

    def start(self, src, dst, at):
        k = self.used
        self.used += 1
        assert k < self.send.shape[0]
        copy = pltpu.make_async_remote_copy(src_ref=src, dst_ref=dst, send_sem=self.send.at[k], recv_sem=self.recv.at[k], device_id=device(at), device_id_type=MESH)
        copy.start()
        return copy


def block(ref, at, whole, cols):
    idx = [slice(None) if axis in whole else at[axis] for axis in ("z", "x", "c", "y")]
    return ref.at[(*idx, slice(None), cols)]


def gather_flow(ref, at, cols, axes, whole, copies, partner, done, source=None):
    start, size = cols
    low_cols, high_cols = pl.ds(start, size // 256 * 128), pl.ds(start + size // 256 * 128, size - size // 256 * 128)
    cols = pl.ds(start, size)
    whole = set(whole)
    for axis in axes:
        up, down = moved(at, axis, 1), moved(at, axis, -1)
        own = block(ref, at, whole, cols)
        src = own if source is None else source.at[:, cols]
        source = None
        a = copies.start(src, own, up)
        b = copies.start(src, own, down)
        yield
        a.wait_recv()
        b.wait_recv()
        low, high = block(ref, down, whole, low_cols), block(ref, up, whole, high_cols)
        c = copies.start(low, low, up)
        d = copies.start(high, high, down)
        for p in (down, up):
            got = block(ref, p, whole, cols)
            done.append(copies.start(got, got, partner))
        yield
        c.wait_recv()
        d.wait_recv()
        far = block(ref, moved(at, axis, 2), whole, cols)
        done.append(copies.start(far, far, partner))
        for s in (a, b, c, d):
            s.wait_send()
        whole.add(axis)


EPSILON = 1e-05
MASKED = -1e30
SCALE = 64 ** -0.5
BF, F32 = jnp.bfloat16, jnp.float32
def mm(a, b):
    return jnp.dot(a, b, preferred_element_type=F32)


def mm_rows(a, b):
    return lax.dot_general(a, b, (((0,), (0,)), ((), ())), preferred_element_type=F32)


def mm_cols(a, b):
    return lax.dot_general(a, b, (((1,), (1,)), ((), ())), preferred_element_type=F32)


def normed(v):
    centred = v - jnp.mean(v, axis=-1, keepdims=True)
    r = lax.rsqrt(jnp.mean(centred * centred, axis=-1, keepdims=True) + EPSILON)
    return centred * r, r


def norm_back(v, d, gain):
    z, r = normed(v)
    w = d * gain
    dv = r * (w - jnp.mean(w, axis=-1, keepdims=True) - z * jnp.mean(w * z, axis=-1, keepdims=True))
    return dv, jnp.sum(d * z, axis=0, keepdims=True), jnp.sum(d, axis=0, keepdims=True)


def loop(n, body):
    def step(i, _):
        body(i)
        return 0

    lax.fori_loop(0, n, step, 0)


def gelu_both(h):
    cdf = 0.5 * (1.0 + lax.erf(h * (0.5 ** 0.5)))
    return h * cdf, cdf + h * jnp.exp(-0.5 * h * h) * (1.0 / (2.0 * 3.141592653589793) ** 0.5)


def lanes_of(pair_shape, head):
    lane = lax.broadcasted_iota(jnp.int32, pair_shape, 1)
    return (lane < 64) if head == 0 else (lane >= 64)


BLOCK = 256
def causal_keep(n, at):
    keys = lax.broadcasted_iota(jnp.int32, (n, BLOCK), 0)
    return keys <= lax.broadcasted_iota(jnp.int32, (n, BLOCK), 1) + at


def project(x, wq, vec, n1, qkv):
    def rows(i):
        r = pl.ds(pl.multiple_of(i * 128, 128), 128)
        z, _ = normed(x[r, :].astype(F32))
        n1[r, :] = (z * vec[0:1, :] + vec[3:4, :]).astype(BF)

    loop(8, rows)

    def cols(i):
        r = pl.ds(pl.multiple_of(i * BLOCK, BLOCK), BLOCK)
        qkv[r, :] = mm(n1[r, :], wq[:, 0:768]).astype(BF)

    loop(4, cols)


def self_forward(qkv, att, lse):
    def pair(p):
        for i in range(1024 // BLOCK):
            n, r = (i + 1) * BLOCK, slice(i * BLOCK, (i + 1) * BLOCK)
            at = lambda part: pl.ds(pl.multiple_of(part * 256 + p * 128, 128), 128)
            q, k, v = qkv[r, at(0)], qkv[0:n, at(1)], qkv[0:n, at(2)]
            keep = causal_keep(n, i * BLOCK)
            mixed = []
            for head in range(2):
                qh = jnp.where(lanes_of(q.shape, head), q, jnp.zeros_like(q))
                s = jnp.where(keep, mm_cols(k, qh) * SCALE, MASKED)
                top = jnp.max(s, axis=0, keepdims=True)
                e = jnp.exp(s - top)
                total = jnp.sum(e, axis=0, keepdims=True)
                lse[2 * p + head, :, r] = top + jnp.log(total)
                mixed.append(mm_rows((e * (1.0 / total)).astype(BF), v))
            att[r, at(0)] = jnp.where(lanes_of(q.shape, 0), mixed[0], mixed[1]).astype(BF)

    loop(2, pair)


def self_backward(p, i, qkv, lse, datt, dqkv, dk, dv):
    at = lambda part: pl.ds(part * 256 + p * 128, 128)
    if i == 0:
        dk[...] = jnp.zeros(dk.shape, F32)
        dv[...] = jnp.zeros(dv.shape, F32)
    n, r = (i + 1) * BLOCK, slice(i * BLOCK, (i + 1) * BLOCK)
    q, k, v, d = qkv[r, at(0)], qkv[0:n, at(1)], qkv[0:n, at(2)], datt[r, at(0)]
    keep = causal_keep(n, i * BLOCK)
    dq = []
    for head in range(2):
        lanes = lanes_of(q.shape, head)
        qh = jnp.where(lanes, q, jnp.zeros_like(q))
        dout = jnp.where(lanes, d, jnp.zeros_like(d))
        prob = jnp.where(keep, jnp.exp(mm_cols(k, qh) * SCALE - lse[2 * p + head, :, r]), 0.0)
        dp = mm_cols(v, dout)
        ds = (prob * (dp - jnp.sum(dp * prob, axis=0, keepdims=True))).astype(BF)
        dv[0:n, :] += mm(prob.astype(BF), dout)
        dk[0:n, :] += mm(ds, qh)
        dq.append(mm_rows(ds, k))
    dqkv[r, at(0)] = (jnp.where(lanes_of(q.shape, 0), dq[0], dq[1]) * SCALE).astype(BF)
    if n == 1024:
        dqkv[:, at(1)] = (dk[...] * SCALE).astype(BF)
        dqkv[:, at(2)] = dv[...].astype(BF)


def greet(others):
    barrier = pltpu.get_barrier_semaphore()
    for o in others:
        pl.semaphore_signal(barrier, inc=1, device_id=device(o), device_id_type=MESH)
    pl.semaphore_wait(barrier, len(others))


def half(n, of):
    return pl.ds(pl.multiple_of(of["c"] * (n // 2), 128), n // 2)


def finish(flows):
    live = list(flows)
    while live:
        for f in list(live):
            if next(f, "end") == "end":
                live.remove(f)


def quarter(of):
    return pl.ds(pl.multiple_of(of["y"] * 256, 256), 256)


def cross_forward(p, length, ck, cv, cq, probs, catt):
    cols = pl.ds(pl.multiple_of(p * 128, 128), 128)
    k, v, q = ck[:, cols], cv[:, cols], cq[:, cols]
    seen = lax.broadcasted_iota(jnp.int32, (128, 256), 0) < length
    mixed = []
    for head in range(2):
        qh = jnp.where(lanes_of(q.shape, head), q, jnp.zeros_like(q))
        s = jnp.where(seen, mm_cols(k, qh) * SCALE, MASKED)
        e = jnp.exp(s - jnp.max(s, axis=0, keepdims=True))
        prob = e / jnp.sum(e, axis=0, keepdims=True)
        probs[2 * p + head] = prob
        mixed.append(mm_rows(prob.astype(BF), v))
    catt[:, cols] = jnp.where(lanes_of(q.shape, 0), mixed[0], mixed[1]).astype(BF)


def gather_kernel(length, w_qkv, w_ckv, w_so, w_cq, w_co, vectors, win_in, wout_in, x_in, cap_in, dy_in,
                  c_out, win_g, wout_g, dy_o, x_out, wq_out, qkv_out, lse_out, att_out, ck_out, cv_out, e_out, x1_out, x2_out, n2_out, n3_out,
                  catt_out, probs_out, cq_out, vec,
                  x_g, wq_o, qkv, lse, att_o, ck_o, cv_o, e_o, x1, x2, n2_o, n3_o, catt_o, probs, cq,
                  q_in, c_in, c_g, q_g, n1, att, ckv, send, recv, local):
    at = position()
    partner = moved(at, "c", 1)
    row = [moved(at, "y", b) for b in (1, 3, 2)]
    q_in[:, :, 1280:1408] = jnp.broadcast_to(vectors[...], (4, 8, 128))
    for q in range(4):
        for m in range(3):
            q_in[q, :, m * 256:(m + 1) * 256] = w_qkv[:, m * 1024 + q * 256:m * 1024 + (q + 1) * 256]
        for m in range(2):
            q_in[q, :, 768 + m * 256:1024 + m * 256] = w_ckv[:, m * 1024 + q * 256:m * 1024 + (q + 1) * 256]
    for m, ref in enumerate((w_so, w_cq, w_co)):
        c_in[:, m * 1024:(m + 1) * 1024] = ref[...]
    greet([moved(at, a, b) for a in "zx" for b in (1, -1)] + row + [partner])
    copies = Copies(send, recv)
    me = (at["z"], at["x"], at["c"], at["y"])
    kept, sent = [], []

    def keep(src, dst):
        cp = pltpu.make_async_copy(src, dst, local.at[len(kept)])
        cp.start()
        kept.append(cp)
        return cp

    keep(q_in.at[at["y"]], q_g.at[me])
    qx = [copies.start(q_in.at[to["y"]], q_g.at[me], to) for to in row]
    q_done, c_done, done = [], [], []
    fc = [gather_flow(c_g, at, (0, 1536), "xzy", (), copies, partner, c_done, c_in),
          gather_flow(c_g, at, (1536, 1536), "zxy", (), copies, partner, c_done, c_in)]
    fab = [gather_flow(dst, at, (k * n, n), axes, (), copies, partner, done, src)
           for k in range(2) for src, dst, axes, n in ((wout_in, wout_g, "yzx", 512), (win_in, win_g, "yxz", 2048))]
    flows = fab[0:2] + fc[0:1] + fab[2:4] + fc[1:2]
    for f in flows:
        next(f)
    keep(x_in, x_g.at[at["y"]])
    up, down = row[0], row[1]
    keep(cap_in, e_o.at[:, quarter(at)])
    ee = [copies.start(cap_in, e_o.at[:, quarter(at)], to) for to in row]
    for src, dst, to in ((wout_in, wout_g, done), (win_in, win_g, done), (c_in, c_g, c_done)):
        keep(src, dst.at[me])
        to.append(copies.start(src, dst.at[me], partner))
    for s in [kept[0]] + qx:
        s.wait()
    q_own = block(q_g, at, {"y"}, slice(None))
    q_done.append(copies.start(q_own, q_own, partner))
    fq = [gather_flow(q_g, at, (0, 640), "zx", {"y"}, copies, partner, q_done),
          gather_flow(q_g, at, (640, 768), "xz", {"y"}, copies, partner, q_done)]
    for f in fq:
        next(f)
    for s in kept[1:]:
        s.wait()
    for k in range(4):
        for f in fq:
            next(f, None)
        for f in flows:
            next(f)
        if k == 0:
            xx = [copies.start(x_in, x_g.at[at["y"]], to) for to in (up, down)]
        if k == 1:
            for s in xx:
                s.wait()
            low, high = slice(0, 128), slice(128, 256)
            x2s = [copies.start(x_g.at[down["y"], low], x_g.at[down["y"], low], up),
                   copies.start(x_g.at[up["y"], high], x_g.at[up["y"], high], down)]
    for s in x2s + ee + q_done:
        s.wait()

    wide = q_g[:, :, :, :, :, 1280:1408].reshape(1024, 128)
    vec[...] = wide.astype(F32).T[0:16, :]
    wq_o[...] = q_g[:, :, :, :, :, 0:1280].reshape(1024, 1280)
    done.append(keep(x_g, x_out))
    done.append(keep(wq_o, wq_out))
    done.append(keep(e_o, e_out))
    project(x_g.reshape(1024, 1024), wq_o, vec, n1, qkv)
    done.append(keep(qkv, qkv_out))
    ckv[...] = mm(e_o[...], wq_o[:, 768:1280]).astype(BF)
    self_forward(qkv, att, lse)
    done.append(keep(lse, lse_out))
    own, theirs = pl.ds(0, 256), pl.ds(256, 256)
    for to in row:
        sent.append(copies.start(att.at[quarter(to)], att_o.at[:, quarter(at)], to))
        sent.append(copies.start(ckv.at[:, 0:256], ck_o.at[:, quarter(at)], to))
        sent.append(copies.start(ckv.at[:, 256:512], cv_o.at[:, quarter(at)], to))
    sent.append(keep(att.at[quarter(at)], att_o.at[:, quarter(at)]))
    sent.append(keep(ckv.at[:, 0:256], ck_o.at[:, quarter(at)]))
    sent.append(keep(ckv.at[:, 256:512], cv_o.at[:, quarter(at)]))
    done.append(keep(dy_in.at[:, half(1024, at)], dy_o.at[own]))
    done.append(copies.start(dy_in.at[:, half(1024, partner)], dy_o.at[theirs], partner))
    for f in fc:
        next(f)
    for f in fc:
        next(f, None)
    for f in fab:
        next(f)
    for s in sent + c_done:
        s.wait()

    done.append(keep(c_g, c_out))
    done.append(keep(ck_o, ck_out))
    done.append(keep(cv_o, cv_out))

    def hand_over(ref, to):
        done.append(copies.start(ref, to.at[theirs], partner))
        done.append(keep(ref, to.at[own]))

    def square(m):
        return c_g[:, :, :, :, :, m * 1024:(m + 1) * 1024].reshape(1024, 1024)

    hand_over(att_o, att_out)
    x1[...] = mm(att_o[...], square(0))

    def by_rows(body):
        loop(4, lambda i: body(pl.ds(pl.multiple_of(i * 64, 64), 64)))

    def after_self(r):
        v = x_g[at["y"], r, :].astype(F32) + x1[r, :] + vec[6:7, :]
        x1[r, :] = v
        z, _ = normed(v)
        n2_o[r, :] = (z * vec[1:2, :] + vec[4:5, :]).astype(BF)

    by_rows(after_self)
    done.append(keep(x1, x1_out))
    hand_over(n2_o, n2_out)
    cq[...] = mm(n2_o[...], square(1)).astype(BF)
    done.append(keep(cq, cq_out))
    loop(8, lambda p: cross_forward(p, length[0], ck_o, cv_o, cq, probs, catt_o))
    done.append(keep(probs, probs_out))
    hand_over(catt_o, catt_out)
    x2[...] = mm(catt_o[...], square(2))

    def after_cross(r):
        v = x1[r, :] + x2[r, :] + vec[7:8, :]
        x2[r, :] = v
        z, _ = normed(v)
        n3_o[r, :] = (z * vec[2:3, :] + vec[5:6, :]).astype(BF)

    by_rows(after_cross)
    done.append(keep(x2, x2_out))
    hand_over(n3_o, n3_out)
    for f in fab:
        next(f, None)
    for s in done:
        s.wait()


def gathered(length, w_qkv, w_ckv, w_so, w_cq, w_co, vectors, win_in, wout_in, x_in, cap_in, dy_in):
    s = jax.ShapeDtypeStruct
    anywhere, vm = pl.BlockSpec(memory_space=pl.ANY), pl.BlockSpec(memory_space=pltpu.VMEM)
    kept = [((4, 256, 1024), BF), ((1024, 1280), BF), ((1024, 768), BF), ((4, 1, 1024), F32), ((512, 1024), BF), ((128, 1024), BF),
            ((128, 1024), BF), ((128, 1024), BF), ((256, 1024), F32), ((256, 1024), F32), ((512, 1024), BF), ((512, 1024), BF),
            ((512, 1024), BF), ((16, 128, 256), F32), ((256, 1024), BF)]
    outs = [s((4, 4, 2, 4, 8, 3072), BF), s((4, 4, 2, 4, 8, 4096), BF), s((4, 4, 2, 4, 32, 1024), BF), s((512, 512), BF)]
    outs += [s(*o) for o in kept] + [s((16, 1024), F32)]
    n = 196
    mine = [pltpu.VMEM((256, 1024) if shape == (512, 1024) else shape, kind) for shape, kind in kept]
    return pl.pallas_call(
        gather_kernel, out_shape=outs, in_specs=[pl.BlockSpec(memory_space=pltpu.SMEM)] + [vm] * 6 + [anywhere] * 5,
        out_specs=[anywhere] * 19 + [vm],
        scratch_shapes=mine + [pltpu.VMEM((4, 8, 1408), BF), pltpu.VMEM((8, 3072), BF), pltpu.VMEM((4, 4, 2, 4, 8, 3072), BF),
                        pltpu.VMEM((4, 4, 2, 4, 8, 1408), BF), pltpu.VMEM((1024, 1024), BF), pltpu.VMEM((1024, 256), BF), pltpu.VMEM((128, 512), BF),
                        pltpu.SemaphoreType.DMA((n,)), pltpu.SemaphoreType.DMA((n,)), pltpu.SemaphoreType.DMA((40,))],
        compiler_params=pltpu.CompilerParams(collective_id=0, has_side_effects=True, vmem_limit_bytes=60 << 20),
        name="gather_and_attend",
    )(length, w_qkv, w_ckv, w_so, w_cq, w_co, vectors, win_in, wout_in, x_in, cap_in, dy_in)


ORDER = ("z", "x", "c", "y")
def part(ref, at, whole, **fixed):
    return ref.at[tuple(fixed[a] if a in fixed else slice(None) if a in whole else at[a] for a in ORDER)]


def each(shape, body):
    total = 1
    for s in shape:
        total *= s

    def step(i, _):
        index, rest = [], i
        for s in reversed(shape):
            index.insert(0, lax.rem(rest, s))
            rest = lax.div(rest, s)
        body(tuple(index))
        return 0

    if total == 1:
        body((0,) * len(shape))
    else:
        lax.fori_loop(0, total, step, 0)


def add_into(dst, *srcs):
    def one(index):
        total = dst[index].astype(jnp.float32)
        for s in srcs:
            total += s[index].astype(jnp.float32)
        dst[index] = total.astype(dst.dtype)

    each(dst.shape[:-2], one)


def landing_shapes(rows, cols, axes):
    whole, shapes = {"z", "x", "y"}, []
    for axis in axes:
        whole = whole - {axis}
        shapes.append(pltpu.VMEM((6, *[4 for a in ("z", "x", "y") if a in whole], rows, cols), jnp.bfloat16))
    return tuple(shapes)


def scatter_flow(g, landing, at, axes, whole, copies, cuts=((),)):
    whole = set(whole)
    for phase, (axis, land) in enumerate(zip(axes, landing)):
        up, down, far = moved(at, axis, 1), moved(at, axis, -1), moved(at, axis, 2)
        rest = whole - {axis}

        def blk(place, core):
            return part(g, at, rest, **{axis: place[axis], "c": core})

        s = []
        for cut in cuts if phase == 0 else ((),):
            of = lambda ref: ref.at[cut] if cut else ref
            s += [
                copies.start(of(blk(far, 0)), of(land.at[0]), up),
                copies.start(of(blk(far, 1)), of(land.at[1]), down),
                copies.start(of(blk(up, 1)), of(land.at[2]), up),
                copies.start(of(blk(down, 0)), of(land.at[3]), down),
            ]
            yield
        for q in s[0::4]:
            q.wait_recv()
        add_into(blk(up, 0), land.at[0])
        more = [copies.start(blk(up, 0), land.at[4], up)]
        for q in s[1::4]:
            q.wait_recv()
        add_into(blk(down, 1), land.at[1])
        more.append(copies.start(blk(down, 1), land.at[5], down))
        yield
        for q in s[2::4]:
            q.wait_recv()
        more[1].wait_recv()
        add_into(blk(at, 1), land.at[2], land.at[5])
        for q in s[3::4]:
            q.wait_recv()
        more[0].wait_recv()
        add_into(blk(at, 0), land.at[3], land.at[4])
        for q in s + more:
            q.wait_send()
        whole = rest


def backward_kernel(x2_in, n3, dy_in, dy_pair, x1_in, probs_in, cq_in, ck_in, cv_in, att, n2, catt, x_in, qkv_in, lse, wq_in, e_in, vec,
                    wc, win, wout,
                    out, out_a, out_b, out_c, out_q, tok, cap,
                    p0, p1, p2, p3, ya, dn, x2, u2, dhs, dh2, spread, units, sums, probs, cq, ck, cv, rows3, r2s, a2, datt4, dckv4,
                    dcap4, gq, gql, wq, ga, gb, gc, la, lb, lc0, lc1, lc2, lq0, lq1, fa, fb, fc, fq, send, recv, local):
    at = position()
    partner = moved(at, "c", 1)
    row = [moved(at, "y", b) for b in (1, 3, 2)]
    ring = row + [moved(o, "c", 1) for o in row] + [partner]
    others = [moved(at, a, b) for a in "zx" for b in (1, -1)] + ring
    barrier = pltpu.get_barrier_semaphore()
    for o in others:
        pl.semaphore_signal(barrier, inc=1, device_id=device(o), device_id_type=MESH)
    c, y = at["c"], at["y"]
    own, theirs = pl.ds(0, 256), pl.ds(256, 256)
    started = []

    def load(src, dst):
        cp = pltpu.make_async_copy(src, dst, local.at[len(started)])
        cp.start()
        started.append(cp)
        return cp

    def ready(loads):
        for l in loads:
            l.wait()

    chunk = 512
    n_chunk = win.shape[1] // chunk
    width = 8 * chunk // 32

    def weights(i):
        cols, s = pl.ds(i * chunk, chunk), (i % 2) * chunk
        return [load(win.at[:, cols], p0.at[:, pl.ds(s, chunk)]), load(wout.at[cols], p1.at[pl.ds(s, chunk)])]

    first = [load(n3, p2.at[pl.ds(0, 512)]), load(dy_in, p2.at[pl.ds(512, 256)]), load(dy_pair, p3.at[pl.ds(0, 512), pl.ds(512, 512)])]
    ffn = {0: weights(0), 1: weights(1)}
    x2_load = load(x2_in, x2)
    late = [load(a, b) for a, b in ((probs_in, probs), (cq_in, cq), (ck_in, ck), (cv_in, cv), (catt, a2.at[0]), (n2, a2.at[1]), (wq_in, wq))]

    def by_rows(body):
        loop(4, lambda i: body(pl.ds(pl.multiple_of(i * 64, 64), 64)))

    def vrow(k):
        return vec[k:k + 1, :]

    for j in range(4):
        src, dst = lax.broadcasted_iota(jnp.int32, (width, chunk), 0), lax.broadcasted_iota(jnp.int32, (width, chunk), 1)
        spread[j] = jnp.where(lax.div(src, 8) * 32 + lax.rem(src, 8) + 8 * j == dst, 1.0, 0.0).astype(BF)
    pieces = lambda j: jnp.concatenate([vec[9 + j:10 + j, i * width:(i + 1) * width] for i in range(n_chunk)], axis=0).astype(BF)
    units[0:8, :] = sum(mm(pieces(j), spread[j]) for j in range(4))
    sums[...] = jnp.zeros_like(sums)
    ya[...] = jnp.zeros_like(ya)
    dn[...] = jnp.zeros_like(dn)
    ready(first)
    p3[:, 0:512] = p2[0:512, :].T

    copies = Copies(send, recv)
    every = {"z", "x", "y"}
    whole = slice(None)
    fl_a = scatter_flow(ga, la, at, ("x", "z", "y"), every, copies, [(z,) for z in range(4)])
    fl_b = scatter_flow(gb, lb, at, ("z", "x", "y"), every, copies, [(whole, whole, whole, pl.ds(k * 512, 512)) for k in range(4)])
    fl_c = [scatter_flow(gc.at[:, :, :, :, :, pl.ds(k * 512, 512)], land, at, axes, every, copies)
            for k, (land, axes) in enumerate(((lc0, "zxy"), (lc1, "xzy"), (lc2, "yzx")))]

    def feed(i):
        ready(ffn[i])
        s = i % 3
        wi, wo = p0.at[:, pl.ds(i % 2 * chunk, chunk)], p1.at[pl.ds(i % 2 * chunk, chunk)]
        dy = p2.at[pl.ds(512, 256)]
        u, slope = gelu_both(mm(p2[0:256, :], wi[...]) + units[i:i + 1, :])
        u = u.astype(BF)
        u2[s, 0:256, :] = u
        ya[...] += mm(u, wo[...])
        d = (mm_cols(dy[...], wo[...]) * slope).astype(BF)
        low_half, high_half = d[:, 0:256], d[:, 256:512]
        dh2[s, 0:256, :] = jnp.where(c == 0, low_half, high_half)
        dhs[s] = jnp.where(c == 0, high_half, low_half)
        units[8 + i:9 + i, :] = jnp.sum(d.astype(F32), axis=0, keepdims=True)
        dn[...] += mm_cols(d, wi[...])

    def weight_grads(i):
        s = i % 3
        ga[i // 2, (i % 2) * 2:(i % 2) * 2 + 2] = mm_rows(u2[s], p3[0:512, 512:1024]).reshape(2, 2, 4, 32, 512).astype(BF)
        gb[:, :, :, :, :, i * 256:(i + 1) * 256] = mm(p3[:, 0:512], dh2[s]).reshape(4, 4, 2, 4, 8, 256).astype(BF)
        if i % 2:
            next(fl_a)
            next(fl_b)

    swaps = {}
    for i in range(n_chunk):
        feed(i)
        if i + 2 < n_chunk:
            ffn[i + 2] = weights(i + 2)
        if i == 0:
            pl.semaphore_wait(barrier, len(others))
        if i > 1:
            weight_grads(i - 2)
        if i:
            ready(swaps[i - 1])
        s = i % 3
        swaps[i] = [copies.start(u2.at[s, own], u2.at[s, theirs], partner), copies.start(dhs.at[s], dh2.at[s, theirs], partner)]
    high = units[8:16, :].astype(BF)
    low = (units[8:16, :] - high.astype(F32)).astype(BF)
    for j in range(4):
        total = mm_cols(high, spread[j]) + mm_cols(low, spread[j])
        for i in range(n_chunk):
            sums[9 + j:10 + j, i * width:(i + 1) * width] = total[i:i + 1, :]
    co_load, wcq_load = load(wc.at[:, pl.ds(2048, 1024)], p0), load(wc.at[:, pl.ds(1024, 1024)], p1)
    x2_load.wait()
    r2, dcq, r1 = rows3.at[0], rows3.at[1], rows3.at[2]

    def after_feed(r):
        v = x2[r, :]
        out[r, :] = (v + ya[r, :] + vrow(8)).astype(BF)
        dy = p2[pl.ds(pl.multiple_of(512 + r.start, 64), 64), :].astype(F32)
        dv, dgain, dshift = norm_back(v, dn[r, :], vrow(2))
        d = dy + dv
        x2[r, :] = d
        r2[r, :] = d.astype(BF)
        sums[2:3, :] += dgain
        sums[5:6, :] += dshift
        sums[7:8, :] += jnp.sum(d, axis=0, keepdims=True)
        sums[8:9, :] += jnp.sum(dy, axis=0, keepdims=True)

    by_rows(after_feed)
    shared = {}

    def share(k):
        src, dst = rows3.at[k], r2s.at[k]
        shared[k] = [load(src.at[:, half(1024, at)], dst.at[own]), copies.start(src.at[:, half(1024, partner)], dst.at[theirs], partner)]

    share(0)
    weight_grads(n_chunk - 2)
    ready(swaps[n_chunk - 1])
    weight_grads(n_chunk - 1)
    x1_load, so_load, x_load = load(x1_in, ya), load(wc.at[:, pl.ds(0, 1024)], p3), load(x_in, p2)

    def grad_c(k, slot):
        for q in shared[k]:
            q.wait()

        def block_rows(z):
            g = mm_rows(a2[slot, :, pl.ds(pl.multiple_of(z * 256, 256), 256)], r2s[k])
            gc[z, :, :, :, :, k * 512:(k + 1) * 512] = g.reshape(4, 2, 4, 8, 512).astype(BF)

        loop(4, block_rows)
        next(fl_c[k])

    ready(late)
    co_load.wait()
    dckv, mixed_grad = u2.at[0], u2.at[1]

    def mixed_from(d, w):
        for k in range(2):
            mixed_grad[k * 256:(k + 1) * 256, :] = mm_cols(d[...], w[k * 512:(k + 1) * 512, :]).astype(BF)

    mixed_from(r2, p0)

    def cross_backward(p):
        cols = pl.ds(pl.multiple_of(p * 128, 128), 128)
        k, v, q = ck[:, cols], cv[:, cols], cq[:, cols]
        d = mixed_grad[pl.ds(pl.multiple_of(lax.div(p, 4) * 256, 256), 256), pl.ds(pl.multiple_of(lax.rem(p, 4) * 128, 128), 128)]
        dk = dv = jnp.zeros((128, 128), F32)
        dq = []
        for head in range(2):
            lanes = lanes_of(q.shape, head)
            qh = jnp.where(lanes, q, jnp.zeros_like(q))
            dout = jnp.where(lanes, d, jnp.zeros_like(d))
            prob = probs[2 * p + head]
            dp = mm_cols(v, dout)
            ds = (prob * (dp - jnp.sum(dp * prob, axis=0, keepdims=True))).astype(BF)
            dv += mm(prob.astype(BF), dout)
            dk += mm(ds, qh)
            dq.append(mm_rows(ds, k))
        dcq[:, cols] = (jnp.where(lanes_of(q.shape, 0), dq[0], dq[1]) * SCALE).astype(BF)
        here, place = pl.ds(pl.multiple_of(lax.div(p, 2) * 128, 128), 128), pl.multiple_of(lax.rem(p, 2) * 128, 128)
        dckv[here, pl.ds(place, 128)] = (dk * SCALE).astype(BF)
        dckv[here, pl.ds(place + 256, 128)] = dv.astype(BF)

    loop(8, cross_backward)
    share(1)
    kv_rows = lambda of: pl.ds(pl.multiple_of(of["y"] * 128, 128), 128)
    kv_own = [load(dckv.at[kv_rows(at)], dckv4.at[y])]
    kvs = [copies.start(dckv.at[kv_rows(to)], dckv4.at[y], to) for to in row]
    next(fl_a)
    next(fl_b)
    wcq_load.wait()
    dn[...] = mm_cols(dcq[...], p1[...])
    x1_load.wait()

    def before_cross(r):
        dv, dgain, dshift = norm_back(ya[r, :], dn[r, :], vrow(1))
        d = x2[r, :] + dv
        x2[r, :] = d
        r1[r, :] = d.astype(BF)
        sums[1:2, :] += dgain
        sums[4:5, :] += dshift
        sums[6:7, :] += jnp.sum(d, axis=0, keepdims=True)

    by_rows(before_cross)
    share(2)
    so_load.wait()
    mixed_from(r1, p3)
    qkv_load = load(qkv_in, p3.at[:, pl.ds(0, 768)])
    for q in shared[1] + shared[2]:
        q.wait()
    own_rows = pl.ds(pl.multiple_of(y * 256, 256), 256)
    mixed_part = lambda of: mixed_grad.at[pl.ds(pl.multiple_of(lax.div(of["y"], 2) * 256, 256), 256), pl.ds(pl.multiple_of(lax.rem(of["y"], 2) * 256, 256), 256)]
    d_own = load(mixed_part(at), datt4.at[own_rows])
    dd = [copies.start(mixed_part(to), datt4.at[own_rows], to) for to in row]
    shared[1] = shared[2] = []
    grad_c(0, 0)
    att_load = load(att, a2.at[0])
    grad_c(1, 1)
    att_load.wait()
    grad_c(2, 0)

    x_load.wait()
    x_all, n1, gain, shift = p2, p0, vec[0:1, :], vec[3:4, :]

    def first_norm(i):
        r = pl.ds(pl.multiple_of(i * 128, 128), 128)
        n1[r, :] = (normed(x_all[r, :].astype(F32))[0] * gain + shift).astype(BF)

    loop(8, first_norm)

    for s in kv_own + kvs:
        s.wait()
    dckv4[0] = sum(dckv4[k].astype(F32) for k in range(4)).astype(BF)
    dcap, e = cq.at[pl.ds(0, 128)], cq.at[pl.ds(128, 128)]
    e_load = load(e_in, e)
    dcap[...] = mm_cols(dckv4[0], wq[:, 768:1280]).astype(BF)
    cap_own = load(dcap.at[:, quarter(at)], dcap4.at[y])
    caps = [copies.start(dcap.at[:, quarter(to)], dcap4.at[y], to) for to in row]

    for s in dd + [d_own, qkv_load, e_load]:
        s.wait()
    qkv, dn_b, dn4 = p3, p1, rows3
    dqkv = a2.reshape(1024, 1024).at[:, pl.ds(0, 768)]
    dkv = probs.reshape(2048, 256)
    dk, dv = dkv.at[pl.ds(0, 1024), pl.ds(0, 128)], dkv.at[pl.ds(0, 1024), pl.ds(128, 128)]
    ab = [fl_a, fl_b]

    def go(flows):
        for f in flows:
            next(f, None)

    def pair(p, *blocks):
        for i in blocks:
            self_backward(p, i, qkv, lse, datt4, dqkv, dk, dv)

    pair(0, 0, 1, 2, 3)
    pair(1, 0, 1, 2, 3)
    go(fl_c)

    def grad_q(z):
        cols = pl.ds(pl.multiple_of(z * 256, 256), 256)
        gq[z, :, :, :, :, 0:768] = mm_rows(n1[:, cols], dqkv[...]).reshape(4, 2, 4, 8, 768).astype(BF)
        gq[z, :, :, :, :, 768:1280] = mm_rows(e[:, cols], dckv4[0]).reshape(4, 2, 4, 8, 512).astype(BF)

    loop(4, grad_q)
    n_q = gq.shape[-1]
    pq = copies.start(gq.at[:, :, :, :, :, pl.ds(pl.multiple_of(partner["c"] * 768, 128), 512)], gql.at[:, :, :, :, :, pl.ds(0, 512)], partner)

    def norm_rows(start, i):
        r = pl.ds(pl.multiple_of(start + i * 128, 128), 128)
        z, _ = normed(x_all[r, :].astype(F32))
        d = mm_cols(dqkv[r, :], wq[:, 0:768])
        dn_b[r, :] = d.astype(BF)
        sums[0:1, :] += jnp.sum(d * z, axis=0, keepdims=True)
        sums[3:4, :] += jnp.sum(d, axis=0, keepdims=True)

    dns = []
    for k in (2, 0, 1):
        start = row[k]["y"] * 256
        loop(2, functools.partial(norm_rows, start))
        dns.append(copies.start(dn_b.at[pl.ds(pl.multiple_of(start, 256), 256)], dn4.at[k], row[k]))
        if k == 0:
            go(fl_c)
    loop(2, functools.partial(norm_rows, y * 256))
    dn[0:128, :] = jnp.zeros((128, 1024), F32)
    dn[0:16, :] = sums[...]
    gq[:, :, :, :, :, 1280:1408] = dn[0:128, :].T.reshape(4, 4, 2, 4, 8, 128).astype(BF)
    gq[:, :, :, :, :, 1408:1536] = jnp.zeros((4, 4, 2, 4, 8, 128), BF)
    pv = copies.start(gq.at[:, :, :, :, :, pl.ds(pl.multiple_of(partner["c"] * 768 + 512, 128), 256)], gql.at[:, :, :, :, :, pl.ds(512, 256)], partner)
    go(ab)
    go(fl_c)
    pq.wait()
    pv.wait()
    mine = gq.at[:, :, :, :, :, half(n_q, at)]
    add_into(mine, gql)
    q_cols = lambda k: gq.at[:, :, :, :, :, pl.ds(pl.multiple_of(c * 768 + k * 384, 128), 384)]
    fl_q = [scatter_flow(q_cols(0), lq0, at, ("x", "z"), every, copies), scatter_flow(q_cols(1), lq1, at, ("z", "x"), every, copies)]
    go(fl_q)
    go(ab)
    go(fl_c)
    go(fl_q)
    go(ab)
    go(fl_c)
    go(fl_q)
    go(ab)
    go(fl_c)
    last = [copies.start(gc.at[at["z"], at["x"], partner["c"], y], fc, partner)]
    go(fl_q)
    go(ab)
    last += [copies.start(g.at[at["z"], at["x"], partner["c"], y], f, partner) for g, f in ((ga, fa), (gb, fb))]
    for s in dns + caps + [cap_own]:
        s.wait()

    def token_rows(i):
        r = pl.ds(pl.multiple_of(i * 64, 64), 64)
        here = pl.ds(pl.multiple_of(y * 256 + i * 64, 64), 64)
        d = dn_b[here, :].astype(F32) + dn4[0, r, :].astype(F32) + dn4[1, r, :].astype(F32) + dn4[2, r, :].astype(F32)
        back, _, _ = norm_back(x_all[here, :].astype(F32), d, gain)
        x2[r, :] += back

    loop(4, token_rows)
    tok_copy = load(x2, tok)
    cap[...] = sum(dcap4[k].astype(F32) for k in range(4))
    finish(fl_q + fl_c + ab)

    for o in ring:
        last.append(copies.start(mine.at[at["z"], at["x"], o["c"], o["y"]], fq.at[c, y], o))
    own_q = load(mine.at[at["z"], at["x"], c, y], fq.at[c, y])
    for g, o in ((ga, out_a), (gb, out_b), (gc, out_c)):
        o[c] = g[at["z"], at["x"], c, y]
    for s in last + [own_q, tok_copy]:
        s.wait()
    for f, o in ((fa, out_a), (fb, out_b), (fc, out_c)):
        o[partner["c"]] = f[...]
    out_q[...] = fq[...]


def backward(*args):
    V = pltpu.VMEM
    n_c, n_q = 1536, 768
    rows = V((256, 1024), F32)
    scratch = [V((1024, 1024), BF)] * 4 + [rows] * 3
    scratch += [V((3, 512, 512), BF), V((3, 256, 256), BF), V((3, 512, 256), BF), V((4, 128, 512), BF), V((16, 512), F32), V((16, 1024), F32), V((16, 128, 256), F32)]
    scratch += [V((256, 1024), BF), V((128, 1024), BF), V((128, 1024), BF), V((3, 256, 1024), BF), V((3, 512, 512), BF)]
    scratch += [V((2, 512, 1024), BF), V((1024, 256), BF), V((4, 128, 512), BF), V((4, 128, 256), BF)]
    scratch += [V((4, 4, 2, 4, 8, 2 * n_q), BF), V((4, 4, 2, 4, 8, n_q), BF), V((1024, 1280), BF)]
    scratch += [V((4, 4, 2, 4, 32, 512), BF), V((4, 4, 2, 4, 8, 2048), BF), V((4, 4, 2, 4, 8, n_c), BF)]
    scratch += [landing_shapes(32, 512, "xzy"), landing_shapes(8, 2048, "zxy")]
    scratch += [landing_shapes(8, 512, axes) for axes in ("zxy", "xzy", "yzx")] + [landing_shapes(8, 384, axes) for axes in ("xz", "zx")]
    scratch += [V((32, 512), BF), V((8, 2048), BF), V((8, n_c), BF), V((2, 4, 8, n_q), BF)]
    n = 208
    scratch += [pltpu.SemaphoreType.DMA((n,)), pltpu.SemaphoreType.DMA((n,)), pltpu.SemaphoreType.DMA((64,))]
    s = jax.ShapeDtypeStruct
    outs = [s((256, 1024), BF), s((2, 32, 512), BF), s((2, 8, 2048), BF), s((2, 8, n_c), BF), s((2, 4, 8, n_q), BF), s((256, 1024), F32),
            s((128, 256), F32)]
    anywhere, vm = pl.BlockSpec(memory_space=pl.ANY), pl.BlockSpec(memory_space=V)
    return pl.pallas_call(
        backward_kernel, out_shape=outs,
        in_specs=[anywhere] * 14 + [vm] + [anywhere] * 2 + [vm] + [anywhere] * 3, out_specs=[vm] * 5 + [anywhere, vm],
        scratch_shapes=scratch,
        compiler_params=pltpu.CompilerParams(collective_id=1, has_side_effects=True, vmem_limit_bytes=62 << 20),
        name="feed_and_reduce",
    )(*args)


def finish_kernel(a, b, c, q, tok_in, cap_in, tok, cap, d_qkv, d_self_out, d_cross_q, d_cross_kv, d_cross_out, d_in, d_out, d_gains, d_shifts, d_biases, d_in_bias):
    tok[...] = tok_in[...]
    cap[...] = cap_in[...]
    for k in range(2):
        d_out[:, k * 512:(k + 1) * 512] = a[k].astype(F32)
        for j in range(8):
            d_in[:, j * 512 + k * 256:j * 512 + (k + 1) * 256] = b[k, :, j * 256:(j + 1) * 256].astype(F32)
        for m, ref in enumerate((d_cross_out, d_cross_q, d_self_out)):
            ref[:, k * 512:(k + 1) * 512] = c[k, :, m * 512:(m + 1) * 512].astype(F32)
    for y in range(4):
        for m in range(3):
            d_qkv[:, m * 1024 + y * 256:m * 1024 + (y + 1) * 256] = q[0, y, :, m * 256:(m + 1) * 256].astype(F32)
        for m in range(2):
            d_cross_kv[:, m * 1024 + y * 256:m * 1024 + (y + 1) * 256] = q[1, y, :, m * 256:(m + 1) * 256].astype(F32)
    vectors = sum(q[1, y, :, 512:640].astype(F32) for y in range(4)).T
    for m, ref in enumerate((d_gains, d_shifts, d_biases)):
        ref[...] = vectors[3 * m:3 * m + 3, :]
    d_in_bias[...] = jnp.concatenate([vectors[9 + j:10 + j, :] for j in range(4)], axis=1)


def assembled(a, b, c, q, tok, cap):
    shapes = [(256, 1024), (128, 256), (8, 3072), (8, 1024), (8, 1024), (8, 2048), (8, 1024), (8, 4096), (32, 1024), (3, 8), (3, 8), (3, 8), (1, 32)]
    vm = pl.BlockSpec(memory_space=pltpu.VMEM)
    return pl.pallas_call(
        finish_kernel, out_shape=[jax.ShapeDtypeStruct(s, F32) for s in shapes], in_specs=[vm] * 6, out_specs=[vm] * 13, name="assemble",
    )(a, b, c, q, tok, cap)


def local(tokens, captions, cap_lengths, w_qkv, w_self_out, w_cross_q, w_cross_kv, w_cross_out, w_in, w_out,
          norm_gains, norm_shifts, out_biases, in_bias, out_grad):
    vectors = jnp.concatenate([norm_gains.T, norm_shifts.T, out_biases.T, in_bias.reshape(4, 8).T], axis=1)
    vectors = jnp.pad(vectors, ((0, 0), (0, 128 - 13)))
    dy = out_grad[0]
    (c_g, win_g, wout_g, dy_pair, x_g, wq, qkv, lse, att, ck, cv, e, x1, x2, n2, n3, catt, probs, cq, vec) = gathered(
        cap_lengths, w_qkv, w_cross_kv, w_self_out, w_cross_q, w_cross_out, vectors, w_in, w_out, tokens[0], captions[0], dy)
    wc, full_in, full_out = c_g.reshape(1024, -1), win_g.reshape(1024, -1), wout_g.reshape(4096, 1024)
    layer_out, out_a, out_b, out_c, out_q, tokens_grad, captions_grad = backward(
        x2, n3, dy, dy_pair, x1, probs, cq, ck, cv, att, n2, catt, x_g.reshape(1024, 1024), qkv, lse, wq, e, vec, wc, full_in, full_out)
    tokens_grad, captions_grad, *grads, d_in_bias = assembled(out_a, out_b, out_c, out_q, tokens_grad, captions_grad)
    return (layer_out[None], tokens_grad[None], captions_grad[None], *grads, d_in_bias.reshape(32))


def solution(mesh):
    rows, tokens, vectors = P(("dp", "seq"), None), P("dp", "seq", None), P(None, ("dp", "seq"))
    captions = P("dp", None, "seq")
    return jax.shard_map(
        local, mesh=mesh,
        in_specs=(tokens, captions, P("dp"), *[rows] * 7, *[vectors] * 3, P(("dp", "seq")), tokens),
        out_specs=(tokens, tokens, captions, *[rows] * 7, *[vectors] * 3, P(("dp", "seq"))),
        check_vma=False,
    )
```
